32 devices in a mesh: tm: 4 (over y, core), roll: 8 (over z, x).
Axes of the slice: x: 2, y: 2, z: 4, core: 2. Of those that a mesh axis runs over, the one named last changes fastest.
Arguments:
- layer_input: bfloat16 [8, 3072, 256], P('roll', 'tm'), may hold values from -6 to 6
- start_memory: bfloat16 [8, 48, 256], P('roll'), may hold values from -6 to 6
- horizon: int32 [8, 64], P('roll'), may hold values from 0 to 15, as said below
- cotangent: bfloat16 [8, 3072, 256], P('roll', 'tm'), may hold values from -6 to 6
- first_gain: float32 [256], replicated, may hold values from 0.5 to 1.5
- first_shift: float32 [256], replicated, may hold values from -2 to 2
- query_projection_weight: bfloat16 [256, 256], replicated, may hold values from -0.375 to 0.375
- key_projection_weight: bfloat16 [256, 256], replicated, may hold values from -0.375 to 0.375
- value_projection_weight: bfloat16 [256, 256], replicated, may hold values from -0.375 to 0.375
- relative_weight: bfloat16 [256, 256], replicated, may hold values from -0.375 to 0.375
- content_bias: float32 [256], replicated, may hold values from -3 to 3
- position_bias: float32 [256], replicated, may hold values from -3 to 3
- output_weight: bfloat16 [256, 256], replicated, may hold values from -2 to 2
- second_gain: float32 [256], replicated, may hold values from 0.5 to 1.5
- second_shift: float32 [256], replicated, may hold values from -2 to 2
- expand_weight: bfloat16 [256, 1024], replicated, may hold values from -0.375 to 0.375
- expand_bias: float32 [1024], replicated, may hold values from -2 to 2
- shrink_weight: bfloat16 [1024, 256], replicated, may hold values from -0.25 to 0.25
- shrink_bias: float32 [256], replicated, may hold values from -2 to 2
Outputs:
- layer_output: bfloat16 [8, 3072, 256], P('roll', 'tm')
- input_grad: bfloat16 [8, 3072, 256], P('roll', 'tm')
- first_gain_grad: float32 [256], replicated
- first_shift_grad: float32 [256], replicated
- query_weight_grad: float32 [256, 256], replicated
- key_weight_grad: float32 [256, 256], replicated
- value_weight_grad: float32 [256, 256], replicated
- relative_weight_grad: float32 [256, 256], replicated
- content_bias_grad: float32 [256], replicated
- position_bias_grad: float32 [256], replicated
- output_weight_grad: float32 [256, 256], replicated
- second_gain_grad: float32 [256], replicated
- second_shift_grad: float32 [256], replicated
- expand_weight_grad: float32 [256, 1024], replicated
- expand_bias_grad: float32 [1024], replicated
- shrink_weight_grad: float32 [1024, 256], replicated
- shrink_bias_grad: float32 [256], replicated
The draws below stay inside these ranges and needn't reach their ends.
Inputs may be any that keep to these rules, and one draw needn't show every extreme that they name: `horizon`: in every pair of consecutive rollouts (0 and 1, 2 and 3, and so on) one rollout has 15 in every segment.
All inputs are finite; a program needn't handle non-finite values.
Results may differ from the reference program's by a relative error of at most 0.012.
The reference program's roundings to bfloat16 on the way count: a program that leaves them out, or rounds other values in their place, can miss the bound.
Values may be sent and summed in bfloat16 or wider, within the bound.
No kernel may reach another device: no remote copies, remote signals or barrier semaphores. Data moves between devices by JAX's collectives and lax.ppermute only.
A program may use at most 64 MiB of HBM per device.

```python
import math
import jax
import jax.numpy as jnp
from jax import lax

D = 256
HEADS = 8
HEAD_DIM = 32
FF = 1024
SEGMENT_TOKENS = 48
STEP = 3
STEPS_SEG = 16
ROLL_DEV = 1
ROLLOUTS = 8
SEGMENTS = 64


def draw_horizon(key, part):
    key = jax.random.fold_in(key, 11)
    steps_key, pick_key = jax.random.split(key)
    random_steps = jax.random.randint(steps_key, (ROLLOUTS, SEGMENTS), 0, STEPS_SEG)
    pairs = ROLLOUTS // 2
    chosen = jax.random.randint(pick_key, (pairs,), 0, 2)
    within = jnp.arange(ROLLOUTS) % 2
    longest = within == jnp.repeat(chosen, 2)
    return jnp.where(longest[:, None], STEPS_SEG - 1, random_steps).astype(jnp.int32)


def block_scale(rng, dims, cuts, low, high):
    level, own = 1.0, jax.random.fold_in(rng, 6)
    for position, parts in cuts:
        steps = jnp.exp(jax.random.uniform(jax.random.fold_in(own, position), (parts,), jnp.float32, low / len(cuts), high / len(cuts)))
        level = level * jnp.repeat(steps, dims[position] // parts).reshape([-1 if axis == position else 1 for axis in range(len(dims))])
    return level


def gaussian(own_key, dims, width, most, shards=(), held_as=jnp.bfloat16):
    drawn = width * jax.random.normal(own_key, dims, jnp.float32)
    if shards:
        drawn = drawn * block_scale(own_key, dims, shards, -0.22, 0.18)
    return jnp.clip(drawn, -most, most).astype(held_as)


def setup_inputs(seed: int = 0) -> dict:
    streams_of = jax.random.split(jax.random.key(seed), 20)
    return {
        "layer_input": gaussian(streams_of[0], (ROLLOUTS, SEGMENTS * SEGMENT_TOKENS, D), 1.0, 6.0, ((0, 8), (1, 4))),
        "start_memory": gaussian(streams_of[1], (ROLLOUTS, SEGMENT_TOKENS, D), 1.0, 6.0, ((0, 8),)),
        "horizon": draw_horizon(jax.random.fold_in(streams_of[19], 71), 0),
        "cotangent": gaussian(streams_of[3], (ROLLOUTS, SEGMENTS * SEGMENT_TOKENS, D), 1.0, 6.0, ((0, 8), (1, 4))),
        "first_gain": jnp.clip(1.0 + 0.1 * jax.random.normal(streams_of[4], (D,), jnp.float32), 0.5, 1.5),
        "first_shift": gaussian(streams_of[5], (D,), 0.3, 2.0, (), jnp.float32),
        "query_projection_weight": gaussian(streams_of[6], (D, D), D ** -0.5, 0.375),
        "key_projection_weight": gaussian(streams_of[7], (D, D), D ** -0.5, 0.375),
        "value_projection_weight": gaussian(streams_of[8], (D, D), D ** -0.5, 0.375),
        "relative_weight": gaussian(streams_of[9], (D, D), D ** -0.5, 0.375),
        "content_bias": gaussian(streams_of[10], (D,), 0.5, 3.0, (), jnp.float32),
        "position_bias": gaussian(streams_of[11], (D,), 0.5, 3.0, (), jnp.float32),
        "output_weight": gaussian(streams_of[12], (D, D), (D // 32) ** -0.5, 2.0),
        "second_gain": jnp.clip(1.0 + 0.1 * jax.random.normal(streams_of[13], (D,), jnp.float32), 0.5, 1.5),
        "second_shift": gaussian(streams_of[14], (D,), 0.3, 2.0, (), jnp.float32),
        "expand_weight": gaussian(streams_of[15], (D, FF), D ** -0.5, 0.375),
        "expand_bias": gaussian(streams_of[16], (FF,), 0.3, 2.0, (), jnp.float32),
        "shrink_weight": gaussian(streams_of[17], (FF, D), (FF // 2) ** -0.5, 0.25),
        "shrink_bias": gaussian(streams_of[18], (D,), 0.3, 2.0, (), jnp.float32),
    }


@jax.custom_vjp
def reduced_forward(v):
    return lax.optimization_barrier(v.astype(jnp.bfloat16)).astype(jnp.float32)

@jax.custom_vjp
def reduced_backward(v):
    return v

def low_keep(v):
    return (reduced_forward(v), None)

def low_pass(kept, grad):
    return (grad,)

def back_keep(v):
    return (v, None)

def back_low(kept, grad):
    return (reduced_forward(grad),)
reduced_forward.defvjp(low_keep, low_pass)
reduced_backward.defvjp(back_keep, back_low)
EPSILON = 1e-05
MASKED = -1000000000.0
EXACT_PRECISION = lax.Precision.HIGHEST

def norm_layer(values, gain, shift):
    center = values - lax.optimization_barrier(jnp.mean(values, axis=-1, keepdims=True))
    spread = lax.optimization_barrier(jnp.mean(center * center, axis=-1, keepdims=True))
    return center * lax.rsqrt(spread + EPSILON) * gain + shift

def shift_relative(scores):
    leading = scores.shape[:-2]
    row_count = scores.shape[-2]
    col_count = scores.shape[-1]
    padded = jnp.pad(scores, [(0, 0)] * len(leading) + [(0, 0), (1, 0)])
    padded = padded.reshape(leading + (col_count + 1, row_count))
    return padded[..., 1:, :].reshape(leading + (row_count, col_count))

def position_table(count, features):
    half_width = features // 2
    distance = (count - 1 - jnp.arange(count)).astype(jnp.float32)
    freqs = 10000.0 ** (-(2.0 * jnp.arange(half_width).astype(jnp.float32)) / features)
    angles = distance[:, None] * freqs[None, :]
    return jnp.concatenate([jnp.sin(angles), jnp.cos(angles)], axis=-1)

def key_mask(previous, current, seg_len, step_len):
    query_pos = jnp.arange(seg_len)[:, None]
    key_pos = jnp.arange(2 * seg_len)[None, :]
    causal = key_pos <= query_pos + seg_len
    itself = key_pos == query_pos + seg_len
    key_step = jnp.where(key_pos < seg_len, key_pos, key_pos - seg_len) // step_len
    limit = jnp.where(key_pos < seg_len, previous[:, None], current[:, None])
    live = key_step < limit
    return causal[None] & (live[:, None, :] | itself[None])

def activation(values):
    return jax.nn.gelu(values, approximate=True)

def layer_units(hid, memory, previous, current, params, relative):
    first_gain, first_shift, query_projection_weight, key_projection_weight, value_projection_weight, content_bias, position_bias, output_weight, second_gain, second_shift, expand_weight, expand_bias, shrink_weight, shrink_bias = params
    count = hid.shape[0]
    joined = jnp.concatenate([memory, hid], axis=1)
    layer_normalized = reduced_forward(norm_layer(joined, first_gain, first_shift))
    query_vectors = reduced_backward(jnp.einsum('twu,ul->twl', layer_normalized[:, SEGMENT_TOKENS:], query_projection_weight, precision=EXACT_PRECISION))
    key_matrix_rows = reduced_forward(reduced_backward(jnp.einsum('twu,ul->twl', layer_normalized, key_projection_weight, precision=EXACT_PRECISION)))
    value_matrix_rows = reduced_forward(reduced_backward(jnp.einsum('twu,ul->twl', layer_normalized, value_projection_weight, precision=EXACT_PRECISION)))
    content = reduced_forward(query_vectors + content_bias).reshape(count, SEGMENT_TOKENS, HEADS, HEAD_DIM)
    placed = reduced_forward(query_vectors + position_bias).reshape(count, SEGMENT_TOKENS, HEADS, HEAD_DIM)
    key_heads = key_matrix_rows.reshape(count, 2 * SEGMENT_TOKENS, HEADS, HEAD_DIM)
    value_heads = value_matrix_rows.reshape(count, 2 * SEGMENT_TOKENS, HEADS, HEAD_DIM)
    rel_heads = relative.reshape(2 * SEGMENT_TOKENS, HEADS, HEAD_DIM)
    direct = jnp.einsum('bihe,bjhe->bhij', content, key_heads, precision=EXACT_PRECISION)
    shifted = shift_relative(jnp.einsum('bihe,jhe->bhij', placed, rel_heads, precision=EXACT_PRECISION))
    scores = reduced_backward((direct + shifted) * (1.0 / math.sqrt(HEAD_DIM)))
    allowed = key_mask(previous, current, SEGMENT_TOKENS, STEP)[:, None]
    scores = jnp.where(allowed, scores, MASKED)
    row_top = lax.optimization_barrier(jnp.max(scores, axis=-1, keepdims=True))
    exponent = jnp.exp(scores - row_top)
    probs = reduced_forward(exponent / lax.optimization_barrier(jnp.sum(exponent, axis=-1, keepdims=True)))
    mixed = jnp.einsum('bhij,bjhe->bihe', probs, value_heads, precision=EXACT_PRECISION).reshape(count, SEGMENT_TOKENS, D)
    mixed = reduced_forward(reduced_backward(mixed))
    hidden = hid + reduced_backward(jnp.einsum('bsd,de->bse', mixed, output_weight, precision=EXACT_PRECISION))
    normed2 = reduced_forward(norm_layer(hidden, second_gain, second_shift))
    pre_act = reduced_backward(jnp.einsum('bsd,df->bsf', normed2, expand_weight, precision=EXACT_PRECISION)) + expand_bias
    activated = reduced_forward(activation(pre_act))
    return hidden + reduced_backward(jnp.einsum('bsf,fd->bsd', activated, shrink_weight, precision=EXACT_PRECISION)) + shrink_bias

def reference(layer_input, start_memory, horizon, cotangent, first_gain, first_shift, query_projection_weight, key_projection_weight, value_projection_weight, relative_weight, content_bias, position_bias, output_weight, second_gain, second_shift, expand_weight, expand_bias, shrink_weight, shrink_bias):
    inputs = layer_input.astype(jnp.float32)
    rollout_rows = inputs.shape[0]
    chain = inputs.shape[1] // SEGMENT_TOKENS
    blocks = inputs.reshape(rollout_rows, chain, SEGMENT_TOKENS, D)
    memory = jnp.concatenate([start_memory.astype(jnp.float32)[:, None], blocks[:, :-1]], axis=1)
    previous = jnp.concatenate([jnp.full((rollout_rows, 1), STEPS_SEG, jnp.int32), horizon[:, :-1]], axis=1)
    weights = tuple((weight.astype(jnp.float32) for weight in (first_gain, first_shift, query_projection_weight, key_projection_weight, value_projection_weight, relative_weight, content_bias, position_bias, output_weight, second_gain, second_shift, expand_weight, expand_bias, shrink_weight, shrink_bias)))
    table = position_table(2 * SEGMENT_TOKENS, D)
    groups = rollout_rows // ROLL_DEV
    group_shape = (groups, ROLL_DEV * chain, SEGMENT_TOKENS, D)
    grouped_memory = memory.reshape(group_shape)
    grouped_previous = previous.reshape(groups, ROLL_DEV * chain)
    grouped_current = horizon.reshape(groups, ROLL_DEV * chain)

    def forward(blocks_in, params):
        relative = reduced_forward(jnp.dot(reduced_forward(table), params[5], precision=EXACT_PRECISION))
        others = params[:5] + params[6:]

        def one_group(items):
            hid, mem, prev_len, cur_len = items
            return layer_units(hid, mem, prev_len, cur_len, others, relative)
        result = lax.map(jax.checkpoint(one_group), (blocks_in.reshape(group_shape), grouped_memory, grouped_previous, grouped_current))
        return result.reshape(rollout_rows, chain * SEGMENT_TOKENS, D)
    output, pullback = jax.vjp(forward, blocks, weights)
    input_grad, grads = pullback(cotangent.astype(jnp.float32))
    return (output.astype(jnp.bfloat16), input_grad.reshape(rollout_rows, chain * SEGMENT_TOKENS, D).astype(jnp.bfloat16), grads[0], grads[1], grads[2], grads[3], grads[4], grads[5], grads[6], grads[7], grads[8], grads[9], grads[10], grads[11], grads[12], grads[13], grads[14])
```

```python
import functools
import math

import jax
import jax.numpy as jnp
import numpy as np
from jax import lax
from jax.experimental import pallas as pl
from jax.experimental.pallas import tpu as pltpu
from jax.sharding import PartitionSpec as P

HEADS = 8
HEAD_DIM = 32
SEG = 48
STEP = 3
FEATURES = 256
HIDDEN = 1024
LANES = 128
GROUP = LANES // HEAD_DIM
EPSILON = 1e-05
MASKED = -1000000000.0
SCALING = 1.0 / math.sqrt(HEAD_DIM)
GELU_A = 0.7978845608028654
GELU_B = 0.044715 * GELU_A
BF = jnp.bfloat16
F32 = jnp.float32

EXPAND_AT = 0
SHRINK_AT = 1024
QUERY_AT = 2048
KEY_AT = 2304
VALUE_AT = 2560
OUTPUT_AT = 2816
RELATIVE_AT = 3072
VECTOR_AT = 3200
BUFFER_ROWS = 3328
(V_CONTENT, V_POSITION, V_GAIN1, V_SHIFT1, V_GAIN2, V_SHIFT2, V_SHRINK, V_EXPAND) = range(8)
VECTOR_ROWS = 16


def position_rows():
    distance = (2 * SEG - 1 - np.arange(2 * SEG)).astype(np.float32)
    freqs = 10000.0 ** (-(2.0 * np.arange(FEATURES // 2)) / FEATURES)
    angles = distance[:, None] * freqs.astype(np.float32)[None, :]
    table = np.concatenate([np.sin(angles), np.cos(angles)], axis=-1)
    return np.pad(table, ((0, LANES - 2 * SEG), (0, 0))).astype(BF)


def relative_basis():
    count = 2 * SEG
    k, c = np.arange(count)[:, None], np.arange(count)[None, :]
    basis = np.cos(np.pi * k * (2 * c + 1) / (2 * count)) * np.where(k == 0, np.sqrt(1.0 / count), np.sqrt(2.0 / count))
    basis = np.pad(basis, ((0, LANES - count), (0, LANES - count)))

    def parts(values):
        high = values.astype(BF)
        low = (values - high.astype(np.float64)).astype(BF)
        return np.concatenate([high, low], axis=0)

    return parts(basis), parts(basis @ position_rows().astype(np.float64))


def tables():
    return jnp.asarray(position_rows()), jnp.asarray(relative_basis()[0])


def dot(a, b):
    return lax.dot_general(a, b, (((1,), (0,)), ((), ())), preferred_element_type=F32)


def dot_t(a, b):
    return lax.dot_general(a, b, (((1,), (1,)), ((), ())), preferred_element_type=F32)


def t_dot(a, b):
    return lax.dot_general(a, b, (((0,), (0,)), ((), ())), preferred_element_type=F32)


def normalize(rows):
    center = rows - jnp.mean(rows, axis=-1, keepdims=True)
    spread = jnp.mean(center * center, axis=-1, keepdims=True)
    scale = lax.rsqrt(spread + EPSILON)
    return center * scale, scale


def column_sum(rows):
    return jnp.sum(rows, axis=0, keepdims=True)


def stack_heads(rows, head_masks):
    return jnp.concatenate([rows * mask for mask in head_masks], axis=0)


def unshift(rows, row_bits):
    rolled = jnp.concatenate(
        [pltpu.roll(rows[a : a + 8], SEG - 8 - a, 1) for a in range(0, SEG - 8, 8)] + [rows[SEG - 8 :]], axis=0
    )
    for step, bit in row_bits:
        rolled = jnp.where(bit, pltpu.roll(rolled, step, 1), rolled)
    return rolled


def pick_heads(rows, lane_head):
    picked = rows[0:SEG]
    for h in range(1, GROUP):
        picked = jnp.where(lane_head == h, rows[h * SEG : (h + 1) * SEG], picked)
    return picked


COPIES = 21
(C_X, C_START, C_ARRIVED, C_COT, C_GAIN1, C_SHIFT1, C_WQ, C_WK, C_WV, C_WR, C_CBIAS, C_PBIAS, C_WO,
 C_GAIN2, C_SHIFT2, C_W1, C_B1, C_W2, C_B2, C_TABLE, C_BASIS) = range(COPIES)
FIRST_COPIES = (C_TABLE, C_WR, C_X, C_GAIN1, C_SHIFT1, C_WQ, C_WK, C_WV, C_START, C_ARRIVED, C_CBIAS, C_PBIAS)
LATER_COPIES = (C_WO, C_GAIN2, C_SHIFT2, C_W1, C_B1, C_COT, C_W2, C_B2, C_BASIS)


def layer_kernel(place, horizon, *refs):
    sources, outputs, targets = refs[:COPIES], refs[COPIES : COPIES + 3], refs[COPIES + 3 : 2 * COPIES + 3]
    sems, scratch = refs[2 * COPIES + 3], refs[2 * COPIES + 4 :]
    moves = [pltpu.make_async_copy(a, b, sems.at[i]) for i, (a, b) in enumerate(zip(sources, targets))]
    for i in FIRST_COPIES + LATER_COPIES:
        moves[i].start()
    compute_layer(place, horizon, moves, *targets, *outputs, *scratch)


def compute_layer(
    place, horizon, moves, x, start, arrived, cot, gain1, shift1, wq, wk, wv, wr, cbias, pbias, wo,
    gain2, shift2, w1, b1, w2, b2, table, basis,
    out, dx, grads,
    nl, xhat, rstd, content, placed, keys, values, relblock, raw, probs, mixed,
    hid, n2, act, bpre, bmix, bhid, bhl, bcont, braw, kgm, kgs, vgm, vgs, vec,
):
    rows = x.shape[0]
    segments = rows // SEG
    position = place[0]
    vec[...] = jnp.zeros_like(vec)

    def loop(count, step):
        def body(i, carry):
            step(i)
            return carry
        lax.fori_loop(0, count, body, 0)

    for i in FIRST_COPIES:
        moves[i].wait()
    rel = dot(table[...], wr[...])
    wide_head = lax.broadcasted_iota(jnp.int32, (LANES, FEATURES), 1) // HEAD_DIM
    for h in range(HEADS):
        relblock[h * LANES : (h + 1) * LANES] = jnp.where(wide_head == h, rel, 0.0).astype(BF)

    def project(normed, at, count):
        keys[pl.ds(at, count)] = dot(normed, wk[...]).astype(BF)
        values[pl.ds(at, count)] = dot(normed, wv[...]).astype(BF)

    memory = jnp.where(position == 0, start[...].astype(F32), arrived[...].astype(F32))
    unit, scale = normalize(memory)
    xhat[0:SEG] = unit
    rstd[0:SEG] = scale
    normed = (unit * gain1[...] + shift1[...]).astype(BF)
    nl[0:SEG] = normed
    project(normed, 0, SEG)
    tail = keys.shape[0] - rows - SEG
    keys[rows + SEG :] = jnp.zeros((tail, FEATURES), BF)
    values[rows + SEG :] = jnp.zeros((tail, FEATURES), BF)

    block = 4 * SEG

    def first_rows(i):
        r = pl.multiple_of(i * block, block)
        unit, scale = normalize(x[pl.ds(r, block)].astype(F32))
        to = pl.multiple_of(r + SEG, SEG)
        xhat[pl.ds(to, block)] = unit
        rstd[pl.ds(to, block)] = scale
        normed = (unit * gain1[...] + shift1[...]).astype(BF)
        nl[pl.ds(to, block)] = normed
        project(normed, to, block)
        query = dot(normed, wq[...])
        content[pl.ds(r, block)] = (query + cbias[...]).astype(BF)
        low = (query + pbias[...]).astype(BF)
        placed[pl.ds(r, block)] = low
        raw[pl.ds(r, block)] = dot_t(low, relblock[...])

    loop(rows // block, first_rows)

    lane_head = lax.broadcasted_iota(jnp.int32, (SEG, LANES), 1) // HEAD_DIM
    head_masks = [(lane_head == h).astype(F32).astype(BF) for h in range(GROUP)]
    key_at = lax.broadcasted_iota(jnp.int32, (SEG, LANES), 1)
    query_at = lax.broadcasted_iota(jnp.int32, (SEG, LANES), 0) + SEG

    low_row = 7 - (query_at & 7)
    row_bits = [(step, (low_row & step) != 0) for step in (1, 2, 4)]

    def attend(s):
        r = pl.multiple_of(s * SEG, SEG)
        number = position * segments + s
        current = horizon[0, number]
        previous = jnp.where(number == 0, SEG // STEP, horizon[0, jnp.maximum(number - 1, 0)])
        live = key_at < jnp.where(key_at < SEG, STEP * previous, SEG + STEP * current)
        allowed = (key_at <= query_at) & (live | (key_at == query_at))
        for g in range(HEADS // GROUP):
            lanes = slice(g * LANES, (g + 1) * LANES)
            direct = dot_t(stack_heads(content[pl.ds(r, SEG), lanes], head_masks), keys[pl.ds(r, LANES), lanes])
            lows = []
            for h in range(GROUP):
                head = g * GROUP + h
                shifted = pltpu.roll(
                    raw[pl.ds(r, SEG), head * LANES : (head + 1) * LANES],
                    LANES - SEG + 1, 1, stride=1, stride_axis=0,
                )
                scores = jnp.where(allowed, (direct[h * SEG : (h + 1) * SEG] + shifted) * SCALING, MASKED)
                exponent = jnp.exp(scores - jnp.max(scores, axis=-1, keepdims=True))
                prob = exponent / jnp.sum(exponent, axis=-1, keepdims=True)
                probs[pl.ds(pl.multiple_of((s * HEADS + head) * SEG, SEG), SEG)] = prob
                lows.append(prob.astype(BF))
            both = dot(jnp.concatenate(lows, axis=0), values[pl.ds(r, LANES), lanes])
            mixed[pl.ds(r, SEG), lanes] = pick_heads(both, lane_head).astype(BF)

    loop(segments, attend)

    for i in LATER_COPIES:
        moves[i].wait()

    def feed(i):
        r = pl.multiple_of(i * block, block)
        at = pl.ds(r, block)
        hidden = x[at].astype(F32) + dot(mixed[at], wo[...])
        unit, scale = normalize(hidden)
        low = (unit * gain2[...] + shift2[...]).astype(BF)
        n2[at] = low
        back = cot[at]
        for f in range(HIDDEN // FEATURES):
            cols = slice(f * FEATURES, (f + 1) * FEATURES)
            v = dot(low, w1[:, cols]) + b1[:, cols]
            square = v * v
            half = 0.5 + 0.5 * jnp.tanh(v * (GELU_A + GELU_B * square))
            active = v * half
            act[at, cols] = active.astype(BF)
            slope = half + (2.0 * active) * (1.0 - half) * (GELU_A + (3.0 * GELU_B) * square)
            grad = dot_t(back, w2[cols]) * slope
            vec[V_EXPAND + f : V_EXPAND + f + 1] += column_sum(grad)
            bpre[at, cols] = grad.astype(BF)
        out[at] = (hidden + dot(act[at], w2[...]) + b2[...]).astype(BF)
        back = back.astype(F32)
        bn = dot_t(bpre[at], w1[...])
        vec[V_SHRINK : V_SHRINK + 1] += column_sum(back)
        vec[V_GAIN2 : V_GAIN2 + 1] += column_sum(bn * unit)
        vec[V_SHIFT2 : V_SHIFT2 + 1] += column_sum(bn)
        u = bn * gain2[...]
        inner = u - jnp.mean(u, axis=-1, keepdims=True) - unit * jnp.mean(u * unit, axis=-1, keepdims=True)
        bh = back + inner * scale
        bhid[at] = bh
        bl = bh.astype(BF)
        bhl[at] = bl
        bmix[at] = dot_t(bl, wo[...]).astype(BF)

    loop(rows // block, feed)

    for f in range(HIDDEN // FEATURES):
        cols = slice(f * FEATURES, (f + 1) * FEATURES)
        grads[EXPAND_AT + f * FEATURES : EXPAND_AT + (f + 1) * FEATURES] = t_dot(n2[...], bpre[:, cols]).astype(BF)
        grads[SHRINK_AT + f * FEATURES : SHRINK_AT + (f + 1) * FEATURES] = t_dot(act[:, cols], cot[...]).astype(BF)
    grads[OUTPUT_AT : OUTPUT_AT + FEATURES] = t_dot(mixed[...], bhl[...]).astype(BF)

    def attend_back(s):
        r = pl.multiple_of(s * SEG, SEG)
        at = pl.ds(r, SEG)
        for g in range(HEADS // GROUP):
            lanes = slice(g * LANES, (g + 1) * LANES)
            window = pl.ds(r, LANES)
            back = stack_heads(bmix[at, lanes], head_masks)
            wide = dot_t(back, values[window, lanes])
            lows, grad_lows = [], []
            for h in range(GROUP):
                head = g * GROUP + h
                prob = probs[pl.ds(pl.multiple_of((s * HEADS + head) * SEG, SEG), SEG)]
                bp = wide[h * SEG : (h + 1) * SEG]
                bs = prob * (bp - jnp.sum(bp * prob, axis=-1, keepdims=True))
                lows.append(prob.astype(BF))
                grad_lows.append(bs.astype(BF))
                braw[at, head * LANES : (head + 1) * LANES] = unshift(bs, row_bits).astype(BF)
            low = jnp.concatenate(lows, axis=0)
            grad_low = jnp.concatenate(grad_lows, axis=0)
            vg = t_dot(low, back).astype(BF)
            vgm[at, lanes] = vg[0:SEG]
            vgs[at, lanes] = vg[SEG : 2 * SEG]
            kg = (t_dot(grad_low, stack_heads(content[at, lanes], head_masks)) * SCALING).astype(BF)
            kgm[at, lanes] = kg[0:SEG]
            kgs[at, lanes] = kg[SEG : 2 * SEG]
            bcont[at, lanes] = pick_heads(dot(grad_low, keys[window, lanes]), lane_head) * SCALING

    loop(segments, attend_back)

    def last_rows(i):
        r = pl.multiple_of(i * block, block)
        at = pl.ds(r, block)
        to = pl.ds(pl.multiple_of(r + SEG, SEG), block)
        bplace = dot(braw[at], relblock[...]) * SCALING
        bc = bcont[at]
        vec[V_CONTENT : V_CONTENT + 1] += column_sum(bc)
        vec[V_POSITION : V_POSITION + 1] += column_sum(bplace)
        bq = (bc + bplace).astype(BF)
        bhl[at] = bq
        bn = dot_t(bq, wq[...]) + dot_t(kgs[at], wk[...]) + dot_t(vgs[at], wv[...])
        bm = dot_t(kgm[at], wk[...]) + dot_t(vgm[at], wv[...])
        unit = xhat[to]
        vec[V_GAIN1 : V_GAIN1 + 1] += column_sum(bn * unit) + column_sum(bm * xhat[at])
        vec[V_SHIFT1 : V_SHIFT1 + 1] += column_sum(bn) + column_sum(bm)
        u = bn * gain1[...]
        inner = u - jnp.mean(u, axis=-1, keepdims=True) - unit * jnp.mean(u * unit, axis=-1, keepdims=True)
        dx[at] = (bhid[at] + inner * rstd[to]).astype(BF)

    loop(rows // block, last_rows)

    segment_rows = nl[SEG : SEG + rows]
    memory_rows = nl[0:rows]
    grads[QUERY_AT : QUERY_AT + FEATURES] = t_dot(segment_rows, bhl[...]).astype(BF)
    grads[KEY_AT : KEY_AT + FEATURES] = (t_dot(segment_rows, kgs[...]) + t_dot(memory_rows, kgm[...])).astype(BF)
    grads[VALUE_AT : VALUE_AT + FEATURES] = (t_dot(segment_rows, vgs[...]) + t_dot(memory_rows, vgm[...])).astype(BF)
    for g in range(HEADS // GROUP):
        lanes = slice(g * LANES, (g + 1) * LANES)
        across = t_dot(placed[:, lanes], braw[:, g * GROUP * LANES : (g + 1) * GROUP * LANES])
        back = jnp.concatenate(
            [across[h * HEAD_DIM : (h + 1) * HEAD_DIM, h * LANES : (h + 1) * LANES] for h in range(GROUP)], axis=0
        ) * SCALING
        high = back.astype(BF)
        low = (back - high.astype(F32)).astype(BF)
        cosines = dot_t(basis[0:LANES], high) + (dot_t(basis[LANES:], high) + dot_t(basis[0:LANES], low))
        grads[RELATIVE_AT : RELATIVE_AT + LANES, lanes] = cosines.astype(BF)
    grads[VECTOR_AT : VECTOR_AT + VECTOR_ROWS] = vec[...].astype(BF)
    grads[VECTOR_AT + VECTOR_ROWS :] = jnp.zeros((BUFFER_ROWS - VECTOR_AT - VECTOR_ROWS, FEATURES), BF)


def run_layer(place, horizon, x, start, arrived, cot, table, basis, params):
    rows = x.shape[0]
    operands = (x, start, arrived, cot, *params, table, basis)
    vmem = pl.BlockSpec(memory_space=pltpu.VMEM)
    hbm = pl.BlockSpec(memory_space=pltpu.HBM)
    smem = pl.BlockSpec(memory_space=pltpu.SMEM)
    padded = rows + SEG + LANES - 2 * SEG
    scratch = [
        pltpu.VMEM((rows + SEG, FEATURES), BF),
        pltpu.VMEM((rows + SEG, FEATURES), F32),
        pltpu.VMEM((rows + SEG, 1), F32),
        pltpu.VMEM((rows, FEATURES), BF),
        pltpu.VMEM((rows, FEATURES), BF),
        pltpu.VMEM((padded, FEATURES), BF),
        pltpu.VMEM((padded, FEATURES), BF),
        pltpu.VMEM((HEADS * LANES, FEATURES), BF),
        pltpu.VMEM((rows, HEADS * LANES), F32),
        pltpu.VMEM((rows * HEADS, LANES), F32),
        pltpu.VMEM((rows, FEATURES), BF),
        pltpu.VMEM((rows, FEATURES), F32),
        pltpu.VMEM((rows, FEATURES), BF),
        pltpu.VMEM((rows, HIDDEN), BF),
        pltpu.VMEM((rows, HIDDEN), BF),
        pltpu.VMEM((rows, FEATURES), BF),
        pltpu.VMEM((rows, FEATURES), F32),
        pltpu.VMEM((rows, FEATURES), BF),
        pltpu.VMEM((rows, FEATURES), F32),
        pltpu.VMEM((rows, HEADS * LANES), BF),
        pltpu.VMEM((rows, FEATURES), BF),
        pltpu.VMEM((rows, FEATURES), BF),
        pltpu.VMEM((rows, FEATURES), BF),
        pltpu.VMEM((rows, FEATURES), BF),
        pltpu.VMEM((VECTOR_ROWS, FEATURES), F32),
    ]
    return pl.pallas_call(
        layer_kernel,
        out_shape=(
            jax.ShapeDtypeStruct((rows, FEATURES), BF),
            jax.ShapeDtypeStruct((rows, FEATURES), BF),
            jax.ShapeDtypeStruct((BUFFER_ROWS, FEATURES), BF),
        ),
        in_specs=[smem, smem] + [hbm] * COPIES,
        out_specs=(vmem, vmem, vmem),
        scratch_shapes=[pltpu.VMEM(a.shape, a.dtype) for a in operands]
        + [pltpu.SemaphoreType.DMA((COPIES,))]
        + scratch,
        compiler_params=pltpu.CompilerParams(vmem_limit_bytes=63 * 1024 * 1024),
        name="layer",
    )(place, horizon, *operands)


def unpack_kernel(
    place, own, other, turned,
    gain1, shift1, wq, wk, wv, wr, cbias, pbias, wo, gain2, shift2, w1, b1, w2, b2,
    whole,
):
    first = place[1] == 0
    half = BUFFER_ROWS // 2

    @pl.when(first)
    def _():
        whole[0:half] = own[...]
        whole[half:] = other[...]

    @pl.when(jnp.logical_not(first))
    def _():
        whole[0:half] = other[...]
        whole[half:] = own[...]

    for f in range(HIDDEN // FEATURES):
        w1[:, f * FEATURES : (f + 1) * FEATURES] = whole[
            EXPAND_AT + f * FEATURES : EXPAND_AT + (f + 1) * FEATURES
        ].astype(F32)
    w2[...] = whole[SHRINK_AT : SHRINK_AT + HIDDEN].astype(F32)
    for ref, at in ((wq, QUERY_AT), (wk, KEY_AT), (wv, VALUE_AT), (wo, OUTPUT_AT)):
        ref[...] = whole[at : at + FEATURES].astype(F32)
    cosines = whole[RELATIVE_AT : RELATIVE_AT + LANES]
    wr[...] = t_dot(turned[0:LANES], cosines) + t_dot(turned[LANES:], cosines)
    vectors = whole[VECTOR_AT : VECTOR_AT + VECTOR_ROWS].astype(F32)
    for ref, at in (
        (cbias, V_CONTENT), (pbias, V_POSITION), (gain1, V_GAIN1), (shift1, V_SHIFT1),
        (gain2, V_GAIN2), (shift2, V_SHIFT2), (b2, V_SHRINK),
    ):
        ref[...] = vectors[at]
    for f in range(HIDDEN // FEATURES):
        b1[f * FEATURES : (f + 1) * FEATURES] = vectors[V_EXPAND + f]


def unpack(place, own, other, turned):
    vmem = pl.BlockSpec(memory_space=pltpu.VMEM)
    smem = pl.BlockSpec(memory_space=pltpu.SMEM)
    vector = jax.ShapeDtypeStruct((FEATURES,), F32)
    square = jax.ShapeDtypeStruct((FEATURES, FEATURES), F32)
    shapes = (
        vector, vector, square, square, square, square, vector, vector, square, vector, vector,
        jax.ShapeDtypeStruct((FEATURES, HIDDEN), F32),
        jax.ShapeDtypeStruct((HIDDEN,), F32),
        jax.ShapeDtypeStruct((HIDDEN, FEATURES), F32),
        vector,
    )
    return pl.pallas_call(
        unpack_kernel,
        out_shape=shapes,
        in_specs=[smem, vmem, vmem, vmem],
        out_specs=(vmem,) * len(shapes),
        scratch_shapes=[pltpu.VMEM((BUFFER_ROWS, FEATURES), BF)],
        compiler_params=pltpu.CompilerParams(vmem_limit_bytes=32 * 1024 * 1024),
        name="unpack",
    )(place, own, other, turned)


AXES = ("tm", "roll")


def exchange_plan(roll_count, tm_count):
    tm_bits = tm_count.bit_length() - 1
    roll_bits = roll_count.bit_length() - 1
    high = [roll_bits + b for b in range(1, tm_bits)]
    rolls = list(range(roll_bits))
    even = high + rolls
    odd = rolls[:1] + high + rolls[1:]
    return [(roll_bits, roll_bits)] + list(zip(even, odd))


def swap(value, bits, roll_count, count):
    even, odd = bits
    pairs = [(d, d ^ (1 << (odd if (d // roll_count) & 1 else even))) for d in range(count)]
    return lax.ppermute(value, AXES, pairs)


def add_low(a, b):
    return (a.astype(F32) + b.astype(F32)).astype(BF)


def sum_everywhere(buffer, core):
    roll_count, tm_count = lax.axis_size("roll"), lax.axis_size("tm")
    count = roll_count * tm_count
    me = lax.axis_index("tm") * roll_count + lax.axis_index("roll")
    stages = exchange_plan(roll_count, tm_count)
    halving = 4
    bits = []
    for even, odd in stages[:halving]:
        bit = jnp.where(core == 0, (me >> even) & 1, (me >> odd) & 1)
        half = buffer.shape[0] // 2
        sent = lax.dynamic_slice_in_dim(buffer, (1 - bit) * half, half, 0)
        kept = lax.dynamic_slice_in_dim(buffer, bit * half, half, 0)
        buffer = add_low(kept, swap(sent, (even, odd), roll_count, count))
        bits.append(bit)
    for even, odd in stages[halving:]:
        buffer = add_low(buffer, swap(buffer, (even, odd), roll_count, count))
    for (even, odd), bit in list(zip(stages, bits))[:0:-1]:
        other = swap(buffer, (even, odd), roll_count, count)
        first = bit == 0
        buffer = jnp.concatenate([jnp.where(first, buffer, other), jnp.where(first, other, buffer)], axis=0)
    return buffer, swap(buffer, stages[0], roll_count, count)


def body(
    layer_input, start_memory, horizon, cotangent, first_gain, first_shift, query_projection_weight,
    key_projection_weight, value_projection_weight, relative_weight, content_bias, position_bias,
    output_weight, second_gain, second_shift, expand_weight, expand_bias, shrink_weight, shrink_bias,
):
    rollouts, columns, features = layer_input.shape
    x = layer_input.reshape(rollouts * columns, features)
    position = lax.axis_index("tm")
    tm_count = lax.axis_size("tm")
    arrived = lax.ppermute(x[-SEG:], "tm", [(i, i + 1) for i in range(tm_count - 1)])
    core = position & 1
    place = jnp.stack([position, core]).astype(jnp.int32)
    table = jnp.asarray(position_rows())
    basis, turned = (jnp.asarray(part) for part in relative_basis())

    def row(v):
        return v.reshape(1, -1)

    params = (
        row(first_gain), row(first_shift), query_projection_weight, key_projection_weight,
        value_projection_weight, relative_weight, row(content_bias), row(position_bias), output_weight,
        row(second_gain), row(second_shift), expand_weight, row(expand_bias), shrink_weight, row(shrink_bias),
    )
    out, dx, grads = run_layer(
        place, horizon, x, start_memory.reshape(SEG, features), arrived,
        cotangent.reshape(rollouts * columns, features), table, basis, params,
    )
    own, other = sum_everywhere(grads, core)
    summed = unpack(place, own, other, turned)
    return (out.reshape(layer_input.shape), dx.reshape(layer_input.shape)) + tuple(summed)


def solution(mesh):
    in_specs = (
        P("roll", "tm", None), P("roll", None, None), P("roll", None), P("roll", "tm", None),
    ) + (P(),) * 15
    out_specs = (P("roll", "tm", None), P("roll", "tm", None)) + (P(),) * 15
    return jax.shard_map(body, mesh=mesh, in_specs=in_specs, out_specs=out_specs, check_vma=False)
```

```python
import functools
import math

import jax
import jax.numpy as jnp
import numpy as np
from jax import lax
from jax.experimental import pallas as pl
from jax.experimental.pallas import tpu as pltpu
from jax.sharding import PartitionSpec as P

HEADS = 8
HEAD_DIM = 32
SEG = 48
STEP = 3
FEATURES = 256
HIDDEN = 1024
LANES = 128
GROUP = LANES // HEAD_DIM
EPSILON = 1e-05
MASKED = -4000000000.0
SCALING = 1.0 / math.sqrt(HEAD_DIM)
SCALING_BITS = SCALING / math.log(2.0)
GELU_A = 0.7978845608028654
GELU_B = 0.044715 * GELU_A
BF = jnp.bfloat16
F32 = jnp.float32

EXPAND_AT = 0
SHRINK_AT = 1024
QUERY_AT = 2048
KEY_AT = 2304
VALUE_AT = 2560
OUTPUT_AT = 2816
RELATIVE_AT = 3072
VECTOR_AT = 3200
BUFFER_ROWS = 3328
PIPES = 2
PART_ROWS = BUFFER_ROWS // (2 * PIPES)
PAIR = 4
PAIR_BACK = 8
(V_CONTENT, V_POSITION, V_GAIN1, V_SHIFT1, V_GAIN2, V_SHIFT2, V_SHRINK, V_EXPAND) = range(8)
VECTOR_ROWS = 16


def position_rows():
    distance = (2 * SEG - 1 - np.arange(2 * SEG)).astype(np.float32)
    freqs = 10000.0 ** (-(2.0 * np.arange(FEATURES // 2)) / FEATURES)
    angles = distance[:, None] * freqs.astype(np.float32)[None, :]
    table = np.concatenate([np.sin(angles), np.cos(angles)], axis=-1)
    return np.pad(table, ((0, LANES - 2 * SEG), (0, 0))).astype(BF)


def relative_basis():
    count = 2 * SEG
    k, c = np.arange(count)[:, None], np.arange(count)[None, :]
    basis = np.cos(np.pi * k * (2 * c + 1) / (2 * count)) * np.where(k == 0, np.sqrt(1.0 / count), np.sqrt(2.0 / count))
    basis = np.pad(basis, ((0, LANES - count), (0, LANES - count)))

    def parts(values):
        high = values.astype(BF)
        low = (values - high.astype(np.float64)).astype(BF)
        return np.concatenate([high, low], axis=0)

    return parts(basis), parts(basis @ position_rows().astype(np.float64))


def tables():
    return jnp.asarray(position_rows()), jnp.asarray(relative_basis()[0])


def dot(a, b):
    return lax.dot_general(a, b, (((1,), (0,)), ((), ())), preferred_element_type=F32)


def dot_t(a, b):
    return lax.dot_general(a, b, (((1,), (1,)), ((), ())), preferred_element_type=F32)


def t_dot(a, b):
    return lax.dot_general(a, b, (((0,), (0,)), ((), ())), preferred_element_type=F32)


def normalize(rows):
    center = rows - jnp.mean(rows, axis=-1, keepdims=True)
    spread = jnp.mean(center * center, axis=-1, keepdims=True)
    scale = lax.rsqrt(spread + EPSILON)
    return center * scale, scale


def column_sum(rows):
    return jnp.sum(rows, axis=0, keepdims=True)


def stack_heads(rows, head_masks):
    return jnp.concatenate([rows * mask for mask in head_masks], axis=0)


def unshift(rows, row_bits):
    rolled = jnp.concatenate(
        [pltpu.roll(rows[a : a + 8], SEG - 8 - a, 1) for a in range(0, SEG - 8, 8)] + [rows[SEG - 8 :]], axis=0
    )
    for step, bit in row_bits:
        rolled = jnp.where(bit, pltpu.roll(rolled, step, 1), rolled)
    return rolled


def pick_heads(rows, lane_head):
    picked = rows[0:SEG]
    for h in range(1, GROUP):
        picked = jnp.where(lane_head == h, rows[h * SEG : (h + 1) * SEG], picked)
    return picked


COPIES = 21
(C_X, C_START, C_ARRIVED, C_COT, C_GAIN1, C_SHIFT1, C_WQ, C_WK, C_WV, C_WR, C_CBIAS, C_PBIAS, C_WO,
 C_GAIN2, C_SHIFT2, C_W1, C_B1, C_W2, C_B2, C_TABLE, C_BASIS) = range(COPIES)
FIRST_COPIES = (C_TABLE, C_WR, C_X, C_GAIN1, C_SHIFT1, C_WQ, C_WK, C_WV, C_START, C_ARRIVED, C_CBIAS, C_PBIAS)
LATER_COPIES = (C_WO, C_GAIN2, C_SHIFT2, C_W1, C_B1, C_COT, C_W2, C_B2, C_BASIS)


def layer_kernel(place, horizon, *refs):
    sources, refs = refs[:COPIES], refs[COPIES:]
    outputs, halves, refs = refs[:2], refs[2 : 2 + 2 * PIPES], refs[2 + 2 * PIPES :]
    targets, (sems, half_sems, grads, *scratch) = refs[:COPIES], refs[COPIES:]
    moves = [pltpu.make_async_copy(a, b, sems.at[i]) for i, (a, b) in enumerate(zip(sources, targets))]
    for i in FIRST_COPIES + LATER_COPIES:
        moves[i].start()
    compute_layer(place, horizon, moves, *targets, *outputs, grads, *scratch)
    core = place[1]
    leaving = []
    for p in range(PIPES):
        for k, half in enumerate((core, 1 - core)):
            at = pl.ds(pl.multiple_of((half * PIPES + p) * PART_ROWS, PART_ROWS), PART_ROWS)
            leaving.append(pltpu.make_async_copy(grads.at[at], halves[2 * p + k], half_sems.at[2 * p + k]))
    for move in leaving:
        move.start()
    for move in leaving:
        move.wait()


def compute_layer(
    place, horizon, moves, x, start, arrived, cot, gain1, shift1, wq, wk, wv, wr, cbias, pbias, wo,
    gain2, shift2, w1, b1, w2, b2, table, basis,
    out, dx, grads,
    nl, xhat, rstd, content, placed, keys, values, relblock, raw, probs, mixed,
    hid, n2, act, bpre, bmix, bhid, bhl, bcont, braw, kgm, kgs, vgm, vgs, vec,
):
    rows = x.shape[0]
    segments = rows // SEG
    position = place[0]
    vec[...] = jnp.zeros_like(vec)

    def loop(count, step, unroll=1):
        def body(i, carry):
            step(i)
            return carry
        lax.fori_loop(0, count, body, 0, unroll=unroll)

    for i in FIRST_COPIES:
        moves[i].wait()
    rel = dot(table[...], wr[...])
    wide_head = lax.broadcasted_iota(jnp.int32, (LANES, FEATURES), 1) // HEAD_DIM
    for h in range(HEADS):
        relblock[h * LANES : (h + 1) * LANES] = jnp.where(wide_head == h, rel, 0.0).astype(BF)

    def project(normed, at, count):
        keys[pl.ds(at, count)] = dot(normed, wk[...]).astype(BF)
        value = dot(normed, wv[...]).astype(BF)
        for g in range(HEADS // GROUP):
            values[pl.ds(at, count), 2 * g * LANES : (2 * g + 1) * LANES] = value[:, g * LANES : (g + 1) * LANES]

    memory = jnp.where(position == 0, start[...].astype(F32), arrived[...].astype(F32))
    unit, scale = normalize(memory)
    xhat[0:SEG] = unit
    rstd[0:SEG] = scale
    normed = (unit * gain1[...] + shift1[...]).astype(BF)
    nl[0:SEG] = normed
    project(normed, 0, SEG)
    tail = keys.shape[0] - rows - SEG
    keys[rows + SEG :] = jnp.zeros((tail, FEATURES), BF)
    values[rows + SEG :] = jnp.zeros((tail, 2 * FEATURES), BF)
    for g in range(HEADS // GROUP):
        values[:, (2 * g + 1) * LANES : (2 * g + 2) * LANES] = jnp.ones((values.shape[0], LANES), BF)

    block = 4 * SEG

    def first_rows(i):
        r = pl.multiple_of(i * block, block)
        unit, scale = normalize(x[pl.ds(r, block)].astype(F32))
        to = pl.multiple_of(r + SEG, SEG)
        xhat[pl.ds(to, block)] = unit
        rstd[pl.ds(to, block)] = scale
        normed = (unit * gain1[...] + shift1[...]).astype(BF)
        nl[pl.ds(to, block)] = normed
        project(normed, to, block)
        query = dot(normed, wq[...])
        content[pl.ds(r, block)] = (query + cbias[...]).astype(BF)
        low = (query + pbias[...]).astype(BF)
        placed[pl.ds(r, block)] = low
        raw[pl.ds(r, block)] = dot_t(low, relblock[...])

    loop(rows // block, first_rows)

    lane_head = lax.broadcasted_iota(jnp.int32, (SEG, LANES), 1) // HEAD_DIM
    head_masks = [(lane_head == h).astype(F32).astype(BF) for h in range(GROUP)]
    key_at = lax.broadcasted_iota(jnp.int32, (SEG, LANES), 1)
    query_at = lax.broadcasted_iota(jnp.int32, (SEG, LANES), 0) + SEG

    low_row = 7 - (query_at & 7)
    row_bits = [(step, (low_row & step) != 0) for step in (1, 2, 4)]

    def attend(i):
        units = []
        for k in range(PAIR):
            s = i * PAIR + k
            r = pl.multiple_of(s * SEG, SEG)
            number = position * segments + s
            current = horizon[0, number]
            previous = jnp.where(number == 0, SEG // STEP, horizon[0, jnp.maximum(number - 1, 0)])
            live = key_at < jnp.where(key_at < SEG, STEP * previous, SEG + STEP * current)
            allowed = (key_at <= query_at) & (live | (key_at == query_at))
            units += [(s, r, allowed, g, slice(g * LANES, (g + 1) * LANES)) for g in range(HEADS // GROUP)]
        direct = [
            dot_t(stack_heads(content[pl.ds(r, SEG), lanes], head_masks), keys[pl.ds(r, LANES), lanes])
            for s, r, allowed, g, lanes in units
        ]
        scores = [
            [
                jnp.where(
                    allowed,
                    d[h * SEG : (h + 1) * SEG]
                    + pltpu.roll(
                        raw[pl.ds(r, SEG), (g * GROUP + h) * LANES : (g * GROUP + h + 1) * LANES],
                        LANES - SEG + 1, 1, stride=1, stride_axis=0,
                    ),
                    MASKED,
                )
                for h in range(GROUP)
            ]
            for d, (s, r, allowed, g, lanes) in zip(direct, units)
        ]
        tops = [[jnp.max(v, axis=-1, keepdims=True) for v in vs] for vs in scores]
        lows = [
            jnp.concatenate([jnp.exp2((v - t) * SCALING_BITS).astype(BF) for v, t in zip(vs, ts)], axis=0)
            for vs, ts in zip(scores, tops)
        ]
        boths = [
            dot(low, values[pl.ds(r, LANES), 2 * g * LANES : (2 * g + 2) * LANES])
            for low, (s, r, allowed, g, lanes) in zip(lows, units)
        ]
        for low, both, (s, r, allowed, g, lanes) in zip(lows, boths, units):
            inverse = 1.0 / both[:, LANES:]
            mx = pick_heads(both[:, :LANES] * inverse, lane_head)
            mixed[pl.ds(r, SEG), lanes] = mx.astype(BF)
            bcont[pl.ds(r, SEG), lanes] = mx
            for h in range(GROUP):
                at = pl.ds(pl.multiple_of((s * HEADS + g * GROUP + h) * SEG, SEG), SEG)
                probs[at] = low[h * SEG : (h + 1) * SEG].astype(F32) * inverse[h * SEG : (h + 1) * SEG]

    loop(segments // PAIR, attend)

    for i in LATER_COPIES:
        moves[i].wait()

    def feed(i):
        r = pl.multiple_of(i * block, block)
        at = pl.ds(r, block)
        hidden = x[at].astype(F32) + dot(mixed[at], wo[...])
        unit, scale = normalize(hidden)
        low = (unit * gain2[...] + shift2[...]).astype(BF)
        n2[at] = low
        back = cot[at]
        for f in range(HIDDEN // FEATURES):
            cols = slice(f * FEATURES, (f + 1) * FEATURES)
            v = dot(low, w1[:, cols]) + b1[:, cols]
            square = v * v
            half = 0.5 + 0.5 * jnp.tanh(v * (GELU_A + GELU_B * square))
            active = v * half
            act[at, cols] = active.astype(BF)
            slope = half + (2.0 * active) * (1.0 - half) * (GELU_A + (3.0 * GELU_B) * square)
            grad = dot_t(back, w2[cols]) * slope
            vec[V_EXPAND + f : V_EXPAND + f + 1] += column_sum(grad)
            bpre[at, cols] = grad.astype(BF)
        out[at] = (hidden + dot(act[at], w2[...]) + b2[...]).astype(BF)
        back = back.astype(F32)
        bn = dot_t(bpre[at], w1[...])
        vec[V_SHRINK : V_SHRINK + 1] += column_sum(back)
        vec[V_GAIN2 : V_GAIN2 + 1] += column_sum(bn * unit)
        vec[V_SHIFT2 : V_SHIFT2 + 1] += column_sum(bn)
        u = bn * gain2[...]
        inner = u - jnp.mean(u, axis=-1, keepdims=True) - unit * jnp.mean(u * unit, axis=-1, keepdims=True)
        bh = back + inner * scale
        bhid[at] = bh
        bl = bh.astype(BF)
        bhl[at] = bl
        bmix[at] = dot_t(bl, wo[...]).astype(BF)

    loop(rows // block, feed)

    for f in range(HIDDEN // FEATURES):
        cols = slice(f * FEATURES, (f + 1) * FEATURES)
        grads[EXPAND_AT + f * FEATURES : EXPAND_AT + (f + 1) * FEATURES] = t_dot(n2[...], bpre[:, cols]).astype(BF)
        grads[SHRINK_AT + f * FEATURES : SHRINK_AT + (f + 1) * FEATURES] = t_dot(act[:, cols], cot[...]).astype(BF)
    grads[OUTPUT_AT : OUTPUT_AT + FEATURES] = t_dot(mixed[...], bhl[...]).astype(BF)

    def attend_back(i):
        units = []
        for k in range(PAIR_BACK):
            s = i * PAIR_BACK + k
            r = pl.multiple_of(s * SEG, SEG)
            units += [
                (s, pl.ds(r, SEG), pl.ds(r, LANES), g, slice(g * LANES, (g + 1) * LANES)) for g in range(HEADS // GROUP)
            ]
        backs, wides = [], []
        for s, at, window, g, lanes in units:
            rows = bmix[at, lanes]
            back = stack_heads(rows, head_masks)
            product = rows.astype(F32) * -bcont[at, lanes]
            high = product.astype(BF)
            rest = (product - high.astype(F32)).astype(BF)
            along = jnp.concatenate([back, stack_heads(high, head_masks)], axis=1)
            wide = dot_t(along, values[window, 2 * g * LANES : (2 * g + 2) * LANES])
            wide += dot_t(stack_heads(rest, head_masks), values[window, (2 * g + 1) * LANES : (2 * g + 2) * LANES])
            backs.append(back)
            wides.append(wide)
        lows, grads_low = [], []
        for wide, (s, at, window, g, lanes) in zip(wides, units):
            prob = probs[pl.ds(pl.multiple_of((s * HEADS + g * GROUP) * SEG, SEG), GROUP * SEG)]
            bs = prob * wide
            lows.append(prob.astype(BF))
            grads_low.append(bs.astype(BF))
            for h in range(GROUP):
                head = g * GROUP + h
                braw[at, head * LANES : (head + 1) * LANES] = unshift(
                    bs[h * SEG : (h + 1) * SEG], row_bits
                ).astype(BF)
        for low, grad_low, back, (s, at, window, g, lanes) in zip(lows, grads_low, backs, units):
            vg = t_dot(low, back).astype(BF)
            vgm[at, lanes] = vg[0:SEG]
            vgs[at, lanes] = vg[SEG : 2 * SEG]
            kg = (t_dot(grad_low, stack_heads(content[at, lanes], head_masks)) * SCALING).astype(BF)
            kgm[at, lanes] = kg[0:SEG]
            kgs[at, lanes] = kg[SEG : 2 * SEG]
            bcont[at, lanes] = pick_heads(dot(grad_low, keys[window, lanes]), lane_head) * SCALING

    loop(segments // PAIR_BACK, attend_back)

    def last_rows(i):
        r = pl.multiple_of(i * block, block)
        at = pl.ds(r, block)
        to = pl.ds(pl.multiple_of(r + SEG, SEG), block)
        bplace = dot(braw[at], relblock[...]) * SCALING
        bc = bcont[at]
        vec[V_CONTENT : V_CONTENT + 1] += column_sum(bc)
        vec[V_POSITION : V_POSITION + 1] += column_sum(bplace)
        bq = (bc + bplace).astype(BF)
        bhl[at] = bq
        bn = dot_t(bq, wq[...]) + dot_t(kgs[at], wk[...]) + dot_t(vgs[at], wv[...])
        bm = dot_t(kgm[at], wk[...]) + dot_t(vgm[at], wv[...])
        unit = xhat[to]
        vec[V_GAIN1 : V_GAIN1 + 1] += column_sum(bn * unit) + column_sum(bm * xhat[at])
        vec[V_SHIFT1 : V_SHIFT1 + 1] += column_sum(bn) + column_sum(bm)
        u = bn * gain1[...]
        inner = u - jnp.mean(u, axis=-1, keepdims=True) - unit * jnp.mean(u * unit, axis=-1, keepdims=True)
        dx[at] = (bhid[at] + inner * rstd[to]).astype(BF)

    loop(rows // block, last_rows)

    segment_rows = nl[SEG : SEG + rows]
    memory_rows = nl[0:rows]
    grads[QUERY_AT : QUERY_AT + FEATURES] = t_dot(segment_rows, bhl[...]).astype(BF)
    grads[KEY_AT : KEY_AT + FEATURES] = (t_dot(segment_rows, kgs[...]) + t_dot(memory_rows, kgm[...])).astype(BF)
    grads[VALUE_AT : VALUE_AT + FEATURES] = (t_dot(segment_rows, vgs[...]) + t_dot(memory_rows, vgm[...])).astype(BF)
    for g in range(HEADS // GROUP):
        lanes = slice(g * LANES, (g + 1) * LANES)
        across = t_dot(placed[:, lanes], braw[:, g * GROUP * LANES : (g + 1) * GROUP * LANES])
        back = jnp.concatenate(
            [across[h * HEAD_DIM : (h + 1) * HEAD_DIM, h * LANES : (h + 1) * LANES] for h in range(GROUP)], axis=0
        ) * SCALING
        high = back.astype(BF)
        low = (back - high.astype(F32)).astype(BF)
        cosines = dot_t(basis[0:LANES], high) + (dot_t(basis[LANES:], high) + dot_t(basis[0:LANES], low))
        grads[RELATIVE_AT : RELATIVE_AT + LANES, lanes] = cosines.astype(BF)
    grads[VECTOR_AT : VECTOR_AT + VECTOR_ROWS] = vec[...].astype(BF)
    grads[VECTOR_AT + VECTOR_ROWS :] = jnp.zeros((BUFFER_ROWS - VECTOR_AT - VECTOR_ROWS, FEATURES), BF)


def run_layer(place, horizon, x, start, arrived, cot, table, basis, params):
    rows = x.shape[0]
    operands = (x, start, arrived, cot, *params, table, basis)
    vmem = pl.BlockSpec(memory_space=pltpu.VMEM)
    hbm = pl.BlockSpec(memory_space=pltpu.HBM)
    smem = pl.BlockSpec(memory_space=pltpu.SMEM)
    padded = rows + SEG + LANES - 2 * SEG
    scratch = [
        pltpu.VMEM((rows + SEG, FEATURES), BF),
        pltpu.VMEM((rows + SEG, FEATURES), F32),
        pltpu.VMEM((rows + SEG, 1), F32),
        pltpu.VMEM((rows, FEATURES), BF),
        pltpu.VMEM((rows, FEATURES), BF),
        pltpu.VMEM((padded, FEATURES), BF),
        pltpu.VMEM((padded, 2 * FEATURES), BF),
        pltpu.VMEM((HEADS * LANES, FEATURES), BF),
        pltpu.VMEM((rows, HEADS * LANES), F32),
        pltpu.VMEM((rows * HEADS, LANES), F32),
        pltpu.VMEM((rows, FEATURES), BF),
        pltpu.VMEM((rows, FEATURES), F32),
        pltpu.VMEM((rows, FEATURES), BF),
        pltpu.VMEM((rows, HIDDEN), BF),
        pltpu.VMEM((rows, HIDDEN), BF),
        pltpu.VMEM((rows, FEATURES), BF),
        pltpu.VMEM((rows, FEATURES), F32),
        pltpu.VMEM((rows, FEATURES), BF),
        pltpu.VMEM((rows, FEATURES), F32),
        pltpu.VMEM((rows, HEADS * LANES), BF),
        pltpu.VMEM((rows, FEATURES), BF),
        pltpu.VMEM((rows, FEATURES), BF),
        pltpu.VMEM((rows, FEATURES), BF),
        pltpu.VMEM((rows, FEATURES), BF),
        pltpu.VMEM((VECTOR_ROWS, FEATURES), F32),
    ]
    return pl.pallas_call(
        layer_kernel,
        out_shape=(
            jax.ShapeDtypeStruct((rows, FEATURES), BF),
            jax.ShapeDtypeStruct((rows, FEATURES), BF),
        )
        + (jax.ShapeDtypeStruct((PART_ROWS, FEATURES), BF),) * (2 * PIPES),
        in_specs=[smem, smem] + [hbm] * COPIES,
        out_specs=(vmem, vmem) + (hbm,) * (2 * PIPES),
        scratch_shapes=[pltpu.VMEM(a.shape, a.dtype) for a in operands]
        + [
            pltpu.SemaphoreType.DMA((COPIES,)),
            pltpu.SemaphoreType.DMA((2 * PIPES,)),
            pltpu.VMEM((BUFFER_ROWS, FEATURES), BF),
        ]
        + scratch,
        compiler_params=pltpu.CompilerParams(vmem_limit_bytes=63 * 1024 * 1024),
        name="layer",
    )(place, horizon, *operands)


def unpack_kernel(place, *refs):
    parts, turned = refs[: 2 * PIPES], refs[2 * PIPES]
    gain1, shift1, wq, wk, wv, wr, cbias, pbias, wo, gain2, shift2, w1, b1, w2, b2, whole = refs[2 * PIPES + 1 :]
    core = place[1]
    for p in range(PIPES):
        for k, half in enumerate((core, 1 - core)):
            at = pl.ds(pl.multiple_of((half * PIPES + p) * PART_ROWS, PART_ROWS), PART_ROWS)
            whole[at] = parts[2 * p + k][...]
    for f in range(HIDDEN // FEATURES):
        w1[:, f * FEATURES : (f + 1) * FEATURES] = whole[
            EXPAND_AT + f * FEATURES : EXPAND_AT + (f + 1) * FEATURES
        ].astype(F32)
    w2[...] = whole[SHRINK_AT : SHRINK_AT + HIDDEN].astype(F32)
    for ref, at in ((wq, QUERY_AT), (wk, KEY_AT), (wv, VALUE_AT), (wo, OUTPUT_AT)):
        ref[...] = whole[at : at + FEATURES].astype(F32)
    cosines = whole[RELATIVE_AT : RELATIVE_AT + LANES]
    wr[...] = t_dot(turned[0:LANES], cosines) + t_dot(turned[LANES:], cosines)
    vectors = whole[VECTOR_AT : VECTOR_AT + VECTOR_ROWS].astype(F32)
    for ref, at in (
        (cbias, V_CONTENT), (pbias, V_POSITION), (gain1, V_GAIN1), (shift1, V_SHIFT1),
        (gain2, V_GAIN2), (shift2, V_SHIFT2), (b2, V_SHRINK),
    ):
        ref[...] = vectors[at]
    for f in range(HIDDEN // FEATURES):
        b1[f * FEATURES : (f + 1) * FEATURES] = vectors[V_EXPAND + f]


def unpack(place, parts, turned):
    vmem = pl.BlockSpec(memory_space=pltpu.VMEM)
    smem = pl.BlockSpec(memory_space=pltpu.SMEM)
    vector = jax.ShapeDtypeStruct((FEATURES,), F32)
    square = jax.ShapeDtypeStruct((FEATURES, FEATURES), F32)
    shapes = (
        vector, vector, square, square, square, square, vector, vector, square, vector, vector,
        jax.ShapeDtypeStruct((FEATURES, HIDDEN), F32),
        jax.ShapeDtypeStruct((HIDDEN,), F32),
        jax.ShapeDtypeStruct((HIDDEN, FEATURES), F32),
        vector,
    )
    return pl.pallas_call(
        unpack_kernel,
        out_shape=shapes,
        in_specs=[smem] + [vmem] * (2 * PIPES + 1),
        out_specs=(vmem,) * len(shapes),
        scratch_shapes=[pltpu.VMEM((BUFFER_ROWS, FEATURES), BF)],
        compiler_params=pltpu.CompilerParams(vmem_limit_bytes=32 * 1024 * 1024),
        name="unpack",
    )(place, *parts, turned)


AXES = ("tm", "roll")


def exchange_plan(roll_count, tm_count):
    tm_bits = tm_count.bit_length() - 1
    roll_bits = roll_count.bit_length() - 1
    high = [roll_bits + b for b in range(1, tm_bits)]
    rolls = list(range(roll_bits))
    even = high + rolls
    odd = rolls[:1] + high + rolls[1:]
    return [(roll_bits, roll_bits)] + list(zip(even, odd))


def swap(value, bits, roll_count, count):
    even, odd = bits
    pairs = [(d, d ^ (1 << (odd if (d // roll_count) & 1 else even))) for d in range(count)]
    return lax.ppermute(value, AXES, pairs)


def add_low(a, b):
    return (a.astype(F32) + b.astype(F32)).astype(BF)


def sum_everywhere(halves, core):
    roll_count, tm_count = lax.axis_size("roll"), lax.axis_size("tm")
    count = roll_count * tm_count
    me = lax.axis_index("tm") * roll_count + lax.axis_index("roll")
    cores, *stages = exchange_plan(roll_count, tm_count)
    halving = 2

    def chain(kept, sent):
        buffer = add_low(kept, swap(sent, cores, roll_count, count))
        bits = []
        for even, odd in stages[:halving]:
            bit = jnp.where(core == 0, (me >> even) & 1, (me >> odd) & 1)
            half = buffer.shape[0] // 2
            sent = lax.dynamic_slice_in_dim(buffer, (1 - bit) * half, half, 0)
            kept = lax.dynamic_slice_in_dim(buffer, bit * half, half, 0)
            buffer = add_low(kept, swap(sent, (even, odd), roll_count, count))
            bits.append(bit)
        for even, odd in stages[halving:]:
            buffer = add_low(buffer, swap(buffer, (even, odd), roll_count, count))
        for (even, odd), bit in list(zip(stages, bits))[::-1]:
            other = swap(buffer, (even, odd), roll_count, count)
            first = bit == 0
            buffer = jnp.concatenate([jnp.where(first, buffer, other), jnp.where(first, other, buffer)], axis=0)
        return [buffer, swap(buffer, cores, roll_count, count)]

    return sum([chain(*halves[2 * p : 2 * p + 2]) for p in range(PIPES)], [])


def body(
    layer_input, start_memory, horizon, cotangent, first_gain, first_shift, query_projection_weight,
    key_projection_weight, value_projection_weight, relative_weight, content_bias, position_bias,
    output_weight, second_gain, second_shift, expand_weight, expand_bias, shrink_weight, shrink_bias,
):
    rollouts, columns, features = layer_input.shape
    x = layer_input.reshape(rollouts * columns, features)
    position = lax.axis_index("tm")
    tm_count = lax.axis_size("tm")
    arrived = lax.ppermute(x[-SEG:], "tm", [(i, (i + 1) % tm_count) for i in range(tm_count)])
    core = position & 1
    place = jnp.stack([position, core]).astype(jnp.int32)
    table = jnp.asarray(position_rows())
    basis, turned = (jnp.asarray(part) for part in relative_basis())

    def row(v):
        return v.reshape(1, -1)

    params = (
        row(first_gain), row(first_shift), query_projection_weight, key_projection_weight,
        value_projection_weight, relative_weight, row(content_bias), row(position_bias), output_weight,
        row(second_gain), row(second_shift), expand_weight, row(expand_bias), shrink_weight, row(shrink_bias),
    )
    out, dx, *halves = run_layer(
        place, horizon, x, start_memory.reshape(SEG, features), arrived,
        cotangent.reshape(rollouts * columns, features), table, basis, params,
    )
    summed = unpack(place, sum_everywhere(halves, core), turned)
    return (out.reshape(layer_input.shape), dx.reshape(layer_input.shape)) + tuple(summed)


def solution(mesh):
    in_specs = (
        P("roll", "tm", None), P("roll", None, None), P("roll", None), P("roll", "tm", None),
    ) + (P(),) * 15
    out_specs = (P("roll", "tm", None), P("roll", "tm", None)) + (P(),) * 15
    return jax.shard_map(body, mesh=mesh, in_specs=in_specs, out_specs=out_specs, check_vma=False)
```

```python
import functools
import math
import types

import jax
import jax.numpy as jnp
import numpy as np
from jax import lax
from jax.experimental import pallas as pl
from jax.experimental.pallas import tpu as pltpu
from jax.sharding import PartitionSpec as P

HEADS = 8
HEAD_DIM = 32
SEG = 48
STEP = 3
FEATURES = 256
HIDDEN = 1024
LANES = 128
GROUP = LANES // HEAD_DIM
EPSILON = 1e-05
MASKED = -4000000000.0
SCALING = 1.0 / math.sqrt(HEAD_DIM)
SCALING_BITS = SCALING / math.log(2.0)
GELU_A = 0.7978845608028654
GELU_B = 0.044715 * GELU_A
BF = jnp.bfloat16
F32 = jnp.float32

EXPAND_AT = 0
SHRINK_AT = 1024
QUERY_AT = 2048
KEY_AT = 2304
VALUE_AT = 2560
OUTPUT_AT = 2816
RELATIVE_AT = 3072
VECTOR_AT = 3200
BUFFER_ROWS = 3328
PIPES = 2
PART_ROWS = BUFFER_ROWS // (2 * PIPES)
(V_CONTENT, V_POSITION, V_GAIN1, V_SHIFT1, V_GAIN2, V_SHIFT2, V_SHRINK, V_EXPAND) = range(8)
VECTOR_ROWS = 16


def position_rows():
    distance = (2 * SEG - 1 - np.arange(2 * SEG)).astype(np.float32)
    freqs = 10000.0 ** (-(2.0 * np.arange(FEATURES // 2)) / FEATURES)
    angles = distance[:, None] * freqs.astype(np.float32)[None, :]
    table = np.concatenate([np.sin(angles), np.cos(angles)], axis=-1)
    return np.pad(table, ((0, LANES - 2 * SEG), (0, 0))).astype(BF)


def relative_basis():
    count = 2 * SEG
    k, c = np.arange(count)[:, None], np.arange(count)[None, :]
    basis = np.cos(np.pi * k * (2 * c + 1) / (2 * count)) * np.where(k == 0, np.sqrt(1.0 / count), np.sqrt(2.0 / count))
    basis = np.pad(basis, ((0, LANES - count), (0, LANES - count)))

    def parts(values):
        high = values.astype(BF)
        low = (values - high.astype(np.float64)).astype(BF)
        return np.concatenate([high, low], axis=0)

    return parts(basis), parts(basis @ position_rows().astype(np.float64))


def tables():
    return jnp.asarray(position_rows()), jnp.asarray(relative_basis()[0])


def interleave(*steps):
    running = [[0, count, part] for count, part in steps]
    while running:
        slowest = min(running, key=lambda entry: entry[0] / entry[1])
        slowest[0] += 1
        if next(slowest[2], None) is None:
            running.remove(slowest)


def dot(a, b):
    return lax.dot_general(a, b, (((1,), (0,)), ((), ())), preferred_element_type=F32)


def dot_t(a, b):
    return lax.dot_general(a, b, (((1,), (1,)), ((), ())), preferred_element_type=F32)


def t_dot(a, b):
    return lax.dot_general(a, b, (((0,), (0,)), ((), ())), preferred_element_type=F32)


def normalize(rows):
    center = rows - jnp.mean(rows, axis=-1, keepdims=True)
    spread = jnp.mean(center * center, axis=-1, keepdims=True)
    scale = lax.rsqrt(spread + EPSILON)
    return center * scale, scale


def column_sum(rows):
    return jnp.sum(rows, axis=0, keepdims=True)


def stack_heads(rows, head_masks):
    return jnp.concatenate([rows * mask for mask in head_masks], axis=0)


def unshift(rows, row_bits):
    rolled = jnp.concatenate(
        [pltpu.roll(rows[a : a + 8], SEG - 8 - a, 1) for a in range(0, SEG - 8, 8)] + [rows[SEG - 8 :]], axis=0
    )
    for step, bit in row_bits:
        rolled = jnp.where(bit, pltpu.roll(rolled, step, 1), rolled)
    return rolled


def pick_heads(rows, lane_head):
    picked = rows[0:SEG]
    for h in range(1, GROUP):
        picked = jnp.where(lane_head == h, rows[h * SEG : (h + 1) * SEG], picked)
    return picked


COPIES = 21
(C_X, C_START, C_ARRIVED, C_COT, C_GAIN1, C_SHIFT1, C_WQ, C_WK, C_WV, C_WR, C_CBIAS, C_PBIAS, C_WO,
 C_GAIN2, C_SHIFT2, C_W1, C_B1, C_W2, C_B2, C_TABLE, C_BASIS) = range(COPIES)
FIRST_COPIES = (C_TABLE, C_WR, C_X, C_GAIN1, C_SHIFT1, C_WQ, C_WK, C_WV, C_START, C_ARRIVED, C_CBIAS, C_PBIAS)
LATER_COPIES = (C_WO, C_GAIN2, C_SHIFT2, C_W1, C_B1, C_COT, C_W2, C_B2, C_BASIS)


def layer_kernel(place, horizon, *refs):
    sources, refs = refs[:COPIES], refs[COPIES:]
    outputs, halves, refs = refs[:2], refs[2 : 2 + 2 * PIPES], refs[2 + 2 * PIPES :]
    targets, (sems, half_sems, grads, *scratch) = refs[:COPIES], refs[COPIES:]
    moves = [pltpu.make_async_copy(a, b, sems.at[i]) for i, (a, b) in enumerate(zip(sources, targets))]
    for i in FIRST_COPIES + LATER_COPIES:
        moves[i].start()
    compute_layer(place, horizon, moves, *targets, *outputs, grads, *scratch)
    side = place[1]
    leaving = []
    for p in range(PIPES):
        for k, half in enumerate((side, 1 - side)):
            at = pl.ds(pl.multiple_of((half * PIPES + p) * PART_ROWS, PART_ROWS), PART_ROWS)
            leaving.append(pltpu.make_async_copy(grads.at[at], halves[2 * p + k], half_sems.at[2 * p + k]))
    for move in leaving:
        move.start()
    for move in leaving:
        move.wait()


def compute_layer(
    place, horizon, moves, x, start, arrived, cot, gain1, shift1, wq, wk, wv, wr, cbias, pbias, wo,
    gain2, shift2, w1, b1, w2, b2, table, basis,
    out, dx, grads,
    nl, xhat, rstd, content, placed, keys, values, relblock, raw, probs, mixed,
    hid, n2, act, bpre, bmix, bhid, bhl, bcont, bql, braw, kgm, kgs, vgm, vgs, vec,
):
    rows = x.shape[0]
    segments = rows // SEG
    position = place[0]
    vec[...] = jnp.zeros_like(vec)

    for i in FIRST_COPIES:
        moves[i].wait()
    rel = dot(table[...], wr[...])
    wide_head = lax.broadcasted_iota(jnp.int32, (LANES, FEATURES), 1) // HEAD_DIM
    for h in range(HEADS):
        relblock[h * LANES : (h + 1) * LANES] = jnp.where(wide_head == h, rel, 0.0).astype(BF)

    def project(normed, at, count):
        keys[pl.ds(at, count)] = dot(normed, wk[...]).astype(BF)
        value = dot(normed, wv[...]).astype(BF)
        for g in range(HEADS // GROUP):
            values[pl.ds(at, count), 2 * g * LANES : (2 * g + 1) * LANES] = value[:, g * LANES : (g + 1) * LANES]

    memory = jnp.where(position == 0, start[...].astype(F32), arrived[...].astype(F32))
    unit, scale = normalize(memory)
    xhat[0:SEG] = unit
    rstd[0:SEG] = scale
    normed = (unit * gain1[...] + shift1[...]).astype(BF)
    nl[0:SEG] = normed
    project(normed, 0, SEG)
    block = 4 * SEG
    for edge in range(block, rows + 1, block):
        ahead = slice(edge + SEG, edge + LANES - SEG)
        keys[ahead] = jnp.zeros((LANES - 2 * SEG, FEATURES), BF)
        values[ahead] = jnp.zeros((LANES - 2 * SEG, 2 * FEATURES), BF)
    for g in range(HEADS // GROUP):
        values[:, (2 * g + 1) * LANES : (2 * g + 2) * LANES] = jnp.ones((values.shape[0], LANES), BF)
    blocks = rows // block
    lane_head = lax.broadcasted_iota(jnp.int32, (SEG, LANES), 1) // HEAD_DIM
    head_masks = [(lane_head == h).astype(F32).astype(BF) for h in range(GROUP)]
    key_at = lax.broadcasted_iota(jnp.int32, (SEG, LANES), 1)
    query_at = lax.broadcasted_iota(jnp.int32, (SEG, LANES), 0) + SEG
    low_row = 7 - (query_at & 7)
    row_bits = [(step, (low_row & step) != 0) for step in (1, 2, 4)]
    upper = (key_at & (HEAD_DIM // 2)) != 0

    def first(i):
        at = pl.ds(i * block, block)
        to = pl.ds(i * block + SEG, block)
        unit, scale = normalize(x[at].astype(F32))
        xhat[to] = unit
        rstd[to] = scale
        normed = (unit * gain1[...] + shift1[...]).astype(BF)
        nl[to] = normed
        yield 1
        project(normed, i * block + SEG, block)
        yield 1
        query = dot(normed, wq[...])
        content[at] = (query + cbias[...]).astype(BF)
        low = (query + pbias[...]).astype(BF)
        placed[at] = low
        yield 1
        for f in range(HEADS * LANES // FEATURES):
            cols = slice(f * FEATURES, (f + 1) * FEATURES)
            raw[at, cols] = dot_t(low, relblock[cols])
            yield 1

    def units_of(i):
        units = []
        for s in range(i * block // SEG, (i + 1) * block // SEG):
            for g in range(HEADS // GROUP):
                u = types.SimpleNamespace()
                u.s, u.g, u.at, u.window = s, g, pl.ds(s * SEG, SEG), pl.ds(s * SEG, LANES)
                u.lanes = slice(g * LANES, (g + 1) * LANES)
                u.beside = slice(2 * g * LANES, (2 * g + 2) * LANES)
                u.heads = pl.ds((s * HEADS + g * GROUP) * SEG, GROUP * SEG)
                units.append(u)
        return units

    def allow(s):
        number = position * segments + s
        current = horizon[0, number]
        previous = jnp.where(number == 0, SEG // STEP, horizon[0, jnp.maximum(number - 1, 0)])
        live = key_at < jnp.where(key_at < SEG, STEP * previous, SEG + STEP * current)
        return (key_at <= query_at) & (live | (key_at == query_at))

    def score(u):
        u.direct = dot_t(stack_heads(content[u.at, u.lanes], head_masks), keys[u.window, u.lanes])

    def mask(u):
        allowed = allow(u.s)
        u.scores = []
        for h in range(GROUP):
            head = u.g * GROUP + h
            shifted = pltpu.roll(
                raw[u.at, head * LANES : (head + 1) * LANES], LANES - SEG + 1, 1, stride=1, stride_axis=0
            )
            u.scores.append(jnp.where(allowed, u.direct[h * SEG : (h + 1) * SEG] + shifted, MASKED))
        u.tops = [jnp.max(v, axis=-1, keepdims=True) for v in u.scores]

    def exponentiate(u):
        u.low = jnp.concatenate(
            [jnp.exp2((v - top) * SCALING_BITS).astype(BF) for v, top in zip(u.scores, u.tops)], axis=0
        )

    def mix(u):
        u.both = dot(u.low, values[u.window, u.beside])

    def finish(u):
        inverse = 1.0 / u.both[:, LANES:]
        mx = pick_heads(u.both[:, :LANES] * inverse, lane_head)
        mixed[u.at, u.lanes] = mx.astype(BF)
        bcont[u.at, u.lanes] = mx
        probs[u.heads] = u.low.astype(F32) * inverse

    def staged(i, stages):
        units = units_of(i)
        for t in range(len(units) + len(stages) - 1):
            for k in reversed(range(len(stages))):
                if 0 <= t - k < len(units):
                    stages[k](units[t - k])
                    yield 1

    def attend(i):
        return staged(i, (score, mask, exponentiate, mix, finish))

    def feed(i):
        at = pl.ds(i * block, block)
        hidden = x[at].astype(F32) + dot(mixed[at], wo[...])
        yield 1
        unit, scale = normalize(hidden)
        low = (unit * gain2[...] + shift2[...]).astype(BF)
        n2[at] = low
        yield 1
        back = cot[at]
        for f in range(HIDDEN // FEATURES):
            cols = slice(f * FEATURES, (f + 1) * FEATURES)
            v = dot(low, w1[:, cols]) + b1[:, cols]
            grad = dot_t(back, w2[cols])
            yield 1
            square = v * v
            half = 0.5 + 0.5 * jnp.tanh(v * (GELU_A + GELU_B * square))
            active = v * half
            act[at, cols] = active.astype(BF)
            slope = half + (2.0 * active) * (1.0 - half) * (GELU_A + (3.0 * GELU_B) * square)
            grad = grad * slope
            vec[V_EXPAND + f : V_EXPAND + f + 1] += column_sum(grad)
            bpre[at, cols] = grad.astype(BF)
            yield 1
        out[at] = (hidden + dot(act[at], w2[...]) + b2[...]).astype(BF)
        yield 1
        bn = dot_t(bpre[at], w1[...])
        yield 1
        back = back.astype(F32)
        vec[V_SHRINK : V_SHRINK + 1] += column_sum(back)
        vec[V_GAIN2 : V_GAIN2 + 1] += column_sum(bn * unit)
        vec[V_SHIFT2 : V_SHIFT2 + 1] += column_sum(bn)
        u = bn * gain2[...]
        inner = u - jnp.mean(u, axis=-1, keepdims=True) - unit * jnp.mean(u * unit, axis=-1, keepdims=True)
        bh = back + inner * scale
        bhid[at] = bh
        bl = bh.astype(BF)
        bhl[at] = bl
        yield 1
        bmix[at] = dot_t(bl, wo[...]).astype(BF)
        yield 1

    def feed_weights():
        for f in range(HIDDEN // FEATURES):
            cols = slice(f * FEATURES, (f + 1) * FEATURES)
            grads[EXPAND_AT + f * FEATURES : EXPAND_AT + (f + 1) * FEATURES] = t_dot(n2[...], bpre[:, cols]).astype(BF)
            yield 1
            grads[SHRINK_AT + f * FEATURES : SHRINK_AT + (f + 1) * FEATURES] = t_dot(act[:, cols], cot[...]).astype(BF)
            yield 1
        grads[OUTPUT_AT : OUTPUT_AT + FEATURES] = t_dot(mixed[...], bhl[...]).astype(BF)
        yield 1

    def spread(u):
        rows = bmix[u.at, u.lanes]
        u.back = stack_heads(rows, head_masks)
        product = rows.astype(F32) * -bcont[u.at, u.lanes]
        left = product + pltpu.roll(product, LANES - HEAD_DIM // 2, 1)
        right = product + pltpu.roll(product, HEAD_DIM // 2, 1)
        along = jnp.where(upper, right, left - left.astype(BF).astype(F32)).astype(BF)
        u.along = jnp.concatenate([u.back, stack_heads(along, head_masks)], axis=1)

    def widen(u):
        u.wide = dot_t(u.along, values[u.window, u.beside])

    def differentiate(u):
        prob = probs[u.heads]
        bs = prob * u.wide
        u.low, u.grad_low = prob.astype(BF), bs.astype(BF)
        for h in range(GROUP):
            head = u.g * GROUP + h
            braw[u.at, head * LANES : (head + 1) * LANES] = unshift(bs[h * SEG : (h + 1) * SEG], row_bits).astype(BF)

    def collect_values(u):
        vg = t_dot(u.low, u.back).astype(BF)
        vgm[u.at, u.lanes] = vg[0:SEG]
        vgs[u.at, u.lanes] = vg[SEG : 2 * SEG]

    def collect_keys(u):
        kg = (t_dot(u.grad_low, stack_heads(content[u.at, u.lanes], head_masks)) * SCALING).astype(BF)
        kgm[u.at, u.lanes] = kg[0:SEG]
        kgs[u.at, u.lanes] = kg[SEG : 2 * SEG]

    def collect_queries(u):
        bcont[u.at, u.lanes] = pick_heads(dot(u.grad_low, keys[u.window, u.lanes]), lane_head) * SCALING

    def attend_back(i):
        return staged(i, (spread, widen, differentiate, collect_values, collect_keys, collect_queries))

    def last(i):
        at = pl.ds(i * block, block)
        to = pl.ds(i * block + SEG, block)
        bplace = dot(braw[at], relblock[...]) * SCALING
        yield 1
        bc = bcont[at]
        vec[V_CONTENT : V_CONTENT + 1] += column_sum(bc)
        vec[V_POSITION : V_POSITION + 1] += column_sum(bplace)
        bq = (bc + bplace).astype(BF)
        bql[at] = bq
        yield 1
        bn = dot_t(bq, wq[...]) + dot_t(kgs[at], wk[...]) + dot_t(vgs[at], wv[...])
        yield 1
        bm = dot_t(kgm[at], wk[...]) + dot_t(vgm[at], wv[...])
        yield 1
        unit = xhat[to]
        vec[V_GAIN1 : V_GAIN1 + 1] += column_sum(bn * unit) + column_sum(bm * xhat[at])
        vec[V_SHIFT1 : V_SHIFT1 + 1] += column_sum(bn) + column_sum(bm)
        u = bn * gain1[...]
        inner = u - jnp.mean(u, axis=-1, keepdims=True) - unit * jnp.mean(u * unit, axis=-1, keepdims=True)
        dx[at] = (bhid[at] + inner * rstd[to]).astype(BF)
        yield 1

    def attention_weights():
        segment_rows = nl[SEG : SEG + rows]
        memory_rows = nl[0:rows]
        grads[QUERY_AT : QUERY_AT + FEATURES] = t_dot(segment_rows, bql[...]).astype(BF)
        yield 1
        grads[KEY_AT : KEY_AT + FEATURES] = (t_dot(segment_rows, kgs[...]) + t_dot(memory_rows, kgm[...])).astype(BF)
        yield 1
        grads[VALUE_AT : VALUE_AT + FEATURES] = (t_dot(segment_rows, vgs[...]) + t_dot(memory_rows, vgm[...])).astype(BF)
        yield 1
        for g in range(HEADS // GROUP):
            lanes = slice(g * LANES, (g + 1) * LANES)
            across = t_dot(placed[:, lanes], braw[:, g * GROUP * LANES : (g + 1) * GROUP * LANES])
            back = jnp.concatenate(
                [across[h * HEAD_DIM : (h + 1) * HEAD_DIM, h * LANES : (h + 1) * LANES] for h in range(GROUP)], axis=0
            ) * SCALING
            high = back.astype(BF)
            low = (back - high.astype(F32)).astype(BF)
            cosines = dot_t(basis[0:LANES], high) + (dot_t(basis[LANES:], high) + dot_t(basis[0:LANES], low))
            grads[RELATIVE_AT : RELATIVE_AT + LANES, lanes] = cosines.astype(BF)
            yield 1

    phases = {
        "first": (8, first), "attend": (40, attend), "feed": (14, feed), "back": (48, attend_back), "last": (5, last),
    }
    for t in range(blocks + 4):
        if t == 2:
            for i in LATER_COPIES:
                moves[i].wait()
        steps = []
        for lag, (count, phase) in enumerate(phases.values()):
            if 0 <= t - lag < blocks:
                steps.append((count, phase(t - lag)))
        if t == blocks + 2:
            steps.append((9, feed_weights()))
        if t == blocks + 3:
            pass
        interleave(*steps)
    interleave((5, attention_weights()))
    grads[VECTOR_AT : VECTOR_AT + VECTOR_ROWS] = vec[...].astype(BF)
    grads[VECTOR_AT + VECTOR_ROWS :] = jnp.zeros((BUFFER_ROWS - VECTOR_AT - VECTOR_ROWS, FEATURES), BF)


def run_layer(place, horizon, x, start, arrived, cot, table, basis, params):
    rows = x.shape[0]
    operands = (x, start, arrived, cot, *params, table, basis)
    vmem = pl.BlockSpec(memory_space=pltpu.VMEM)
    hbm = pl.BlockSpec(memory_space=pltpu.HBM)
    smem = pl.BlockSpec(memory_space=pltpu.SMEM)
    padded = rows + SEG + LANES - 2 * SEG
    scratch = [
        pltpu.VMEM((rows + SEG, FEATURES), BF),
        pltpu.VMEM((rows + SEG, FEATURES), F32),
        pltpu.VMEM((rows + SEG, 1), F32),
        pltpu.VMEM((rows, FEATURES), BF),
        pltpu.VMEM((rows, FEATURES), BF),
        pltpu.VMEM((padded, FEATURES), BF),
        pltpu.VMEM((padded, 2 * FEATURES), BF),
        pltpu.VMEM((HEADS * LANES, FEATURES), BF),
        pltpu.VMEM((rows, HEADS * LANES), F32),
        pltpu.VMEM((rows * HEADS, LANES), F32),
        pltpu.VMEM((rows, FEATURES), BF),
        pltpu.VMEM((rows, FEATURES), F32),
        pltpu.VMEM((rows, FEATURES), BF),
        pltpu.VMEM((rows, HIDDEN), BF),
        pltpu.VMEM((rows, HIDDEN), BF),
        pltpu.VMEM((rows, FEATURES), BF),
        pltpu.VMEM((rows, FEATURES), F32),
        pltpu.VMEM((rows, FEATURES), BF),
        pltpu.VMEM((rows, FEATURES), F32),
        pltpu.VMEM((rows, FEATURES), BF),
        pltpu.VMEM((rows, HEADS * LANES), BF),
        pltpu.VMEM((rows, FEATURES), BF),
        pltpu.VMEM((rows, FEATURES), BF),
        pltpu.VMEM((rows, FEATURES), BF),
        pltpu.VMEM((rows, FEATURES), BF),
        pltpu.VMEM((VECTOR_ROWS, FEATURES), F32),
    ]
    return pl.pallas_call(
        layer_kernel,
        out_shape=(
            jax.ShapeDtypeStruct((rows, FEATURES), BF),
            jax.ShapeDtypeStruct((rows, FEATURES), BF),
        )
        + (jax.ShapeDtypeStruct((PART_ROWS, FEATURES), BF),) * (2 * PIPES),
        in_specs=[smem, smem] + [hbm] * COPIES,
        out_specs=(vmem, vmem) + (hbm,) * (2 * PIPES),
        scratch_shapes=[pltpu.VMEM(a.shape, a.dtype) for a in operands]
        + [
            pltpu.SemaphoreType.DMA((COPIES,)),
            pltpu.SemaphoreType.DMA((2 * PIPES,)),
            pltpu.VMEM((BUFFER_ROWS, FEATURES), BF),
        ]
        + scratch,
        compiler_params=pltpu.CompilerParams(vmem_limit_bytes=63 * 1024 * 1024),
        name="layer",
    )(place, horizon, *operands)


def unpack_kernel(place, *refs):
    parts, turned = refs[: 2 * PIPES], refs[2 * PIPES]
    gain1, shift1, wq, wk, wv, wr, cbias, pbias, wo, gain2, shift2, w1, b1, w2, b2, whole = refs[2 * PIPES + 1 :]
    side = place[1]
    for p in range(PIPES):
        for k, half in enumerate((side, 1 - side)):
            at = pl.ds(pl.multiple_of((half * PIPES + p) * PART_ROWS, PART_ROWS), PART_ROWS)
            whole[at] = parts[2 * p + k][...]
    for f in range(HIDDEN // FEATURES):
        w1[:, f * FEATURES : (f + 1) * FEATURES] = whole[
            EXPAND_AT + f * FEATURES : EXPAND_AT + (f + 1) * FEATURES
        ].astype(F32)
    w2[...] = whole[SHRINK_AT : SHRINK_AT + HIDDEN].astype(F32)
    for ref, at in ((wq, QUERY_AT), (wk, KEY_AT), (wv, VALUE_AT), (wo, OUTPUT_AT)):
        ref[...] = whole[at : at + FEATURES].astype(F32)
    cosines = whole[RELATIVE_AT : RELATIVE_AT + LANES]
    wr[...] = t_dot(turned[0:LANES], cosines) + t_dot(turned[LANES:], cosines)
    vectors = whole[VECTOR_AT : VECTOR_AT + VECTOR_ROWS].astype(F32)
    for ref, at in (
        (cbias, V_CONTENT), (pbias, V_POSITION), (gain1, V_GAIN1), (shift1, V_SHIFT1),
        (gain2, V_GAIN2), (shift2, V_SHIFT2), (b2, V_SHRINK),
    ):
        ref[...] = vectors[at]
    for f in range(HIDDEN // FEATURES):
        b1[f * FEATURES : (f + 1) * FEATURES] = vectors[V_EXPAND + f]


def unpack(place, parts, turned):
    vmem = pl.BlockSpec(memory_space=pltpu.VMEM)
    smem = pl.BlockSpec(memory_space=pltpu.SMEM)
    vector = jax.ShapeDtypeStruct((FEATURES,), F32)
    square = jax.ShapeDtypeStruct((FEATURES, FEATURES), F32)
    shapes = (
        vector, vector, square, square, square, square, vector, vector, square, vector, vector,
        jax.ShapeDtypeStruct((FEATURES, HIDDEN), F32),
        jax.ShapeDtypeStruct((HIDDEN,), F32),
        jax.ShapeDtypeStruct((HIDDEN, FEATURES), F32),
        vector,
    )
    return pl.pallas_call(
        unpack_kernel,
        out_shape=shapes,
        in_specs=[smem] + [vmem] * (2 * PIPES + 1),
        out_specs=(vmem,) * len(shapes),
        scratch_shapes=[pltpu.VMEM((BUFFER_ROWS, FEATURES), BF)],
        compiler_params=pltpu.CompilerParams(vmem_limit_bytes=32 * 1024 * 1024),
        name="unpack",
    )(place, *parts, turned)


AXES = ("tm", "roll")


def exchange_plan(roll_count, tm_count):
    tm_bits = tm_count.bit_length() - 1
    roll_bits = roll_count.bit_length() - 1
    high = [roll_bits + b for b in range(1, tm_bits)]
    rolls = list(range(roll_bits))
    even = high + rolls
    odd = rolls[:1] + high + rolls[1:]
    return roll_bits, list(zip(even, odd))


def side_of(device):
    return bin(device).count("1") & 1


def swap_cores(value, core, count):
    return lax.ppermute(value, AXES, [(d, d ^ (1 << core)) for d in range(count)])


def swap(value, bits, core, count):
    return lax.ppermute(value, AXES, [(d, d ^ (1 << bits[side_of(d)]) ^ (1 << core)) for d in range(count)])


def add_low(a, b):
    return (a.astype(F32) + b.astype(F32)).astype(BF)


def sum_everywhere(halves, me, side):
    roll_count, tm_count = lax.axis_size("roll"), lax.axis_size("tm")
    count = roll_count * tm_count
    core, stages = exchange_plan(roll_count, tm_count)
    halving = 3

    def chain(kept, sent):
        buffer = add_low(kept, swap_cores(sent, core, count))
        firsts = []
        for bits in stages[:halving]:
            bit = jnp.where(side == 0, (me >> bits[0]) & 1, (me >> bits[1]) & 1)
            half = buffer.shape[0] // 2
            sent = lax.dynamic_slice_in_dim(buffer, (1 - bit) * half, half, 0)
            kept = lax.dynamic_slice_in_dim(buffer, bit * half, half, 0)
            buffer = add_low(kept, swap(sent, bits, core, count))
            firsts.append(bit == 0)
        for bits in stages[halving:]:
            buffer = add_low(buffer, swap(buffer, bits, core, count))
        for bits, first in list(zip(stages, firsts))[::-1]:
            other = swap(buffer, bits, core, count)
            buffer = jnp.concatenate([jnp.where(first, buffer, other), jnp.where(first, other, buffer)], axis=0)
        return [buffer, swap_cores(buffer, core, count)]

    return sum([chain(*halves[2 * p : 2 * p + 2]) for p in range(PIPES)], [])


def body(
    layer_input, start_memory, horizon, cotangent, first_gain, first_shift, query_projection_weight,
    key_projection_weight, value_projection_weight, relative_weight, content_bias, position_bias,
    output_weight, second_gain, second_shift, expand_weight, expand_bias, shrink_weight, shrink_bias,
):
    rollouts, columns, features = layer_input.shape
    x = layer_input.reshape(rollouts * columns, features)
    position = lax.axis_index("tm")
    tm_count = lax.axis_size("tm")
    arrived = lax.ppermute(x[-SEG:], "tm", [(i, (i + 1) % tm_count) for i in range(tm_count)])
    me = position * lax.axis_size("roll") + lax.axis_index("roll")
    side = me
    for shift in (16, 8, 4, 2, 1):
        side = side ^ (side >> shift)
    side = side & 1
    place = jnp.stack([position, side]).astype(jnp.int32)
    table = jnp.asarray(position_rows())
    basis, turned = (jnp.asarray(part) for part in relative_basis())

    def row(v):
        return v.reshape(1, -1)

    params = (
        row(first_gain), row(first_shift), query_projection_weight, key_projection_weight,
        value_projection_weight, relative_weight, row(content_bias), row(position_bias), output_weight,
        row(second_gain), row(second_shift), expand_weight, row(expand_bias), shrink_weight, row(shrink_bias),
    )
    out, dx, *halves = run_layer(
        place, horizon, x, start_memory.reshape(SEG, features), arrived,
        cotangent.reshape(rollouts * columns, features), table, basis, params,
    )
    summed = unpack(place, sum_everywhere(halves, me, side), turned)
    return (out.reshape(layer_input.shape), dx.reshape(layer_input.shape)) + tuple(summed)


def solution(mesh):
    in_specs = (
        P("roll", "tm", None), P("roll", None, None), P("roll", None), P("roll", "tm", None),
    ) + (P(),) * 15
    out_specs = (P("roll", "tm", None), P("roll", "tm", None)) + (P(),) * 15
    return jax.shard_map(body, mesh=mesh, in_specs=in_specs, out_specs=out_specs, check_vma=False)
```

```python
import functools
import math
import types

import jax
import jax.numpy as jnp
import numpy as np
from jax import lax
from jax.experimental import pallas as pl
from jax.experimental.pallas import tpu as pltpu
from jax.sharding import PartitionSpec as P

HEADS = 8
HEAD_DIM = 32
SEG = 48
STEP = 3
FEATURES = 256
HIDDEN = 1024
LANES = 128
GROUP = LANES // HEAD_DIM
EPSILON = 1e-05
MASKED = -4000000000.0
SCALING = 1.0 / math.sqrt(HEAD_DIM)
SCALING_BITS = SCALING / math.log(2.0)
GELU_A = 0.7978845608028654
GELU_B = 0.044715 * GELU_A
BF = jnp.bfloat16
F32 = jnp.float32

PIPES = 2
PART_ROWS = 832
EARLY_ROWS = (832, 320)
LATE_ROWS = 512
EXPAND_AT = (0, 256, 512, 1664)
SHRINK_AT = (832, 1088, 1344, 1984)
OUTPUT_AT = (768, 1600, 1920, 2240)
OUTPUT_PIECE = 64
QUERY_AT, KEY_AT, VALUE_AT, RELATIVE_AT, VECTOR_AT = 0, 256, 512, 768, 896
(V_CONTENT, V_POSITION, V_GAIN1, V_SHIFT1, V_GAIN2, V_SHIFT2, V_SHRINK, V_EXPAND) = range(8)
VECTOR_ROWS = 16


def position_rows():
    distance = (2 * SEG - 1 - np.arange(2 * SEG)).astype(np.float32)
    freqs = 10000.0 ** (-(2.0 * np.arange(FEATURES // 2)) / FEATURES)
    angles = distance[:, None] * freqs.astype(np.float32)[None, :]
    table = np.concatenate([np.sin(angles), np.cos(angles)], axis=-1)
    return np.pad(table, ((0, LANES - 2 * SEG), (0, 0))).astype(BF)


def relative_basis():
    count = 2 * SEG
    k, c = np.arange(count)[:, None], np.arange(count)[None, :]
    basis = np.cos(np.pi * k * (2 * c + 1) / (2 * count)) * np.where(k == 0, np.sqrt(1.0 / count), np.sqrt(2.0 / count))
    basis = np.pad(basis, ((0, LANES - count), (0, LANES - count)))

    def parts(values):
        high = values.astype(BF)
        low = (values - high.astype(np.float64)).astype(BF)
        return np.concatenate([high, low], axis=0)

    return parts(basis), parts(basis @ position_rows().astype(np.float64))


def tables():
    return jnp.asarray(position_rows()), jnp.asarray(relative_basis()[0])


def interleave(*steps):
    running = [[0, count, part] for count, part in steps]
    while running:
        slowest = min(running, key=lambda entry: entry[0] / entry[1])
        slowest[0] += 1
        if next(slowest[2], None) is None:
            running.remove(slowest)


def dot(a, b):
    return lax.dot_general(a, b, (((1,), (0,)), ((), ())), preferred_element_type=F32)


def dot_t(a, b):
    return lax.dot_general(a, b, (((1,), (1,)), ((), ())), preferred_element_type=F32)


def t_dot(a, b):
    return lax.dot_general(a, b, (((0,), (0,)), ((), ())), preferred_element_type=F32)


def normalize(rows):
    center = rows - jnp.mean(rows, axis=-1, keepdims=True)
    spread = jnp.mean(center * center, axis=-1, keepdims=True)
    scale = lax.rsqrt(spread + EPSILON)
    return center * scale, scale


def column_sum(rows):
    return jnp.sum(rows, axis=0, keepdims=True)


def stack_heads(rows, head_masks):
    return jnp.concatenate([rows * mask for mask in head_masks], axis=0)


def unshift(rows, row_bits):
    rolled = jnp.concatenate(
        [pltpu.roll(rows[a : a + 8], SEG - 8 - a, 1) for a in range(0, SEG - 8, 8)] + [rows[SEG - 8 :]], axis=0
    )
    for step, bit in row_bits:
        rolled = jnp.where(bit, pltpu.roll(rolled, step, 1), rolled)
    return rolled


def pick_heads(rows, lane_head):
    picked = rows[0:SEG]
    for h in range(1, GROUP):
        picked = jnp.where(lane_head == h, rows[h * SEG : (h + 1) * SEG], picked)
    return picked


COPIES = 21
(C_X, C_START, C_ARRIVED, C_COT, C_GAIN1, C_SHIFT1, C_WQ, C_WK, C_WV, C_WR, C_CBIAS, C_PBIAS, C_WO,
 C_GAIN2, C_SHIFT2, C_W1, C_B1, C_W2, C_B2, C_TABLE, C_BASIS) = range(COPIES)
FIRST_COPIES = (C_TABLE, C_WR, C_X, C_GAIN1, C_SHIFT1, C_START, C_ARRIVED, C_WK, C_WV, C_WQ, C_CBIAS, C_PBIAS)
LATER_COPIES = (C_WO, C_GAIN2, C_SHIFT2, C_W1, C_B1, C_COT, C_W2, C_B2, C_BASIS)


def own_place():
    position = lax.axis_index("tm")
    me = position * lax.axis_size("roll") + lax.axis_index("roll")
    side = me
    for shift in (16, 8, 4, 2, 1):
        side = side ^ (side >> shift)
    return position, me, side & 1


def layer_kernel(horizon_source, *refs):
    sources, refs = refs[:COPIES], refs[COPIES:]
    (out_target, dx_target, *halves), refs = refs[: 2 + 2 * PIPES], refs[2 + 2 * PIPES :]
    targets, (sems, out_sems, half_sems, horizon, out, dx, early, late, *scratch) = refs[:COPIES], refs[COPIES:]
    position, _, side = own_place()
    lengths = pltpu.make_async_copy(horizon_source, horizon, sems.at[COPIES])
    lengths.start()
    moves = [pltpu.make_async_copy(a, b, sems.at[i]) for i, (a, b) in enumerate(zip(sources, targets))]
    for i in FIRST_COPIES + LATER_COPIES:
        moves[i].start()
    leaving = []

    def leave(move):
        move.start()
        leaving.append(move)

    def send_rows(which, at):
        source, target = ((out, out_target), (dx, dx_target))[which]
        leave(pltpu.make_async_copy(source.at[at], target.at[at], out_sems.at[len(leaving)]))

    def send_early():
        start = 0
        for p in range(PIPES):
            for k, half in enumerate((side, 1 - side)):
                at = pl.ds(pl.multiple_of(start + half * EARLY_ROWS[p], 64), EARLY_ROWS[p])
                to = halves[2 * p + k].at[0 : EARLY_ROWS[p]]
                leave(pltpu.make_async_copy(early.at[at], to, half_sems.at[2 * p + k]))
            start += 2 * EARLY_ROWS[p]

    def send_late():
        for k, half in enumerate((side, 1 - side)):
            at = pl.ds(pl.multiple_of(half * LATE_ROWS, LATE_ROWS), LATE_ROWS)
            to = halves[2 + k].at[EARLY_ROWS[1] : PART_ROWS]
            leave(pltpu.make_async_copy(late.at[at], to, half_sems.at[2 * PIPES + k]))

    compute_layer(
        position, horizon, lengths, moves, (send_rows, send_early, send_late), *targets, out, dx, early, late, *scratch
    )
    for move in leaving:
        move.wait()


def compute_layer(
    position, horizon, lengths, moves, sends, x, start, arrived, cot, gain1, shift1, wq, wk, wv, wr, cbias, pbias, wo,
    gain2, shift2, w1, b1, w2, b2, table, basis,
    out, dx, early, late,
    nl, xhat, rstd, content, placed, keys_even, keys_odd, values_even, values_odd, relblock, raw, lows, inverses, mixed,
    hid, n2, act, bpre, bmix, bhid, bhl, bcont, bql, braw, kgm, kgs, vgm, vgs, vec,
):
    rows = x.shape[0]
    segments = rows // SEG
    send_rows, send_early, send_late = sends
    vec[...] = jnp.zeros_like(vec)

    def wait_for(*names):
        for i in names:
            moves[i].wait()

    wait_for(C_TABLE, C_WR)
    rel = dot(table[...], wr[...])
    wide_head = lax.broadcasted_iota(jnp.int32, (LANES, FEATURES), 1) // HEAD_DIM
    for h in range(HEADS):
        relblock[h * LANES : (h + 1) * LANES] = jnp.where(wide_head == h, rel, 0.0).astype(BF)

    wait_for(C_X, C_GAIN1, C_SHIFT1, C_START, C_ARRIVED, C_WK, C_WV)
    odd_lane = (lax.broadcasted_iota(jnp.int32, (1, LANES), 1) // HEAD_DIM) & 1
    parity_masks = [(odd_lane == q).astype(F32) for q in range(2)]

    def project(normed, at, count):
        key, value = dot(normed, wk[...]), dot(normed, wv[...])
        for q, (ks, vs) in enumerate(((keys_even, values_even), (keys_odd, values_odd))):
            for g in range(HEADS // GROUP):
                lanes = slice(g * LANES, (g + 1) * LANES)
                ks[pl.ds(at, count), lanes] = (key[:, lanes] * parity_masks[q]).astype(BF)
                vs[pl.ds(at, count), 2 * g * LANES : (2 * g + 1) * LANES] = (value[:, lanes] * parity_masks[q]).astype(BF)

    memory = jnp.where(position == 0, start[...].astype(F32), arrived[...].astype(F32))
    unit, scale = normalize(memory)
    xhat[0:SEG] = unit
    rstd[0:SEG] = scale
    normed = (unit * gain1[...] + shift1[...]).astype(BF)
    nl[0:SEG] = normed
    project(normed, 0, SEG)
    wait_for(C_WQ, C_CBIAS, C_PBIAS)
    lengths.wait()
    block = 8 * SEG
    for edge in range(block, rows + 1, block):
        ahead = slice(edge + SEG, edge + LANES - SEG)
        for ref in (keys_even, keys_odd, values_even, values_odd):
            ref[ahead] = jnp.zeros((LANES - 2 * SEG, ref.shape[1]), BF)
    for q, ref in enumerate((values_even, values_odd)):
        ones = jnp.broadcast_to(parity_masks[q], (ref.shape[0], LANES)).astype(BF)
        for g in range(HEADS // GROUP):
            ref[:, (2 * g + 1) * LANES : (2 * g + 2) * LANES] = ones
    blocks = rows // block
    lane_head = lax.broadcasted_iota(jnp.int32, (SEG, LANES), 1) // HEAD_DIM
    head_masks = [(lane_head == h).astype(F32).astype(BF) for h in range(GROUP)]
    key_at = lax.broadcasted_iota(jnp.int32, (SEG, LANES), 1)
    query_at = lax.broadcasted_iota(jnp.int32, (SEG, LANES), 0) + SEG
    low_row = 7 - (query_at & 7)
    row_bits = [(step, (low_row & step) != 0) for step in (1, 2, 4)]
    upper = (lax.broadcasted_iota(jnp.int32, (SEG, FEATURES), 1) & (HEAD_DIM // 2)) != 0
    first_pair = key_at < 2 * HEAD_DIM
    pair_masks = [first_pair.astype(F32).astype(BF), (key_at >= 2 * HEAD_DIM).astype(F32).astype(BF)]
    blank = jnp.zeros((SEG, LANES), BF)

    def first(i):
        at = pl.ds(i * block, block)
        to = pl.ds(i * block + SEG, block)
        unit, scale = normalize(x[at].astype(F32))
        xhat[to] = unit
        rstd[to] = scale
        normed = (unit * gain1[...] + shift1[...]).astype(BF)
        nl[to] = normed
        yield 1
        project(normed, i * block + SEG, block)
        yield 1
        query = dot(normed, wq[...])
        content[at] = (query + cbias[...]).astype(BF)
        low = (query + pbias[...]).astype(BF)
        placed[at] = low
        yield 1
        for f in range(HEADS * LANES // FEATURES):
            cols = slice(f * FEATURES, (f + 1) * FEATURES)
            raw[at, cols] = dot_t(low, relblock[cols])
            yield 1

    def units_of(i):
        units = []
        for s in range(i * block // SEG, (i + 1) * block // SEG):
            u = types.SimpleNamespace()
            u.s, u.at, u.window = s, pl.ds(s * SEG, SEG), pl.ds(s * SEG, LANES)
            u.pairs = [pl.ds((s * HEADS // 2 + p) * SEG, SEG) for p in range(HEADS // 2)]
            units.append(u)
        return units

    def window_keys(u):
        return jnp.concatenate([keys_even[u.window], keys_odd[u.window]], axis=0)

    def window_values(u, g):
        lanes = slice(2 * g * LANES, (2 * g + 2) * LANES)
        return jnp.concatenate([values_even[u.window, lanes], values_odd[u.window, lanes]], axis=0)

    def group_lanes(g):
        return slice(g * LANES, (g + 1) * LANES)

    def allow(s):
        number = position * segments + s
        current = horizon[0, number]
        previous = jnp.where(number == 0, SEG // STEP, horizon[0, jnp.maximum(number - 1, 0)])
        live = key_at < jnp.where(key_at < SEG, STEP * previous, SEG + STEP * current)
        return (key_at <= query_at) & (live | (key_at == query_at))

    def score(u):
        parts = []
        for p in range(HEADS // 2):
            g = p // 2
            part = content[u.at, group_lanes(g)] * pair_masks[p % 2]
            parts.append(jnp.concatenate([part, blank] if g == 0 else [blank, part], axis=1))
        u.direct = dot_t(jnp.concatenate(parts, axis=0), window_keys(u))

    def mask(u):
        allowed = allow(u.s)
        u.scores = []
        for head in range(HEADS):
            p, q = head // 2, head % 2
            shifted = pltpu.roll(
                raw[u.at, head * LANES : (head + 1) * LANES], LANES - SEG + 1, 1, stride=1, stride_axis=0
            )
            direct = u.direct[p * SEG : (p + 1) * SEG, q * LANES : (q + 1) * LANES]
            u.scores.append(jnp.where(allowed, direct + shifted, MASKED))
        u.tops = [jnp.max(v, axis=-1, keepdims=True) for v in u.scores]

    def exponentiate(u):
        u.low = [jnp.exp2((v - top) * SCALING_BITS).astype(BF) for v, top in zip(u.scores, u.tops)]
        u.low = [jnp.concatenate(u.low[2 * p : 2 * p + 2], axis=1) for p in range(HEADS // 2)]
        for p in range(HEADS // 2):
            lows[u.pairs[p]] = u.low[p]

    def mix(u):
        u.both = [
            dot(jnp.concatenate(u.low[2 * g : 2 * g + 2], axis=0), window_values(u, g)) for g in range(HEADS // GROUP)
        ]

    def finish(u):
        for g in range(HEADS // GROUP):
            both = u.both[g]
            total = jnp.where(first_pair, both[:SEG, LANES:], both[SEG:, LANES:])
            inverse = 1.0 / total
            mx = jnp.where(first_pair, both[:SEG, :LANES], both[SEG:, :LANES]) * inverse
            mixed[u.at, group_lanes(g)] = mx.astype(BF)
            bcont[u.at, group_lanes(g)] = mx
            inverses[u.at, group_lanes(g)] = inverse

    def staged(i, stages):
        units = units_of(i)
        for stage in stages:
            for u in units:
                stage(u)
                yield 1

    def attend(i):
        return staged(i, (score, mask, exponentiate, mix, finish))

    def feed(i):
        at = pl.ds(i * block, block)
        hidden = x[at].astype(F32) + dot(mixed[at], wo[...])
        yield 1
        unit, scale = normalize(hidden)
        low = (unit * gain2[...] + shift2[...]).astype(BF)
        n2[at] = low
        yield 1
        back = cot[at]
        for f in range(HIDDEN // FEATURES):
            cols = slice(f * FEATURES, (f + 1) * FEATURES)
            v = dot(low, w1[:, cols]) + b1[:, cols]
            grad = dot_t(back, w2[cols])
            yield 1
            square = v * v
            half = 0.5 + 0.5 * jnp.tanh(v * (GELU_A + GELU_B * square))
            active = v * half
            act[at, cols] = active.astype(BF)
            slope = half + (2.0 * active) * (1.0 - half) * (GELU_A + (3.0 * GELU_B) * square)
            grad = grad * slope
            vec[V_EXPAND + f : V_EXPAND + f + 1] += column_sum(grad)
            bpre[at, cols] = grad.astype(BF)
            yield 1
        out[at] = (hidden + dot(act[at], w2[...]) + b2[...]).astype(BF)
        send_rows(0, at)
        yield 1
        bn = dot_t(bpre[at], w1[...])
        yield 1
        back = back.astype(F32)
        vec[V_SHRINK : V_SHRINK + 1] += column_sum(back)
        vec[V_GAIN2 : V_GAIN2 + 1] += column_sum(bn * unit)
        vec[V_SHIFT2 : V_SHIFT2 + 1] += column_sum(bn)
        u = bn * gain2[...]
        inner = u - jnp.mean(u, axis=-1, keepdims=True) - unit * jnp.mean(u * unit, axis=-1, keepdims=True)
        bh = back + inner * scale
        bhid[at] = bh
        bl = bh.astype(BF)
        bhl[at] = bl
        yield 1
        bmix[at] = dot_t(bl, wo[...]).astype(BF)
        yield 1

    def feed_weights():
        for f in range(HIDDEN // FEATURES):
            cols = slice(f * FEATURES, (f + 1) * FEATURES)
            early[EXPAND_AT[f] : EXPAND_AT[f] + FEATURES] = t_dot(n2[...], bpre[:, cols]).astype(BF)
            yield 1
            early[SHRINK_AT[f] : SHRINK_AT[f] + FEATURES] = t_dot(act[:, cols], cot[...]).astype(BF)
            yield 1
        weight = t_dot(mixed[...], bhl[...]).astype(BF)
        for k, to in enumerate(OUTPUT_AT):
            early[to : to + OUTPUT_PIECE] = weight[k * OUTPUT_PIECE : (k + 1) * OUTPUT_PIECE]
        send_early()
        yield 1

    def spread(u):
        u.back = (bmix[u.at].astype(F32) * inverses[u.at]).astype(BF)
        product = u.back.astype(F32) * -bcont[u.at]
        left, right = [], []
        for g in range(HEADS // GROUP):
            part = product[:, group_lanes(g)]
            left.append(part + pltpu.roll(part, LANES - HEAD_DIM // 2, 1))
            right.append(part + pltpu.roll(part, HEAD_DIM // 2, 1))
        left, right = jnp.concatenate(left, axis=1), jnp.concatenate(right, axis=1)
        u.along = jnp.where(upper, right, left - left.astype(BF).astype(F32)).astype(BF)

    def widen(u):
        u.wide = []
        for g in range(HEADS // GROUP):
            rows_in = [
                jnp.concatenate([u.back[:, group_lanes(g)] * m, u.along[:, group_lanes(g)] * m], axis=1)
                for m in pair_masks
            ]
            u.wide.append(dot_t(jnp.concatenate(rows_in, axis=0), window_values(u, g)))

    def differentiate(u):
        u.low, u.grad_low = [], []
        for p in range(HEADS // 2):
            low = lows[u.pairs[p]]
            bs = low.astype(F32) * u.wide[p // 2][(p % 2) * SEG : (p % 2 + 1) * SEG]
            u.low.append(low)
            u.grad_low.append(bs.astype(BF))
            for q in range(2):
                head = 2 * p + q
                braw[u.at, head * LANES : (head + 1) * LANES] = unshift(
                    bs[:, q * LANES : (q + 1) * LANES], row_bits
                ).astype(BF)

    def by_head(pairs, g):
        return jnp.concatenate(
            [pairs[p][:, q * LANES : (q + 1) * LANES] for p in (2 * g, 2 * g + 1) for q in range(2)], axis=0
        )

    def collect_values(u):
        for g in range(HEADS // GROUP):
            lanes = group_lanes(g)
            vg = t_dot(by_head(u.low, g), stack_heads(u.back[:, lanes], head_masks)).astype(BF)
            vgm[u.at, lanes] = vg[0:SEG]
            vgs[u.at, lanes] = vg[SEG : 2 * SEG]

    def collect_keys(u):
        for g in range(HEADS // GROUP):
            lanes = group_lanes(g)
            kg = (t_dot(by_head(u.grad_low, g), stack_heads(content[u.at, lanes], head_masks)) * SCALING).astype(BF)
            kgm[u.at, lanes] = kg[0:SEG]
            kgs[u.at, lanes] = kg[SEG : 2 * SEG]

    def collect_queries(u):
        wide = dot(jnp.concatenate(u.grad_low, axis=0), window_keys(u))
        for g in range(HEADS // GROUP):
            lanes = group_lanes(g)
            bcont[u.at, lanes] = SCALING * jnp.where(
                first_pair, wide[2 * g * SEG : (2 * g + 1) * SEG, lanes], wide[(2 * g + 1) * SEG : (2 * g + 2) * SEG, lanes]
            )

    def attend_back(i):
        return staged(i, (spread, widen, differentiate, collect_values, collect_keys, collect_queries))

    def last(i):
        at = pl.ds(i * block, block)
        to = pl.ds(i * block + SEG, block)
        bplace = dot(braw[at], relblock[...]) * SCALING
        yield 1
        bc = bcont[at]
        vec[V_CONTENT : V_CONTENT + 1] += column_sum(bc)
        vec[V_POSITION : V_POSITION + 1] += column_sum(bplace)
        bq = (bc + bplace).astype(BF)
        bql[at] = bq
        yield 1
        bn = dot_t(bq, wq[...]) + dot_t(kgs[at], wk[...]) + dot_t(vgs[at], wv[...])
        yield 1
        bm = dot_t(kgm[at], wk[...]) + dot_t(vgm[at], wv[...])
        yield 1
        unit = xhat[to]
        vec[V_GAIN1 : V_GAIN1 + 1] += column_sum(bn * unit) + column_sum(bm * xhat[at])
        vec[V_SHIFT1 : V_SHIFT1 + 1] += column_sum(bn) + column_sum(bm)
        u = bn * gain1[...]
        inner = u - jnp.mean(u, axis=-1, keepdims=True) - unit * jnp.mean(u * unit, axis=-1, keepdims=True)
        dx[at] = (bhid[at] + inner * rstd[to]).astype(BF)
        send_rows(1, at)
        yield 1

    def attention_weights():
        segment_rows = nl[SEG : SEG + rows]
        memory_rows = nl[0:rows]
        late[QUERY_AT : QUERY_AT + FEATURES] = t_dot(segment_rows, bql[...]).astype(BF)
        yield 1
        late[KEY_AT : KEY_AT + FEATURES] = (t_dot(segment_rows, kgs[...]) + t_dot(memory_rows, kgm[...])).astype(BF)
        yield 1
        late[VALUE_AT : VALUE_AT + FEATURES] = (t_dot(segment_rows, vgs[...]) + t_dot(memory_rows, vgm[...])).astype(BF)
        yield 1
        for g in range(HEADS // GROUP):
            lanes = slice(g * LANES, (g + 1) * LANES)
            across = t_dot(placed[:, lanes], braw[:, g * GROUP * LANES : (g + 1) * GROUP * LANES])
            back = jnp.concatenate(
                [across[h * HEAD_DIM : (h + 1) * HEAD_DIM, h * LANES : (h + 1) * LANES] for h in range(GROUP)], axis=0
            ) * SCALING
            high = back.astype(BF)
            low = (back - high.astype(F32)).astype(BF)
            cosines = dot_t(basis[0:LANES], high) + (dot_t(basis[LANES:], high) + dot_t(basis[0:LANES], low))
            late[RELATIVE_AT : RELATIVE_AT + LANES, lanes] = cosines.astype(BF)
            yield 1

    phases = {
        "first": (8, first), "attend": (5 * block // SEG, attend), "feed": (14, feed), "back": (6 * block // SEG, attend_back), "last": (5, last),
    }
    for t in range(blocks + 4):
        if t == 2:
            wait_for(*LATER_COPIES)
        steps = []
        for lag, (count, phase) in enumerate(phases.values()):
            if 0 <= t - lag < blocks:
                steps.append((count, phase(t - lag)))
        if t == blocks + 2:
            steps.append((9, feed_weights()))
        if t == blocks + 3:
            pass
        interleave(*steps)
    interleave((5, attention_weights()))
    late[VECTOR_AT : VECTOR_AT + VECTOR_ROWS] = vec[...].astype(BF)
    late[VECTOR_AT + VECTOR_ROWS :] = jnp.zeros((2 * LATE_ROWS - VECTOR_AT - VECTOR_ROWS, FEATURES), BF)
    send_late()


def run_layer(horizon, x, start, arrived, cot, table, basis, params):
    rows = x.shape[0]
    operands = (x, start, arrived, cot, *params, table, basis)
    vmem = pl.BlockSpec(memory_space=pltpu.VMEM)
    hbm = pl.BlockSpec(memory_space=pltpu.HBM)
    padded = rows + SEG + LANES - 2 * SEG
    scratch = [
        pltpu.VMEM((rows + SEG, FEATURES), BF),
        pltpu.VMEM((rows + SEG, FEATURES), F32),
        pltpu.VMEM((rows + SEG, 1), F32),
        pltpu.VMEM((rows, FEATURES), BF),
        pltpu.VMEM((rows, FEATURES), BF),
        pltpu.VMEM((padded, FEATURES), BF),
        pltpu.VMEM((padded, FEATURES), BF),
        pltpu.VMEM((padded, 2 * FEATURES), BF),
        pltpu.VMEM((padded, 2 * FEATURES), BF),
        pltpu.VMEM((HEADS * LANES, FEATURES), BF),
        pltpu.VMEM((rows, HEADS * LANES), F32),
        pltpu.VMEM((rows * HEADS // 2, 2 * LANES), BF),
        pltpu.VMEM((rows, FEATURES), F32),
        pltpu.VMEM((rows, FEATURES), BF),
        pltpu.VMEM((rows, FEATURES), F32),
        pltpu.VMEM((rows, FEATURES), BF),
        pltpu.VMEM((rows, HIDDEN), BF),
        pltpu.VMEM((rows, HIDDEN), BF),
        pltpu.VMEM((rows, FEATURES), BF),
        pltpu.VMEM((rows, FEATURES), F32),
        pltpu.VMEM((rows, FEATURES), BF),
        pltpu.VMEM((rows, FEATURES), F32),
        pltpu.VMEM((rows, FEATURES), BF),
        pltpu.VMEM((rows, HEADS * LANES), BF),
        pltpu.VMEM((rows, FEATURES), BF),
        pltpu.VMEM((rows, FEATURES), BF),
        pltpu.VMEM((rows, FEATURES), BF),
        pltpu.VMEM((rows, FEATURES), BF),
        pltpu.VMEM((VECTOR_ROWS, FEATURES), F32),
    ]
    return pl.pallas_call(
        layer_kernel,
        out_shape=(
            jax.ShapeDtypeStruct((rows, FEATURES), BF),
            jax.ShapeDtypeStruct((rows, FEATURES), BF),
        )
        + (jax.ShapeDtypeStruct((PART_ROWS, FEATURES), BF),) * (2 * PIPES),
        in_specs=[hbm] * (COPIES + 1),
        out_specs=(hbm,) * (2 + 2 * PIPES),
        scratch_shapes=[pltpu.VMEM(a.shape, a.dtype) for a in operands]
        + [
            pltpu.SemaphoreType.DMA((COPIES + 1,)),
            pltpu.SemaphoreType.DMA((4 * (rows // SEG) + 2 * PIPES,)),
            pltpu.SemaphoreType.DMA((2 * PIPES + 2,)),
            pltpu.SMEM(horizon.shape, horizon.dtype),
            pltpu.VMEM((rows, FEATURES), BF),
            pltpu.VMEM((rows, FEATURES), BF),
            pltpu.VMEM((2 * sum(EARLY_ROWS), FEATURES), BF),
            pltpu.VMEM((2 * LATE_ROWS, FEATURES), BF),
        ]
        + scratch,
        compiler_params=pltpu.CompilerParams(vmem_limit_bytes=63 * 1024 * 1024),
        name="layer",
    )(horizon, *operands)


def join(own, other, whole):
    _, _, side = own_place()
    for k, part in ((side, own), (1 - side, other)):
        whole[pl.ds(pl.multiple_of(k * PART_ROWS, PART_ROWS), PART_ROWS)] = part[...]


BLOCKS = HIDDEN // FEATURES


def first_unpack_kernel(own, other, w1, w2, wo, whole, expand, shrink, output, sems):
    join(own, other, whole)
    moves = []

    def leave(source, target):
        moves.append(pltpu.make_async_copy(source, target, sems.at[len(moves)]))
        moves[-1].start()

    for f in range(BLOCKS - 1):
        cols = slice(f * FEATURES, (f + 1) * FEATURES)
        expand[f] = whole[f * FEATURES : (f + 1) * FEATURES].astype(F32)
        leave(expand.at[f], w1.at[:, cols])
        shrink[f] = whole[PART_ROWS + f * FEATURES : PART_ROWS + (f + 1) * FEATURES].astype(F32)
        leave(shrink.at[f], w2.at[cols])
    for k in range(2):
        end = (k + 1) * PART_ROWS
        output[k] = whole[end - OUTPUT_PIECE : end].astype(F32)
        leave(output.at[k], wo.at[k * OUTPUT_PIECE : (k + 1) * OUTPUT_PIECE])
    for move in moves:
        move.wait()


def second_unpack_kernel(
    w1_old, w2_old, wo_old, own, other, turned,
    w1, w2, wo, wq, wk, wv, wr, gain1, shift1, cbias, pbias, gain2, shift2, b1, b2,
    whole, expand, shrink, output, sems,
):
    join(own, other, whole)
    moves = []

    def leave(source, target):
        moves.append(pltpu.make_async_copy(source, target, sems.at[len(moves)]))
        moves[-1].start()

    cols = slice(HIDDEN - FEATURES, HIDDEN)
    expand[...] = whole[0:FEATURES].astype(F32)
    leave(expand, w1.at[:, cols])
    shrink[...] = whole[PART_ROWS : PART_ROWS + FEATURES].astype(F32)
    leave(shrink, w2.at[cols])
    for k in range(2):
        start = k * PART_ROWS + FEATURES
        output[k] = whole[start : start + OUTPUT_PIECE].astype(F32)
        leave(output.at[k], wo.at[(k + 2) * OUTPUT_PIECE : (k + 3) * OUTPUT_PIECE])

    def late(at, count):
        at += EARLY_ROWS[1] if at < LATE_ROWS else EARLY_ROWS[1] + PART_ROWS - LATE_ROWS
        return whole[at : at + count]

    for ref, at in ((wq, QUERY_AT), (wk, KEY_AT), (wv, VALUE_AT)):
        ref[...] = late(at, FEATURES).astype(F32)
    cosines = late(RELATIVE_AT, LANES)
    wr[...] = t_dot(turned[0:LANES], cosines) + t_dot(turned[LANES:], cosines)
    vectors = late(VECTOR_AT, VECTOR_ROWS).astype(F32)
    for ref, at in (
        (cbias, V_CONTENT), (pbias, V_POSITION), (gain1, V_GAIN1), (shift1, V_SHIFT1),
        (gain2, V_GAIN2), (shift2, V_SHIFT2), (b2, V_SHRINK),
    ):
        ref[...] = vectors[at]
    for f in range(BLOCKS):
        b1[f * FEATURES : (f + 1) * FEATURES] = vectors[V_EXPAND + f]
    for move in moves:
        move.wait()


def unpack_all(parts, turned):
    vmem = pl.BlockSpec(memory_space=pltpu.VMEM)
    hbm = pl.BlockSpec(memory_space=pl.ANY)
    square, vector = (FEATURES, FEATURES), (FEATURES,)
    split = ((FEATURES, HIDDEN), (HIDDEN, FEATURES), square)
    rest = (square,) * 4 + (vector,) * 6 + ((HIDDEN,), vector)

    def pieces(count):
        lead = (count,) if count > 1 else ()
        return [
            pltpu.VMEM((2 * PART_ROWS, FEATURES), BF),
            pltpu.VMEM((*lead, *square), F32),
            pltpu.VMEM((*lead, *square), F32),
            pltpu.VMEM((2, OUTPUT_PIECE, FEATURES), F32),
            pltpu.SemaphoreType.DMA((2 * count + 2,)),
        ]

    def shapes(dims):
        return tuple(jax.ShapeDtypeStruct(shape, F32) for shape in dims)

    params = pltpu.CompilerParams(vmem_limit_bytes=32 * 1024 * 1024)
    begun = pl.pallas_call(
        first_unpack_kernel,
        out_shape=shapes(split),
        in_specs=[vmem, vmem],
        out_specs=(hbm,) * 3,
        scratch_shapes=pieces(BLOCKS - 1),
        compiler_params=params,
        name="unpack_first",
    )(*parts[:2])
    w1, w2, wo, wq, wk, wv, wr, gain1, shift1, cbias, pbias, gain2, shift2, b1, b2 = pl.pallas_call(
        second_unpack_kernel,
        out_shape=shapes(split + rest),
        in_specs=[hbm] * 3 + [vmem] * 3,
        out_specs=(hbm,) * 3 + (vmem,) * len(rest),
        scratch_shapes=pieces(1),
        input_output_aliases={0: 0, 1: 1, 2: 2},
        compiler_params=params,
        name="unpack_second",
    )(*begun, *parts[2:], turned)
    return gain1, shift1, wq, wk, wv, wr, cbias, pbias, wo, gain2, shift2, w1, b1, w2, b2


AXES = ("tm", "roll")


def exchange_plan(roll_count, tm_count):
    tm_bits = tm_count.bit_length() - 1
    roll_bits = roll_count.bit_length() - 1
    high = [roll_bits + b for b in range(1, tm_bits)]
    rolls = list(range(roll_bits))
    even = high + rolls
    odd = rolls[:1] + high + rolls[1:]
    return roll_bits, list(zip(even, odd))


def side_of(device):
    return bin(device).count("1") & 1


def swap_cores(value, core, count):
    return lax.ppermute(value, AXES, [(d, d ^ (1 << core)) for d in range(count)])


def swap(value, bits, core, count):
    return lax.ppermute(value, AXES, [(d, d ^ (1 << bits[side_of(d)]) ^ (1 << core)) for d in range(count)])


def add_low(a, b):
    return (a.astype(F32) + b.astype(F32)).astype(BF)


def sum_everywhere(halves, me, side):
    roll_count, tm_count = lax.axis_size("roll"), lax.axis_size("tm")
    count = roll_count * tm_count
    core, stages = exchange_plan(roll_count, tm_count)
    halving = 3

    def chain(kept, sent):
        got = swap_cores(sent, core, count)
        firsts = []
        for number, bits in enumerate(stages[:halving]):
            bit = jnp.where(side == 0, (me >> bits[0]) & 1, (me >> bits[1]) & 1)
            half = kept.shape[0] // 2

            def cut(value, which):
                return lax.dynamic_slice_in_dim(value, which * half, half, 0)

            leaving, staying = cut(kept, 1 - bit), cut(kept, bit)
            if number == 0:
                leaving, staying = lax.optimization_barrier((leaving, staying))
            sent = add_low(leaving, cut(got, 1 - bit))
            kept = add_low(staying, cut(got, bit))
            got = swap(sent, bits, core, count)
            firsts.append(bit == 0)
        buffer = add_low(kept, got)
        for bits in stages[halving:]:
            buffer = add_low(buffer, swap(buffer, bits, core, count))
        for bits, first in list(zip(stages, firsts))[::-1]:
            other = swap(buffer, bits, core, count)
            buffer = jnp.concatenate([jnp.where(first, buffer, other), jnp.where(first, other, buffer)], axis=0)
        return [buffer, swap_cores(buffer, core, count)]

    return sum([chain(*halves[2 * p : 2 * p + 2]) for p in range(PIPES)], [])


def body(
    layer_input, start_memory, horizon, cotangent, first_gain, first_shift, query_projection_weight,
    key_projection_weight, value_projection_weight, relative_weight, content_bias, position_bias,
    output_weight, second_gain, second_shift, expand_weight, expand_bias, shrink_weight, shrink_bias,
):
    rollouts, columns, features = layer_input.shape
    x = layer_input.reshape(rollouts * columns, features)
    tm_count = lax.axis_size("tm")
    arrived = lax.ppermute(x[-SEG:], "tm", [(i, (i + 1) % tm_count) for i in range(tm_count)])
    _, me, side = own_place()
    table = jnp.asarray(position_rows())
    basis, turned = (jnp.asarray(part) for part in relative_basis())

    def row(v):
        return v.reshape(1, -1)

    params = (
        row(first_gain), row(first_shift), query_projection_weight, key_projection_weight,
        value_projection_weight, relative_weight, row(content_bias), row(position_bias), output_weight,
        row(second_gain), row(second_shift), expand_weight, row(expand_bias), shrink_weight, row(shrink_bias),
    )
    out, dx, *halves = run_layer(
        horizon, x, start_memory.reshape(SEG, features), arrived,
        cotangent.reshape(rollouts * columns, features), table, basis, params,
    )
    summed = unpack_all(sum_everywhere(halves, me, side), turned)
    return (out.reshape(layer_input.shape), dx.reshape(layer_input.shape)) + tuple(summed)


def solution(mesh):
    in_specs = (
        P("roll", "tm", None), P("roll", None, None), P("roll", None), P("roll", "tm", None),
    ) + (P(),) * 15
    out_specs = (P("roll", "tm", None), P("roll", "tm", None)) + (P(),) * 15
    return jax.shard_map(body, mesh=mesh, in_specs=in_specs, out_specs=out_specs, check_vma=False)
```

```python
import functools
import math
import types

import jax
import jax.numpy as jnp
import numpy as np
from jax import lax
from jax.experimental import pallas as pl
from jax.experimental.pallas import tpu as pltpu
from jax.sharding import PartitionSpec as P

HEADS = 8
HEAD_DIM = 32
SEG = 48
STEP = 3
FEATURES = 256
HIDDEN = 1024
LANES = 128
GROUP = LANES // HEAD_DIM
EPSILON = 1e-05
MASKED = -4000000000.0
SCALING = 1.0 / math.sqrt(HEAD_DIM)
SCALING_BITS = SCALING / math.log(2.0)
GELU_A = 0.7978845608028654
GELU_B = 0.044715 * GELU_A
BF = jnp.bfloat16
F32 = jnp.float32

PIPES = 2
PART_ROWS = 832
EARLY_ROWS = (832, 320)
LATE_ROWS = 512
EXPAND_AT = (0, 256, 512, 1664)
SHRINK_AT = (832, 1088, 1344, 1984)
OUTPUT_AT = (768, 1600, 1920, 2240)
OUTPUT_PIECE = 64
QUERY_AT, KEY_AT, VALUE_AT, RELATIVE_AT, VECTOR_AT = 0, 256, 512, 768, 896
(V_CONTENT, V_POSITION, V_GAIN1, V_SHIFT1, V_GAIN2, V_SHIFT2, V_SHRINK, V_EXPAND) = range(8)
VECTOR_ROWS = 16


def position_rows():
    distance = (2 * SEG - 1 - np.arange(2 * SEG)).astype(np.float32)
    freqs = 10000.0 ** (-(2.0 * np.arange(FEATURES // 2)) / FEATURES)
    angles = distance[:, None] * freqs.astype(np.float32)[None, :]
    table = np.concatenate([np.sin(angles), np.cos(angles)], axis=-1)
    return np.pad(table, ((0, LANES - 2 * SEG), (0, 0))).astype(BF)


def relative_basis():
    count = 2 * SEG
    k, c = np.arange(count)[:, None], np.arange(count)[None, :]
    basis = np.cos(np.pi * k * (2 * c + 1) / (2 * count)) * np.where(k == 0, np.sqrt(1.0 / count), np.sqrt(2.0 / count))
    basis = np.pad(basis, ((0, LANES - count), (0, LANES - count)))

    def parts(values):
        high = values.astype(BF)
        low = (values - high.astype(np.float64)).astype(BF)
        return np.concatenate([high, low], axis=0)

    return parts(basis), parts(basis @ position_rows().astype(np.float64))


def tables():
    return jnp.asarray(position_rows()), jnp.asarray(relative_basis()[0])


def interleave(*steps):
    running = [[0, count, part] for count, part in steps]
    while running:
        slowest = min(running, key=lambda entry: entry[0] / entry[1])
        slowest[0] += 1
        if next(slowest[2], None) is None:
            running.remove(slowest)


def dot(a, b):
    return lax.dot_general(a, b, (((1,), (0,)), ((), ())), preferred_element_type=F32)


def dot_t(a, b):
    return lax.dot_general(a, b, (((1,), (1,)), ((), ())), preferred_element_type=F32)


def t_dot(a, b):
    return lax.dot_general(a, b, (((0,), (0,)), ((), ())), preferred_element_type=F32)


def normalize(rows):
    center = rows - jnp.mean(rows, axis=-1, keepdims=True)
    spread = jnp.mean(center * center, axis=-1, keepdims=True)
    scale = lax.rsqrt(spread + EPSILON)
    return center * scale, scale


def column_sum(rows):
    return jnp.sum(rows, axis=0, keepdims=True)


def stack_heads(rows, head_masks):
    return jnp.concatenate([rows * mask for mask in head_masks], axis=0)


def unshift(rows, row_bits):
    rolled = jnp.concatenate(
        [pltpu.roll(rows[a : a + 16], SEG - 16 - a, 1) for a in range(0, SEG - 16, 16)] + [rows[SEG - 16 :]], axis=0
    )
    for step, bit in row_bits:
        rolled = jnp.where(bit, pltpu.roll(rolled, step, 1), rolled)
    return rolled


def pick_heads(rows, lane_head):
    picked = rows[0:SEG]
    for h in range(1, GROUP):
        picked = jnp.where(lane_head == h, rows[h * SEG : (h + 1) * SEG], picked)
    return picked


COPIES = 21
(C_X, C_START, C_ARRIVED, C_COT, C_GAIN1, C_SHIFT1, C_WQ, C_WK, C_WV, C_WR, C_CBIAS, C_PBIAS, C_WO,
 C_GAIN2, C_SHIFT2, C_W1, C_B1, C_W2, C_B2, C_TABLE, C_BASIS) = range(COPIES)
FIRST_COPIES = (C_TABLE, C_WR, C_X, C_GAIN1, C_SHIFT1, C_START, C_ARRIVED, C_WK, C_WV, C_WQ, C_CBIAS, C_PBIAS)
LATER_COPIES = (C_WO, C_GAIN2, C_SHIFT2, C_W1, C_B1, C_COT, C_W2, C_B2, C_BASIS)


def own_place():
    position = lax.axis_index("tm")
    me = position * lax.axis_size("roll") + lax.axis_index("roll")
    side = me
    for shift in (16, 8, 4, 2, 1):
        side = side ^ (side >> shift)
    return position, me, side & 1


def layer_kernel(horizon_source, *refs):
    sources, refs = refs[:COPIES], refs[COPIES:]
    (out_target, dx_target, *halves), refs = refs[: 2 + 2 * PIPES], refs[2 + 2 * PIPES :]
    targets, (sems, out_sems, half_sems, horizon, out, dx, early, late, *scratch) = refs[:COPIES], refs[COPIES:]
    position, _, side = own_place()
    lengths = pltpu.make_async_copy(horizon_source, horizon, sems.at[COPIES])
    lengths.start()
    moves = [pltpu.make_async_copy(a, b, sems.at[i]) for i, (a, b) in enumerate(zip(sources, targets))]
    for i in FIRST_COPIES + LATER_COPIES:
        moves[i].start()
    leaving = []

    def leave(move):
        move.start()
        leaving.append(move)

    def send_rows(which, at):
        source, target = ((out, out_target), (dx, dx_target))[which]
        leave(pltpu.make_async_copy(source.at[at], target.at[at], out_sems.at[len(leaving)]))

    def send_early():
        start = 0
        for p in range(PIPES):
            for k, half in enumerate((side, 1 - side)):
                at = pl.ds(pl.multiple_of(start + half * EARLY_ROWS[p], 64), EARLY_ROWS[p])
                to = halves[2 * p + k].at[0 : EARLY_ROWS[p]]
                leave(pltpu.make_async_copy(early.at[at], to, half_sems.at[2 * p + k]))
            start += 2 * EARLY_ROWS[p]

    def send_late():
        for k, half in enumerate((side, 1 - side)):
            at = pl.ds(pl.multiple_of(half * LATE_ROWS, LATE_ROWS), LATE_ROWS)
            to = halves[2 + k].at[EARLY_ROWS[1] : PART_ROWS]
            leave(pltpu.make_async_copy(late.at[at], to, half_sems.at[2 * PIPES + k]))

    compute_layer(
        position, horizon, lengths, moves, (send_rows, send_early, send_late), *targets, out, dx, early, late, *scratch
    )
    for move in leaving:
        move.wait()


def compute_layer(
    position, horizon, lengths, moves, sends, x, start, arrived, cot, gain1, shift1, wq, wk, wv, wr, cbias, pbias, wo,
    gain2, shift2, w1, b1, w2, b2, table, basis,
    out, dx, early, late,
    nl, xhat, rstd, content, placed, keys_even, keys_odd, values_even, values_odd, relblock, raw, lows, inverses, mixed,
    hid, n2, act, bpre, bmix, bhid, bhl, bcont, bql, braw, kgm, kgs, vgm, vgs, vec,
):
    rows = x.shape[0]
    segments = rows // SEG
    send_rows, send_early, send_late = sends
    vec[...] = jnp.zeros_like(vec)

    def wait_for(*names):
        for i in names:
            moves[i].wait()

    wait_for(C_TABLE, C_WR)
    rel = dot(table[...], wr[...])
    wide_head = lax.broadcasted_iota(jnp.int32, (LANES, FEATURES), 1) // HEAD_DIM
    for h in range(HEADS):
        relblock[h * LANES : (h + 1) * LANES] = jnp.where(wide_head == h, rel, 0.0).astype(BF)

    wait_for(C_X, C_GAIN1, C_SHIFT1, C_START, C_ARRIVED, C_WK, C_WV)
    odd_lane = (lax.broadcasted_iota(jnp.int32, (1, LANES), 1) // HEAD_DIM) & 1
    parity_masks = [(odd_lane == q).astype(F32) for q in range(2)]

    def project(normed, at, count):
        key, value = dot(normed, wk[...]), dot(normed, wv[...])
        for q, (ks, vs) in enumerate(((keys_even, values_even), (keys_odd, values_odd))):
            for g in range(HEADS // GROUP):
                lanes = slice(g * LANES, (g + 1) * LANES)
                ks[pl.ds(at, count), lanes] = (key[:, lanes] * parity_masks[q]).astype(BF)
                vs[pl.ds(at, count), 2 * g * LANES : (2 * g + 1) * LANES] = (value[:, lanes] * parity_masks[q]).astype(BF)

    memory = jnp.where(position == 0, start[...].astype(F32), arrived[...].astype(F32))
    unit, scale = normalize(memory)
    xhat[0:SEG] = unit
    rstd[0:SEG] = scale
    normed = (unit * gain1[...] + shift1[...]).astype(BF)
    nl[0:SEG] = normed
    project(normed, 0, SEG)
    wait_for(C_WQ, C_CBIAS, C_PBIAS)
    lengths.wait()
    block = 8 * SEG
    for edge in range(block, rows + 1, block):
        ahead = slice(edge + SEG, edge + LANES - SEG)
        for ref in (keys_even, keys_odd, values_even, values_odd):
            ref[ahead] = jnp.zeros((LANES - 2 * SEG, ref.shape[1]), BF)
    for q, ref in enumerate((values_even, values_odd)):
        ones = jnp.broadcast_to(parity_masks[q], (ref.shape[0], LANES)).astype(BF)
        for g in range(HEADS // GROUP):
            ref[:, (2 * g + 1) * LANES : (2 * g + 2) * LANES] = ones
    blocks = rows // block
    lane_head = lax.broadcasted_iota(jnp.int32, (SEG, LANES), 1) // HEAD_DIM
    head_masks = [(lane_head == h).astype(F32).astype(BF) for h in range(GROUP)]
    key_at = lax.broadcasted_iota(jnp.int32, (SEG, LANES), 1)
    query_at = lax.broadcasted_iota(jnp.int32, (SEG, LANES), 0) + SEG
    low_row = 15 - (query_at & 15)
    row_bits = [(step, (low_row & step).astype(F32).astype(BF) > 0.5) for step in (8, 4, 2, 1)]
    upper = (lax.broadcasted_iota(jnp.int32, (SEG, FEATURES), 1) & (HEAD_DIM // 2)) != 0
    first_pair = key_at < 2 * HEAD_DIM
    pair_masks = [first_pair.astype(F32).astype(BF), (key_at >= 2 * HEAD_DIM).astype(F32).astype(BF)]
    blank = jnp.zeros((SEG, LANES), BF)

    def first(i):
        at = pl.ds(i * block, block)
        to = pl.ds(i * block + SEG, block)
        unit, scale = normalize(x[at].astype(F32))
        xhat[to] = unit
        rstd[to] = scale
        normed = (unit * gain1[...] + shift1[...]).astype(BF)
        nl[to] = normed
        yield 1
        project(normed, i * block + SEG, block)
        yield 1
        query = dot(normed, wq[...])
        content[at] = (query + cbias[...]).astype(BF)
        low = (query + pbias[...]).astype(BF)
        placed[at] = low
        yield 1
        for f in range(HEADS * LANES // FEATURES):
            cols = slice(f * FEATURES, (f + 1) * FEATURES)
            raw[at, cols] = dot_t(low, relblock[cols])
            yield 1

    def units_of(i):
        units = []
        for s in range(i * block // SEG, (i + 1) * block // SEG):
            u = types.SimpleNamespace()
            u.s, u.at, u.window = s, pl.ds(s * SEG, SEG), pl.ds(s * SEG, LANES)
            u.pairs = [pl.ds((s * HEADS // 2 + p) * SEG, SEG) for p in range(HEADS // 2)]
            units.append(u)
        return units

    def window_keys(u):
        return jnp.concatenate([keys_even[u.window], keys_odd[u.window]], axis=0)

    def window_values(u, g):
        lanes = slice(2 * g * LANES, (2 * g + 2) * LANES)
        return jnp.concatenate([values_even[u.window, lanes], values_odd[u.window, lanes]], axis=0)

    def group_lanes(g):
        return slice(g * LANES, (g + 1) * LANES)

    def allow(s):
        number = position * segments + s
        current = horizon[0, number]
        previous = jnp.where(number == 0, SEG // STEP, horizon[0, jnp.maximum(number - 1, 0)])
        live = key_at < jnp.where(key_at < SEG, STEP * previous, SEG + STEP * current)
        return (key_at <= query_at) & (live | (key_at == query_at))

    def score(u):
        parts = []
        for p in range(HEADS // 2):
            g = p // 2
            part = content[u.at, group_lanes(g)] * pair_masks[p % 2]
            parts.append(jnp.concatenate([part, blank] if g == 0 else [blank, part], axis=1))
        u.direct = dot_t(jnp.concatenate(parts, axis=0), window_keys(u))

    def mask(u):
        allowed = allow(u.s)
        u.scores = []
        for head in range(HEADS):
            p, q = head // 2, head % 2
            shifted = pltpu.roll(
                raw[u.at, head * LANES : (head + 1) * LANES], LANES - SEG + 1, 1, stride=1, stride_axis=0
            )
            direct = u.direct[p * SEG : (p + 1) * SEG, q * LANES : (q + 1) * LANES]
            u.scores.append(jnp.where(allowed, direct + shifted, MASKED))
        u.tops = [jnp.max(v, axis=-1, keepdims=True) for v in u.scores]

    def exponentiate(u):
        u.low = [jnp.exp2((v - top) * SCALING_BITS).astype(BF) for v, top in zip(u.scores, u.tops)]
        u.low = [jnp.concatenate(u.low[2 * p : 2 * p + 2], axis=1) for p in range(HEADS // 2)]
        for p in range(HEADS // 2):
            lows[u.pairs[p]] = u.low[p]

    def mix(u):
        u.both = [
            dot(jnp.concatenate(u.low[2 * g : 2 * g + 2], axis=0), window_values(u, g)) for g in range(HEADS // GROUP)
        ]

    def finish(u):
        for g in range(HEADS // GROUP):
            both = u.both[g]
            total = jnp.where(first_pair, both[:SEG, LANES:], both[SEG:, LANES:])
            inverse = 1.0 / total
            mx = jnp.where(first_pair, both[:SEG, :LANES], both[SEG:, :LANES]) * inverse
            mixed[u.at, group_lanes(g)] = mx.astype(BF)
            bcont[u.at, group_lanes(g)] = mx
            inverses[u.at, group_lanes(g)] = inverse

    def staged(i, stages):
        units = units_of(i)
        for stage in stages:
            for u in units:
                stage(u)
                yield 1

    def attend(i):
        return staged(i, (score, mask, exponentiate, mix, finish))

    def feed(i):
        at = pl.ds(i * block, block)
        hidden = x[at].astype(F32) + dot(mixed[at], wo[...])
        yield 1
        unit, scale = normalize(hidden)
        low = (unit * gain2[...] + shift2[...]).astype(BF)
        n2[at] = low
        yield 1
        back = cot[at]
        for f in range(HIDDEN // FEATURES):
            cols = slice(f * FEATURES, (f + 1) * FEATURES)
            v = dot(low, w1[:, cols]) + b1[:, cols]
            grad = dot_t(back, w2[cols])
            yield 1
            square = v * v
            half = 0.5 + 0.5 * jnp.tanh(v * (GELU_A + GELU_B * square))
            active = v * half
            act[at, cols] = active.astype(BF)
            slope = half + (2.0 * active) * (1.0 - half) * (GELU_A + (3.0 * GELU_B) * square)
            grad = grad * slope
            vec[V_EXPAND + f : V_EXPAND + f + 1] += column_sum(grad)
            bpre[at, cols] = grad.astype(BF)
            yield 1
        out[at] = (hidden + dot(act[at], w2[...]) + b2[...]).astype(BF)
        send_rows(0, at)
        yield 1
        bn = dot_t(bpre[at], w1[...])
        yield 1
        back = back.astype(F32)
        vec[V_SHRINK : V_SHRINK + 1] += column_sum(back)
        vec[V_GAIN2 : V_GAIN2 + 1] += column_sum(bn * unit)
        vec[V_SHIFT2 : V_SHIFT2 + 1] += column_sum(bn)
        u = bn * gain2[...]
        inner = u - jnp.mean(u, axis=-1, keepdims=True) - unit * jnp.mean(u * unit, axis=-1, keepdims=True)
        bh = back + inner * scale
        bhid[at] = bh
        bl = bh.astype(BF)
        bhl[at] = bl
        yield 1
        bmix[at] = dot_t(bl, wo[...]).astype(BF)
        yield 1

    def feed_weights():
        for f in range(HIDDEN // FEATURES):
            cols = slice(f * FEATURES, (f + 1) * FEATURES)
            early[EXPAND_AT[f] : EXPAND_AT[f] + FEATURES] = t_dot(n2[...], bpre[:, cols]).astype(BF)
            yield 1
            early[SHRINK_AT[f] : SHRINK_AT[f] + FEATURES] = t_dot(act[:, cols], cot[...]).astype(BF)
            yield 1
        weight = t_dot(mixed[...], bhl[...]).astype(BF)
        for k, to in enumerate(OUTPUT_AT):
            early[to : to + OUTPUT_PIECE] = weight[k * OUTPUT_PIECE : (k + 1) * OUTPUT_PIECE]
        send_early()
        yield 1

    def spread(u):
        u.back = (bmix[u.at].astype(F32) * inverses[u.at]).astype(BF)
        product = u.back.astype(F32) * -bcont[u.at]
        left, right = [], []
        for g in range(HEADS // GROUP):
            part = product[:, group_lanes(g)]
            left.append(part + pltpu.roll(part, LANES - HEAD_DIM // 2, 1))
            right.append(part + pltpu.roll(part, HEAD_DIM // 2, 1))
        left, right = jnp.concatenate(left, axis=1), jnp.concatenate(right, axis=1)
        u.along = jnp.where(upper, right, left - left.astype(BF).astype(F32)).astype(BF)

    def widen(u):
        u.wide = []
        for g in range(HEADS // GROUP):
            rows_in = [
                jnp.concatenate([u.back[:, group_lanes(g)] * m, u.along[:, group_lanes(g)] * m], axis=1)
                for m in pair_masks
            ]
            u.wide.append(dot_t(jnp.concatenate(rows_in, axis=0), window_values(u, g)))

    def differentiate(u):
        u.low, u.grad_low = [], []
        for p in range(HEADS // 2):
            low = lows[u.pairs[p]]
            bs = low.astype(F32) * u.wide[p // 2][(p % 2) * SEG : (p % 2 + 1) * SEG]
            u.low.append(low)
            u.grad_low.append(bs.astype(BF))
            for q in range(2):
                head = 2 * p + q
                braw[u.at, head * LANES : (head + 1) * LANES] = unshift(
                    u.grad_low[p][:, q * LANES : (q + 1) * LANES], row_bits
                )

    def by_head(pairs, g):
        return jnp.concatenate(
            [pairs[p][:, q * LANES : (q + 1) * LANES] for p in (2 * g, 2 * g + 1) for q in range(2)], axis=0
        )

    def collect_values(u):
        for g in range(HEADS // GROUP):
            lanes = group_lanes(g)
            vg = t_dot(by_head(u.low, g), stack_heads(u.back[:, lanes], head_masks)).astype(BF)
            vgm[u.at, lanes] = vg[0:SEG]
            vgs[u.at, lanes] = vg[SEG : 2 * SEG]

    def collect_keys(u):
        for g in range(HEADS // GROUP):
            lanes = group_lanes(g)
            kg = (t_dot(by_head(u.grad_low, g), stack_heads(content[u.at, lanes], head_masks)) * SCALING).astype(BF)
            kgm[u.at, lanes] = kg[0:SEG]
            kgs[u.at, lanes] = kg[SEG : 2 * SEG]

    def collect_queries(u):
        wide = dot(jnp.concatenate(u.grad_low, axis=0), window_keys(u))
        for g in range(HEADS // GROUP):
            lanes = group_lanes(g)
            bcont[u.at, lanes] = SCALING * jnp.where(
                first_pair, wide[2 * g * SEG : (2 * g + 1) * SEG, lanes], wide[(2 * g + 1) * SEG : (2 * g + 2) * SEG, lanes]
            )

    def attend_back(i):
        return staged(i, (spread, widen, differentiate, collect_values, collect_keys, collect_queries))

    def last(i):
        at = pl.ds(i * block, block)
        to = pl.ds(i * block + SEG, block)
        bplace = dot(braw[at], relblock[...]) * SCALING
        yield 1
        bc = bcont[at]
        vec[V_CONTENT : V_CONTENT + 1] += column_sum(bc)
        vec[V_POSITION : V_POSITION + 1] += column_sum(bplace)
        bq = (bc + bplace).astype(BF)
        bql[at] = bq
        yield 1
        bn = dot_t(bq, wq[...]) + dot_t(kgs[at], wk[...]) + dot_t(vgs[at], wv[...])
        yield 1
        bm = dot_t(kgm[at], wk[...]) + dot_t(vgm[at], wv[...])
        yield 1
        unit = xhat[to]
        vec[V_GAIN1 : V_GAIN1 + 1] += column_sum(bn * unit) + column_sum(bm * xhat[at])
        vec[V_SHIFT1 : V_SHIFT1 + 1] += column_sum(bn) + column_sum(bm)
        u = bn * gain1[...]
        inner = u - jnp.mean(u, axis=-1, keepdims=True) - unit * jnp.mean(u * unit, axis=-1, keepdims=True)
        dx[at] = (bhid[at] + inner * rstd[to]).astype(BF)
        send_rows(1, at)
        yield 1

    def attention_weights():
        segment_rows = nl[SEG : SEG + rows]
        memory_rows = nl[0:rows]
        late[QUERY_AT : QUERY_AT + FEATURES] = t_dot(segment_rows, bql[...]).astype(BF)
        yield 1
        late[KEY_AT : KEY_AT + FEATURES] = (t_dot(segment_rows, kgs[...]) + t_dot(memory_rows, kgm[...])).astype(BF)
        yield 1
        late[VALUE_AT : VALUE_AT + FEATURES] = (t_dot(segment_rows, vgs[...]) + t_dot(memory_rows, vgm[...])).astype(BF)
        yield 1
        for g in range(HEADS // GROUP):
            lanes = slice(g * LANES, (g + 1) * LANES)
            across = t_dot(placed[:, lanes], braw[:, g * GROUP * LANES : (g + 1) * GROUP * LANES])
            back = jnp.concatenate(
                [across[h * HEAD_DIM : (h + 1) * HEAD_DIM, h * LANES : (h + 1) * LANES] for h in range(GROUP)], axis=0
            ) * SCALING
            high = back.astype(BF)
            low = (back - high.astype(F32)).astype(BF)
            cosines = dot_t(basis[0:LANES], high) + (dot_t(basis[LANES:], high) + dot_t(basis[0:LANES], low))
            late[RELATIVE_AT : RELATIVE_AT + LANES, lanes] = cosines.astype(BF)
            yield 1

    phases = {
        "first": (8, first), "attend": (2 * block // SEG, attend), "feed": (14, feed), "back": (6 * block // SEG, attend_back), "last": (5, last),
    }
    for t in range(blocks + 4):
        if t == 2:
            wait_for(*LATER_COPIES)
        steps = []
        for lag, (count, phase) in enumerate(phases.values()):
            if 0 <= t - lag < blocks:
                steps.append((count, phase(t - lag)))
        if t == blocks + 2:
            steps.append((9, feed_weights()))
        if t == blocks + 3:
            pass
        interleave(*steps)
    interleave((5, attention_weights()))
    late[VECTOR_AT : VECTOR_AT + VECTOR_ROWS] = vec[...].astype(BF)
    late[VECTOR_AT + VECTOR_ROWS :] = jnp.zeros((2 * LATE_ROWS - VECTOR_AT - VECTOR_ROWS, FEATURES), BF)
    send_late()


def run_layer(horizon, x, start, arrived, cot, table, basis, params):
    rows = x.shape[0]
    operands = (x, start, arrived, cot, *params, table, basis)
    vmem = pl.BlockSpec(memory_space=pltpu.VMEM)
    hbm = pl.BlockSpec(memory_space=pltpu.HBM)
    padded = rows + SEG + LANES - 2 * SEG
    scratch = [
        pltpu.VMEM((rows + SEG, FEATURES), BF),
        pltpu.VMEM((rows + SEG, FEATURES), F32),
        pltpu.VMEM((rows + SEG, 1), F32),
        pltpu.VMEM((rows, FEATURES), BF),
        pltpu.VMEM((rows, FEATURES), BF),
        pltpu.VMEM((padded, FEATURES), BF),
        pltpu.VMEM((padded, FEATURES), BF),
        pltpu.VMEM((padded, 2 * FEATURES), BF),
        pltpu.VMEM((padded, 2 * FEATURES), BF),
        pltpu.VMEM((HEADS * LANES, FEATURES), BF),
        pltpu.VMEM((rows, HEADS * LANES), F32),
        pltpu.VMEM((rows * HEADS // 2, 2 * LANES), BF),
        pltpu.VMEM((rows, FEATURES), F32),
        pltpu.VMEM((rows, FEATURES), BF),
        pltpu.VMEM((rows, FEATURES), F32),
        pltpu.VMEM((rows, FEATURES), BF),
        pltpu.VMEM((rows, HIDDEN), BF),
        pltpu.VMEM((rows, HIDDEN), BF),
        pltpu.VMEM((rows, FEATURES), BF),
        pltpu.VMEM((rows, FEATURES), F32),
        pltpu.VMEM((rows, FEATURES), BF),
        pltpu.VMEM((rows, FEATURES), F32),
        pltpu.VMEM((rows, FEATURES), BF),
        pltpu.VMEM((rows, HEADS * LANES), BF),
        pltpu.VMEM((rows, FEATURES), BF),
        pltpu.VMEM((rows, FEATURES), BF),
        pltpu.VMEM((rows, FEATURES), BF),
        pltpu.VMEM((rows, FEATURES), BF),
        pltpu.VMEM((VECTOR_ROWS, FEATURES), F32),
    ]
    return pl.pallas_call(
        layer_kernel,
        out_shape=(
            jax.ShapeDtypeStruct((rows, FEATURES), BF),
            jax.ShapeDtypeStruct((rows, FEATURES), BF),
        )
        + (jax.ShapeDtypeStruct((PART_ROWS, FEATURES), BF),) * (2 * PIPES),
        in_specs=[hbm] * (COPIES + 1),
        out_specs=(hbm,) * (2 + 2 * PIPES),
        scratch_shapes=[pltpu.VMEM(a.shape, a.dtype) for a in operands]
        + [
            pltpu.SemaphoreType.DMA((COPIES + 1,)),
            pltpu.SemaphoreType.DMA((4 * (rows // SEG) + 2 * PIPES,)),
            pltpu.SemaphoreType.DMA((2 * PIPES + 2,)),
            pltpu.SMEM(horizon.shape, horizon.dtype),
            pltpu.VMEM((rows, FEATURES), BF),
            pltpu.VMEM((rows, FEATURES), BF),
            pltpu.VMEM((2 * sum(EARLY_ROWS), FEATURES), BF),
            pltpu.VMEM((2 * LATE_ROWS, FEATURES), BF),
        ]
        + scratch,
        compiler_params=pltpu.CompilerParams(vmem_limit_bytes=63 * 1024 * 1024),
        name="layer",
    )(horizon, *operands)


def join(own, other, whole):
    _, _, side = own_place()
    for k, part in ((side, own), (1 - side, other)):
        whole[pl.ds(pl.multiple_of(k * PART_ROWS, PART_ROWS), PART_ROWS)] = part[...]


BLOCKS = HIDDEN // FEATURES


def first_unpack_kernel(own, other, w1, w2, wo, whole, expand, shrink, output, sems):
    join(own, other, whole)
    moves = []

    def leave(source, target):
        moves.append(pltpu.make_async_copy(source, target, sems.at[len(moves)]))
        moves[-1].start()

    for f in range(BLOCKS - 1):
        cols = slice(f * FEATURES, (f + 1) * FEATURES)
        expand[f] = whole[f * FEATURES : (f + 1) * FEATURES].astype(F32)
        leave(expand.at[f], w1.at[:, cols])
        shrink[f] = whole[PART_ROWS + f * FEATURES : PART_ROWS + (f + 1) * FEATURES].astype(F32)
        leave(shrink.at[f], w2.at[cols])
    for k in range(2):
        end = (k + 1) * PART_ROWS
        output[k] = whole[end - OUTPUT_PIECE : end].astype(F32)
        leave(output.at[k], wo.at[k * OUTPUT_PIECE : (k + 1) * OUTPUT_PIECE])
    for move in moves:
        move.wait()


def second_unpack_kernel(
    w1_old, w2_old, wo_old, own, other, turned, w1, w2, wo, wq, wk, wv, wr, *refs
):
    vectors, (squares, output, longer, whole, sems, *kept) = refs[: V_EXPAND + 1], refs[V_EXPAND + 1 :]
    join(own, other, whole)
    moves = []

    def leave(source, target):
        moves.append(pltpu.make_async_copy(source, target, sems.at[len(moves)]))
        moves[-1].start()

    def late(at, count):
        at += EARLY_ROWS[1] if at < LATE_ROWS else EARLY_ROWS[1] + PART_ROWS - LATE_ROWS
        return whole[at : at + count]

    cosines = late(RELATIVE_AT, LANES)
    squares[5] = t_dot(turned[0:LANES], cosines) + t_dot(turned[LANES:], cosines)
    rows = late(VECTOR_AT, VECTOR_ROWS).astype(F32)
    for k in range(V_EXPAND):
        kept[k][...] = rows[k]
        leave(kept[k], vectors[k])
    for f in range(BLOCKS):
        longer[f * FEATURES : (f + 1) * FEATURES] = rows[V_EXPAND + f]
    leave(longer, vectors[V_EXPAND])
    cols = slice(HIDDEN - FEATURES, HIDDEN)
    squares[0] = whole[0:FEATURES].astype(F32)
    leave(squares.at[0], w1.at[:, cols])
    squares[1] = whole[PART_ROWS : PART_ROWS + FEATURES].astype(F32)
    leave(squares.at[1], w2.at[cols])
    for k, (ref, at) in enumerate(((wq, QUERY_AT), (wk, KEY_AT), (wv, VALUE_AT))):
        squares[k + 2] = late(at, FEATURES).astype(F32)
        leave(squares.at[k + 2], ref)
    leave(squares.at[5], wr)
    for k in range(2):
        start = k * PART_ROWS + FEATURES
        output[k] = whole[start : start + OUTPUT_PIECE].astype(F32)
        leave(output.at[k], wo.at[(k + 2) * OUTPUT_PIECE : (k + 3) * OUTPUT_PIECE])
    for move in moves:
        move.wait()


def unpack_all(parts, turned):
    vmem = pl.BlockSpec(memory_space=pltpu.VMEM)
    hbm = pl.BlockSpec(memory_space=pl.ANY)
    square, vector = (FEATURES, FEATURES), (FEATURES,)
    split = ((FEATURES, HIDDEN), (HIDDEN, FEATURES), square)
    rest = (square,) * 4 + (vector,) * V_EXPAND + ((HIDDEN,),)
    whole = pltpu.VMEM((2 * PART_ROWS, FEATURES), BF)
    output = pltpu.VMEM((2, OUTPUT_PIECE, FEATURES), F32)

    def shapes(dims):
        return tuple(jax.ShapeDtypeStruct(shape, F32) for shape in dims)

    params = pltpu.CompilerParams(vmem_limit_bytes=32 * 1024 * 1024)
    begun = pl.pallas_call(
        first_unpack_kernel,
        out_shape=shapes(split),
        in_specs=[vmem, vmem],
        out_specs=(hbm,) * 3,
        scratch_shapes=[
            whole,
            pltpu.VMEM((BLOCKS - 1, *square), F32),
            pltpu.VMEM((BLOCKS - 1, *square), F32),
            output,
            pltpu.SemaphoreType.DMA((2 * BLOCKS,)),
        ],
        compiler_params=params,
        name="unpack_first",
    )(*parts[:2])
    w1, w2, wo, wq, wk, wv, wr, cbias, pbias, gain1, shift1, gain2, shift2, b2, b1 = pl.pallas_call(
        second_unpack_kernel,
        out_shape=shapes(split + rest),
        in_specs=[hbm] * 3 + [vmem] * 3,
        out_specs=(hbm,) * (3 + len(rest)),
        scratch_shapes=[
            pltpu.VMEM((6, *square), F32),
            output,
            pltpu.VMEM((HIDDEN,), F32),
            whole,
            pltpu.SemaphoreType.DMA((8 + V_EXPAND + 1,)),
        ]
        + [pltpu.VMEM(vector, F32)] * V_EXPAND,
        input_output_aliases={0: 0, 1: 1, 2: 2},
        compiler_params=params,
        name="unpack_second",
    )(*begun, *parts[2:], turned)
    return gain1, shift1, wq, wk, wv, wr, cbias, pbias, wo, gain2, shift2, w1, b1, w2, b2


AXES = ("tm", "roll")


def exchange_plan(roll_count, tm_count):
    tm_bits = tm_count.bit_length() - 1
    roll_bits = roll_count.bit_length() - 1
    high = [roll_bits + b for b in range(1, tm_bits)]
    rolls = list(range(roll_bits))
    even = high + rolls
    odd = rolls[:1] + high + rolls[1:]
    return roll_bits, list(zip(even, odd))


def side_of(device):
    return bin(device).count("1") & 1


def swap_cores(value, core, count):
    return lax.ppermute(value, AXES, [(d, d ^ (1 << core)) for d in range(count)])


def swap(value, bits, core, count):
    return lax.ppermute(value, AXES, [(d, d ^ (1 << bits[side_of(d)]) ^ (1 << core)) for d in range(count)])


def add_low(a, b):
    return (a.astype(F32) + b.astype(F32)).astype(BF)


def sum_everywhere(halves, me, side):
    roll_count, tm_count = lax.axis_size("roll"), lax.axis_size("tm")
    count = roll_count * tm_count
    core, stages = exchange_plan(roll_count, tm_count)
    halving = 3

    def chain(kept, sent):
        got = swap_cores(sent, core, count)
        firsts = []
        for number, bits in enumerate(stages[:halving]):
            bit = jnp.where(side == 0, (me >> bits[0]) & 1, (me >> bits[1]) & 1)
            half = kept.shape[0] // 2

            def cut(value, which):
                return lax.dynamic_slice_in_dim(value, which * half, half, 0)

            leaving, staying = cut(kept, 1 - bit), cut(kept, bit)
            if number == 0:
                leaving, staying = lax.optimization_barrier((leaving, staying))
            sent = add_low(leaving, cut(got, 1 - bit))
            kept = add_low(staying, cut(got, bit))
            got = swap(sent, bits, core, count)
            firsts.append(bit == 0)
        buffer = add_low(kept, got)
        for bits in stages[halving:]:
            buffer = add_low(buffer, swap(buffer, bits, core, count))
        for bits, first in list(zip(stages, firsts))[::-1]:
            other = swap(buffer, bits, core, count)
            buffer = jnp.concatenate([jnp.where(first, buffer, other), jnp.where(first, other, buffer)], axis=0)
        return [buffer, swap_cores(buffer, core, count)]

    return sum([chain(*halves[2 * p : 2 * p + 2]) for p in range(PIPES)], [])


def body(
    layer_input, start_memory, horizon, cotangent, first_gain, first_shift, query_projection_weight,
    key_projection_weight, value_projection_weight, relative_weight, content_bias, position_bias,
    output_weight, second_gain, second_shift, expand_weight, expand_bias, shrink_weight, shrink_bias,
):
    rollouts, columns, features = layer_input.shape
    x = layer_input.reshape(rollouts * columns, features)
    tm_count = lax.axis_size("tm")
    arrived = lax.ppermute(x[-SEG:], "tm", [(i, (i + 1) % tm_count) for i in range(tm_count)])
    _, me, side = own_place()
    table = jnp.asarray(position_rows())
    basis, turned = (jnp.asarray(part) for part in relative_basis())

    def row(v):
        return v.reshape(1, -1)

    params = (
        row(first_gain), row(first_shift), query_projection_weight, key_projection_weight,
        value_projection_weight, relative_weight, row(content_bias), row(position_bias), output_weight,
        row(second_gain), row(second_shift), expand_weight, row(expand_bias), shrink_weight, row(shrink_bias),
    )
    out, dx, *halves = run_layer(
        horizon, x, start_memory.reshape(SEG, features), arrived,
        cotangent.reshape(rollouts * columns, features), table, basis, params,
    )
    summed = unpack_all(sum_everywhere(halves, me, side), turned)
    return (out.reshape(layer_input.shape), dx.reshape(layer_input.shape)) + tuple(summed)


def solution(mesh):
    in_specs = (
        P("roll", "tm", None), P("roll", None, None), P("roll", None), P("roll", "tm", None),
    ) + (P(),) * 15
    out_specs = (P("roll", "tm", None), P("roll", "tm", None)) + (P(),) * 15
    return jax.shard_map(body, mesh=mesh, in_specs=in_specs, out_specs=out_specs, check_vma=False)
```

```python
import functools
import math
import types

import jax
import jax.numpy as jnp
import numpy as np
from jax import lax
from jax.experimental import pallas as pl
from jax.experimental.pallas import tpu as pltpu
from jax.sharding import PartitionSpec as P

HEADS = 8
HEAD_DIM = 32
SEG = 48
STEP = 3
FEATURES = 256
HIDDEN = 1024
LANES = 128
GROUP = LANES // HEAD_DIM
EPSILON = 1e-05
MASKED = -4000000000.0
SCALING = 1.0 / math.sqrt(HEAD_DIM)
SCALING_BITS = SCALING / math.log(2.0)
GELU_A = 0.7978845608028654
GELU_B = 0.044715 * GELU_A
BF = jnp.bfloat16
F32 = jnp.float32

PIPES = 2
PART_ROWS = 832
EARLY_ROWS = (832, 320)
LATE_ROWS = 512
EXPAND_AT = (0, 256, 512, 1664)
SHRINK_AT = (832, 1088, 1344, 1984)
OUTPUT_AT = (768, 1600, 1920, 2240)
OUTPUT_PIECE = 64
QUERY_AT, KEY_AT, VALUE_AT, RELATIVE_AT, VECTOR_AT = 0, 256, 512, 768, 896
(V_CONTENT, V_POSITION, V_GAIN1, V_SHIFT1, V_GAIN2, V_SHIFT2, V_SHRINK, V_EXPAND) = range(8)
VECTOR_ROWS = 16


def position_rows():
    distance = (2 * SEG - 1 - np.arange(2 * SEG)).astype(np.float32)
    freqs = 10000.0 ** (-(2.0 * np.arange(FEATURES // 2)) / FEATURES)
    angles = distance[:, None] * freqs.astype(np.float32)[None, :]
    table = np.concatenate([np.sin(angles), np.cos(angles)], axis=-1)
    return np.pad(table, ((0, LANES - 2 * SEG), (0, 0))).astype(BF)


def relative_basis():
    count = 2 * SEG
    k, c = np.arange(count)[:, None], np.arange(count)[None, :]
    basis = np.cos(np.pi * k * (2 * c + 1) / (2 * count)) * np.where(k == 0, np.sqrt(1.0 / count), np.sqrt(2.0 / count))
    basis = np.pad(basis, ((0, LANES - count), (0, LANES - count)))

    def parts(values):
        high = values.astype(BF)
        low = (values - high.astype(np.float64)).astype(BF)
        return np.concatenate([high, low], axis=0)

    return parts(basis), parts(basis @ position_rows().astype(np.float64))


def tables():
    return jnp.asarray(position_rows()), jnp.asarray(relative_basis()[0])


def interleave(*steps):
    running = [[0, count, part] for count, part in steps]
    while running:
        slowest = min(running, key=lambda entry: entry[0] / entry[1])
        slowest[0] += 1
        if next(slowest[2], None) is None:
            running.remove(slowest)


def dot(a, b):
    return lax.dot_general(a, b, (((1,), (0,)), ((), ())), preferred_element_type=F32)


def dot_t(a, b):
    return lax.dot_general(a, b, (((1,), (1,)), ((), ())), preferred_element_type=F32)


def t_dot(a, b):
    return lax.dot_general(a, b, (((0,), (0,)), ((), ())), preferred_element_type=F32)


def normalize(rows):
    center = rows - jnp.mean(rows, axis=-1, keepdims=True)
    spread = jnp.mean(center * center, axis=-1, keepdims=True)
    scale = lax.rsqrt(spread + EPSILON)
    return center * scale, scale


def column_sum(rows):
    return jnp.sum(rows, axis=0, keepdims=True)


def stack_heads(rows, head_masks):
    return jnp.concatenate([rows * mask for mask in head_masks], axis=0)


def unshift(rows, row_bits):
    rolled = jnp.concatenate(
        [pltpu.roll(rows[a : a + 16], SEG - 16 - a, 1) for a in range(0, SEG - 16, 16)] + [rows[SEG - 16 :]], axis=0
    )
    for step, bit in row_bits:
        rolled = jnp.where(bit, pltpu.roll(rolled, step, 1), rolled)
    return rolled


def pick_heads(rows, lane_head):
    picked = rows[0:SEG]
    for h in range(1, GROUP):
        picked = jnp.where(lane_head == h, rows[h * SEG : (h + 1) * SEG], picked)
    return picked


COPIES = 21
(C_X, C_START, C_ARRIVED, C_COT, C_GAIN1, C_SHIFT1, C_WQ, C_WK, C_WV, C_WR, C_CBIAS, C_PBIAS, C_WO,
 C_GAIN2, C_SHIFT2, C_W1, C_B1, C_W2, C_B2, C_TABLE, C_BASIS) = range(COPIES)
FIRST_COPIES = (C_TABLE, C_WR, C_X, C_GAIN1, C_SHIFT1, C_START, C_ARRIVED, C_WK, C_WV, C_WQ, C_CBIAS, C_PBIAS)
LATER_COPIES = (C_WO, C_GAIN2, C_SHIFT2, C_W1, C_B1, C_COT, C_W2, C_B2, C_BASIS)


def own_place():
    position = lax.axis_index("tm")
    me = position * lax.axis_size("roll") + lax.axis_index("roll")
    side = me
    for shift in (16, 8, 4, 2, 1):
        side = side ^ (side >> shift)
    return position, me, side & 1


def layer_kernel(horizon_source, *refs):
    sources, refs = refs[:COPIES], refs[COPIES:]
    (out_target, dx_target, *halves), refs = refs[: 2 + 2 * PIPES], refs[2 + 2 * PIPES :]
    targets, (sems, out_sems, half_sems, horizon, out, dx, early, late, *scratch) = refs[:COPIES], refs[COPIES:]
    position, _, side = own_place()
    lengths = pltpu.make_async_copy(horizon_source, horizon, sems.at[COPIES])
    lengths.start()
    moves = [pltpu.make_async_copy(a, b, sems.at[i]) for i, (a, b) in enumerate(zip(sources, targets))]
    for i in FIRST_COPIES + LATER_COPIES:
        moves[i].start()
    leaving = []

    def leave(move):
        move.start()
        leaving.append(move)

    def send_rows(which, at):
        source, target = ((out, out_target), (dx, dx_target))[which]
        leave(pltpu.make_async_copy(source.at[at], target.at[at], out_sems.at[len(leaving)]))

    def send_early():
        start = 0
        for p in range(PIPES):
            for k, half in enumerate((side, 1 - side)):
                at = pl.ds(pl.multiple_of(start + half * EARLY_ROWS[p], 64), EARLY_ROWS[p])
                to = halves[2 * p + k].at[0 : EARLY_ROWS[p]]
                leave(pltpu.make_async_copy(early.at[at], to, half_sems.at[2 * p + k]))
            start += 2 * EARLY_ROWS[p]

    def send_late(piece):
        for k, half in enumerate((side, 1 - side)):
            at = pl.ds(pl.multiple_of(half * LATE_ROWS + piece * FEATURES, FEATURES), FEATURES)
            to = halves[2 + k].at[EARLY_ROWS[1] + piece * FEATURES : EARLY_ROWS[1] + (piece + 1) * FEATURES]
            leave(pltpu.make_async_copy(late.at[at], to, half_sems.at[2 * PIPES + 2 * piece + k]))

    compute_layer(
        position, horizon, lengths, moves, (send_rows, send_early, send_late), *targets, out, dx, early, late, *scratch
    )
    for move in leaving:
        move.wait()


def compute_layer(
    position, horizon, lengths, moves, sends, x, start, arrived, cot, gain1, shift1, wq, wk, wv, wr, cbias, pbias, wo,
    gain2, shift2, w1, b1, w2, b2, table, basis,
    out, dx, early, late,
    nl, xhat, rstd, content, placed, keys_even, keys_odd, values_even, values_odd, relblock, raw, lows, inverses, mixed,
    hid, n2, act, bpre, bmix, bhid, bhl, bcont, bql, braw, kgm, kgs, vgm, vgs, vec,
):
    rows = x.shape[0]
    segments = rows // SEG
    send_rows, send_early, send_late = sends
    vec[...] = jnp.zeros_like(vec)

    def wait_for(*names):
        for i in names:
            moves[i].wait()

    wait_for(C_TABLE, C_WR)
    rel = dot(table[...], wr[...])
    wide_head = lax.broadcasted_iota(jnp.int32, (LANES, FEATURES), 1) // HEAD_DIM
    for h in range(HEADS):
        relblock[h * LANES : (h + 1) * LANES] = jnp.where(wide_head == h, rel, 0.0).astype(BF)

    wait_for(C_X, C_GAIN1, C_SHIFT1, C_START, C_ARRIVED, C_WK, C_WV)
    odd_lane = (lax.broadcasted_iota(jnp.int32, (1, LANES), 1) // HEAD_DIM) & 1
    parity_masks = [(odd_lane == q).astype(F32) for q in range(2)]

    def project(normed, at, count):
        key, value = dot(normed, wk[...]), dot(normed, wv[...])
        for q, (ks, vs) in enumerate(((keys_even, values_even), (keys_odd, values_odd))):
            for g in range(HEADS // GROUP):
                lanes = slice(g * LANES, (g + 1) * LANES)
                ks[pl.ds(at, count), lanes] = (key[:, lanes] * parity_masks[q]).astype(BF)
                vs[pl.ds(at, count), 2 * g * LANES : (2 * g + 1) * LANES] = (value[:, lanes] * parity_masks[q]).astype(BF)

    memory = jnp.where(position == 0, start[...].astype(F32), arrived[...].astype(F32))
    unit, scale = normalize(memory)
    xhat[0:SEG] = unit
    rstd[0:SEG] = scale
    normed = (unit * gain1[...] + shift1[...]).astype(BF)
    nl[0:SEG] = normed
    project(normed, 0, SEG)
    wait_for(C_WQ, C_CBIAS, C_PBIAS)
    lengths.wait()
    block = 8 * SEG
    for edge in range(block, rows + 1, block):
        ahead = slice(edge + SEG, edge + LANES - SEG)
        for ref in (keys_even, keys_odd, values_even, values_odd):
            ref[ahead] = jnp.zeros((LANES - 2 * SEG, ref.shape[1]), BF)
    for q, ref in enumerate((values_even, values_odd)):
        ones = jnp.broadcast_to(parity_masks[q], (ref.shape[0], LANES)).astype(BF)
        for g in range(HEADS // GROUP):
            ref[:, (2 * g + 1) * LANES : (2 * g + 2) * LANES] = ones
    blocks = rows // block
    lane_head = lax.broadcasted_iota(jnp.int32, (SEG, LANES), 1) // HEAD_DIM
    head_masks = [(lane_head == h).astype(F32).astype(BF) for h in range(GROUP)]
    key_at = lax.broadcasted_iota(jnp.int32, (SEG, LANES), 1)
    query_at = lax.broadcasted_iota(jnp.int32, (SEG, LANES), 0) + SEG
    low_row = 15 - (query_at & 15)
    row_bits = [(step, (low_row & step).astype(F32).astype(BF) > 0.5) for step in (8, 4, 2, 1)]
    upper = (lax.broadcasted_iota(jnp.int32, (SEG, FEATURES), 1) & (HEAD_DIM // 2)) != 0
    first_pair = key_at < 2 * HEAD_DIM
    pair_masks = [first_pair.astype(F32).astype(BF), (key_at >= 2 * HEAD_DIM).astype(F32).astype(BF)]
    blank = jnp.zeros((SEG, LANES), BF)

    def first(i):
        at = pl.ds(i * block, block)
        to = pl.ds(i * block + SEG, block)
        unit, scale = normalize(x[at].astype(F32))
        xhat[to] = unit
        rstd[to] = scale
        normed = (unit * gain1[...] + shift1[...]).astype(BF)
        nl[to] = normed
        yield 1
        project(normed, i * block + SEG, block)
        yield 1
        query = dot(normed, wq[...])
        content[at] = (query + cbias[...]).astype(BF)
        low = (query + pbias[...]).astype(BF)
        placed[at] = low
        yield 1
        for f in range(HEADS * LANES // FEATURES):
            cols = slice(f * FEATURES, (f + 1) * FEATURES)
            raw[at, cols] = dot_t(low, relblock[cols])
            yield 1

    def units_of(i):
        units = []
        for s in range(i * block // SEG, (i + 1) * block // SEG):
            u = types.SimpleNamespace()
            u.s, u.at, u.window = s, pl.ds(s * SEG, SEG), pl.ds(s * SEG, LANES)
            u.pairs = [pl.ds((s * HEADS // 2 + p) * SEG, SEG) for p in range(HEADS // 2)]
            units.append(u)
        return units

    def window_keys(u):
        return jnp.concatenate([keys_even[u.window], keys_odd[u.window]], axis=0)

    def window_values(u, g):
        lanes = slice(2 * g * LANES, (2 * g + 2) * LANES)
        return jnp.concatenate([values_even[u.window, lanes], values_odd[u.window, lanes]], axis=0)

    def group_lanes(g):
        return slice(g * LANES, (g + 1) * LANES)

    def allow(s):
        number = position * segments + s
        current = horizon[0, number]
        previous = jnp.where(number == 0, SEG // STEP, horizon[0, jnp.maximum(number - 1, 0)])
        live = key_at < jnp.where(key_at < SEG, STEP * previous, SEG + STEP * current)
        return (key_at <= query_at) & (live | (key_at == query_at))

    def score(u):
        parts = []
        for p in range(HEADS // 2):
            g = p // 2
            part = content[u.at, group_lanes(g)] * pair_masks[p % 2]
            parts.append(jnp.concatenate([part, blank] if g == 0 else [blank, part], axis=1))
        u.direct = dot_t(jnp.concatenate(parts, axis=0), window_keys(u))

    def mask(u):
        allowed = allow(u.s)
        u.scores = []
        for head in range(HEADS):
            p, q = head // 2, head % 2
            shifted = pltpu.roll(
                raw[u.at, head * LANES : (head + 1) * LANES], LANES - SEG + 1, 1, stride=1, stride_axis=0
            )
            direct = u.direct[p * SEG : (p + 1) * SEG, q * LANES : (q + 1) * LANES]
            u.scores.append(jnp.where(allowed, direct + shifted, MASKED))
        u.tops = [jnp.max(v, axis=-1, keepdims=True) for v in u.scores]

    def exponentiate(u):
        u.low = [jnp.exp2((v - top) * SCALING_BITS).astype(BF) for v, top in zip(u.scores, u.tops)]
        u.low = [jnp.concatenate(u.low[2 * p : 2 * p + 2], axis=1) for p in range(HEADS // 2)]
        for p in range(HEADS // 2):
            lows[u.pairs[p]] = u.low[p]

    def mix(u):
        u.both = [
            dot(jnp.concatenate(u.low[2 * g : 2 * g + 2], axis=0), window_values(u, g)) for g in range(HEADS // GROUP)
        ]

    def finish(u):
        for g in range(HEADS // GROUP):
            both = u.both[g]
            total = jnp.where(first_pair, both[:SEG, LANES:], both[SEG:, LANES:])
            inverse = 1.0 / total
            mx = jnp.where(first_pair, both[:SEG, :LANES], both[SEG:, :LANES]) * inverse
            mixed[u.at, group_lanes(g)] = mx.astype(BF)
            bcont[u.at, group_lanes(g)] = mx
            inverses[u.at, group_lanes(g)] = inverse

    def staged(i, stages):
        units = units_of(i)
        for stage in stages:
            for u in units:
                stage(u)
                yield 1

    def attend(i):
        return staged(i, (score, mask, exponentiate, mix, finish))

    def feed(i):
        at = pl.ds(i * block, block)
        hidden = x[at].astype(F32) + dot(mixed[at], wo[...])
        yield 1
        unit, scale = normalize(hidden)
        low = (unit * gain2[...] + shift2[...]).astype(BF)
        n2[at] = low
        yield 1
        back = cot[at]
        for f in range(HIDDEN // FEATURES):
            cols = slice(f * FEATURES, (f + 1) * FEATURES)
            v = dot(low, w1[:, cols]) + b1[:, cols]
            grad = dot_t(back, w2[cols])
            yield 1
            square = v * v
            half = 0.5 + 0.5 * jnp.tanh(v * (GELU_A + GELU_B * square))
            active = v * half
            act[at, cols] = active.astype(BF)
            slope = half + (2.0 * active) * (1.0 - half) * (GELU_A + (3.0 * GELU_B) * square)
            grad = grad * slope
            vec[V_EXPAND + f : V_EXPAND + f + 1] += column_sum(grad)
            bpre[at, cols] = grad.astype(BF)
            yield 1
        out[at] = (hidden + dot(act[at], w2[...]) + b2[...]).astype(BF)
        send_rows(0, at)
        yield 1
        bn = dot_t(bpre[at], w1[...])
        yield 1
        back = back.astype(F32)
        vec[V_SHRINK : V_SHRINK + 1] += column_sum(back)
        vec[V_GAIN2 : V_GAIN2 + 1] += column_sum(bn * unit)
        vec[V_SHIFT2 : V_SHIFT2 + 1] += column_sum(bn)
        u = bn * gain2[...]
        inner = u - jnp.mean(u, axis=-1, keepdims=True) - unit * jnp.mean(u * unit, axis=-1, keepdims=True)
        bh = back + inner * scale
        bhid[at] = bh
        bl = bh.astype(BF)
        bhl[at] = bl
        yield 1
        bmix[at] = dot_t(bl, wo[...]).astype(BF)
        yield 1

    def feed_weights():
        for f in range(HIDDEN // FEATURES):
            cols = slice(f * FEATURES, (f + 1) * FEATURES)
            early[EXPAND_AT[f] : EXPAND_AT[f] + FEATURES] = t_dot(n2[...], bpre[:, cols]).astype(BF)
            yield 1
            early[SHRINK_AT[f] : SHRINK_AT[f] + FEATURES] = t_dot(act[:, cols], cot[...]).astype(BF)
            yield 1
        weight = t_dot(mixed[...], bhl[...]).astype(BF)
        for k, to in enumerate(OUTPUT_AT):
            early[to : to + OUTPUT_PIECE] = weight[k * OUTPUT_PIECE : (k + 1) * OUTPUT_PIECE]
        send_early()
        yield 1

    def spread(u):
        u.back = (bmix[u.at].astype(F32) * inverses[u.at]).astype(BF)
        product = u.back.astype(F32) * -bcont[u.at]
        left, right = [], []
        for g in range(HEADS // GROUP):
            part = product[:, group_lanes(g)]
            left.append(part + pltpu.roll(part, LANES - HEAD_DIM // 2, 1))
            right.append(part + pltpu.roll(part, HEAD_DIM // 2, 1))
        left, right = jnp.concatenate(left, axis=1), jnp.concatenate(right, axis=1)
        u.along = jnp.where(upper, right, left - left.astype(BF).astype(F32)).astype(BF)

    def widen(u):
        u.wide = []
        for g in range(HEADS // GROUP):
            rows_in = [
                jnp.concatenate([u.back[:, group_lanes(g)] * m, u.along[:, group_lanes(g)] * m], axis=1)
                for m in pair_masks
            ]
            u.wide.append(dot_t(jnp.concatenate(rows_in, axis=0), window_values(u, g)))

    def differentiate(u):
        u.low, u.grad_low = [], []
        for p in range(HEADS // 2):
            low = lows[u.pairs[p]]
            bs = low.astype(F32) * u.wide[p // 2][(p % 2) * SEG : (p % 2 + 1) * SEG]
            u.low.append(low)
            u.grad_low.append(bs.astype(BF))
            for q in range(2):
                head = 2 * p + q
                braw[u.at, head * LANES : (head + 1) * LANES] = unshift(
                    u.grad_low[p][:, q * LANES : (q + 1) * LANES], row_bits
                )

    def by_head(pairs, g):
        return jnp.concatenate(
            [pairs[p][:, q * LANES : (q + 1) * LANES] for p in (2 * g, 2 * g + 1) for q in range(2)], axis=0
        )

    def collect_values(u):
        for g in range(HEADS // GROUP):
            lanes = group_lanes(g)
            vg = t_dot(by_head(u.low, g), stack_heads(u.back[:, lanes], head_masks)).astype(BF)
            vgm[u.at, lanes] = vg[0:SEG]
            vgs[u.at, lanes] = vg[SEG : 2 * SEG]

    def collect_keys(u):
        for g in range(HEADS // GROUP):
            lanes = group_lanes(g)
            kg = (t_dot(by_head(u.grad_low, g), stack_heads(content[u.at, lanes], head_masks)) * SCALING).astype(BF)
            kgm[u.at, lanes] = kg[0:SEG]
            kgs[u.at, lanes] = kg[SEG : 2 * SEG]

    def collect_queries(u):
        wide = dot(jnp.concatenate(u.grad_low, axis=0), window_keys(u))
        for g in range(HEADS // GROUP):
            lanes = group_lanes(g)
            bcont[u.at, lanes] = SCALING * jnp.where(
                first_pair, wide[2 * g * SEG : (2 * g + 1) * SEG, lanes], wide[(2 * g + 1) * SEG : (2 * g + 2) * SEG, lanes]
            )

    def attend_back(i):
        return staged(i, (spread, widen, differentiate, collect_values, collect_keys, collect_queries))

    def last(i):
        at = pl.ds(i * block, block)
        to = pl.ds(i * block + SEG, block)
        bplace = dot(braw[at], relblock[...]) * SCALING
        yield 1
        bc = bcont[at]
        vec[V_CONTENT : V_CONTENT + 1] += column_sum(bc)
        vec[V_POSITION : V_POSITION + 1] += column_sum(bplace)
        bq = (bc + bplace).astype(BF)
        bql[at] = bq
        yield 1
        bn = dot_t(bq, wq[...]) + dot_t(kgs[at], wk[...]) + dot_t(vgs[at], wv[...])
        yield 1
        bm = dot_t(kgm[at], wk[...]) + dot_t(vgm[at], wv[...])
        yield 1
        unit = xhat[to]
        vec[V_GAIN1 : V_GAIN1 + 1] += column_sum(bn * unit) + column_sum(bm * xhat[at])
        vec[V_SHIFT1 : V_SHIFT1 + 1] += column_sum(bn) + column_sum(bm)
        u = bn * gain1[...]
        inner = u - jnp.mean(u, axis=-1, keepdims=True) - unit * jnp.mean(u * unit, axis=-1, keepdims=True)
        dx[at] = (bhid[at] + inner * rstd[to]).astype(BF)
        send_rows(1, at)
        yield 1

    def attention_weights():
        segment_rows = nl[SEG : SEG + rows]
        memory_rows = nl[0:rows]
        late[QUERY_AT : QUERY_AT + FEATURES] = t_dot(segment_rows, bql[...]).astype(BF)
        yield 1
        late[VALUE_AT : VALUE_AT + FEATURES] = (t_dot(segment_rows, vgs[...]) + t_dot(memory_rows, vgm[...])).astype(BF)
        send_late(0)
        yield 1
        late[KEY_AT : KEY_AT + FEATURES] = (t_dot(segment_rows, kgs[...]) + t_dot(memory_rows, kgm[...])).astype(BF)
        yield 1
        for g in range(HEADS // GROUP):
            lanes = slice(g * LANES, (g + 1) * LANES)
            across = t_dot(placed[:, lanes], braw[:, g * GROUP * LANES : (g + 1) * GROUP * LANES])
            back = jnp.concatenate(
                [across[h * HEAD_DIM : (h + 1) * HEAD_DIM, h * LANES : (h + 1) * LANES] for h in range(GROUP)], axis=0
            ) * SCALING
            high = back.astype(BF)
            low = (back - high.astype(F32)).astype(BF)
            cosines = dot_t(basis[0:LANES], high) + (dot_t(basis[LANES:], high) + dot_t(basis[0:LANES], low))
            late[RELATIVE_AT : RELATIVE_AT + LANES, lanes] = cosines.astype(BF)
            yield 1

    phases = {
        "first": (8, first), "attend": (2 * block // SEG, attend), "feed": (14, feed), "back": (6 * block // SEG, attend_back), "last": (5, last),
    }
    for t in range(blocks + 4):
        if t == 2:
            wait_for(*LATER_COPIES)
        steps = []
        for lag, (count, phase) in enumerate(phases.values()):
            if 0 <= t - lag < blocks:
                steps.append((count, phase(t - lag)))
        if t == blocks + 2:
            steps.append((18, feed_weights()))
        if t == blocks + 3:
            pass
        interleave(*steps)
    interleave((5, attention_weights()))
    late[VECTOR_AT : VECTOR_AT + VECTOR_ROWS] = vec[...].astype(BF)
    late[VECTOR_AT + VECTOR_ROWS :] = jnp.zeros((2 * LATE_ROWS - VECTOR_AT - VECTOR_ROWS, FEATURES), BF)
    send_late(1)


def run_layer(horizon, x, start, arrived, cot, table, basis, params):
    rows = x.shape[0]
    operands = (x, start, arrived, cot, *params, table, basis)
    vmem = pl.BlockSpec(memory_space=pltpu.VMEM)
    hbm = pl.BlockSpec(memory_space=pltpu.HBM)
    padded = rows + SEG + LANES - 2 * SEG
    scratch = [
        pltpu.VMEM((rows + SEG, FEATURES), BF),
        pltpu.VMEM((rows + SEG, FEATURES), F32),
        pltpu.VMEM((rows + SEG, 1), F32),
        pltpu.VMEM((rows, FEATURES), BF),
        pltpu.VMEM((rows, FEATURES), BF),
        pltpu.VMEM((padded, FEATURES), BF),
        pltpu.VMEM((padded, FEATURES), BF),
        pltpu.VMEM((padded, 2 * FEATURES), BF),
        pltpu.VMEM((padded, 2 * FEATURES), BF),
        pltpu.VMEM((HEADS * LANES, FEATURES), BF),
        pltpu.VMEM((rows, HEADS * LANES), F32),
        pltpu.VMEM((rows * HEADS // 2, 2 * LANES), BF),
        pltpu.VMEM((rows, FEATURES), F32),
        pltpu.VMEM((rows, FEATURES), BF),
        pltpu.VMEM((rows, FEATURES), F32),
        pltpu.VMEM((rows, FEATURES), BF),
        pltpu.VMEM((rows, HIDDEN), BF),
        pltpu.VMEM((rows, HIDDEN), BF),
        pltpu.VMEM((rows, FEATURES), BF),
        pltpu.VMEM((rows, FEATURES), F32),
        pltpu.VMEM((rows, FEATURES), BF),
        pltpu.VMEM((rows, FEATURES), F32),
        pltpu.VMEM((rows, FEATURES), BF),
        pltpu.VMEM((rows, HEADS * LANES), BF),
        pltpu.VMEM((rows, FEATURES), BF),
        pltpu.VMEM((rows, FEATURES), BF),
        pltpu.VMEM((rows, FEATURES), BF),
        pltpu.VMEM((rows, FEATURES), BF),
        pltpu.VMEM((VECTOR_ROWS, FEATURES), F32),
    ]
    return pl.pallas_call(
        layer_kernel,
        out_shape=(
            jax.ShapeDtypeStruct((rows, FEATURES), BF),
            jax.ShapeDtypeStruct((rows, FEATURES), BF),
        )
        + (jax.ShapeDtypeStruct((PART_ROWS, FEATURES), BF),) * (2 * PIPES),
        in_specs=[hbm] * (COPIES + 1),
        out_specs=(hbm,) * (2 + 2 * PIPES),
        scratch_shapes=[pltpu.VMEM(a.shape, a.dtype) for a in operands]
        + [
            pltpu.SemaphoreType.DMA((COPIES + 1,)),
            pltpu.SemaphoreType.DMA((4 * (rows // SEG) + 2 * PIPES,)),
            pltpu.SemaphoreType.DMA((2 * PIPES + 4,)),
            pltpu.SMEM(horizon.shape, horizon.dtype),
            pltpu.VMEM((rows, FEATURES), BF),
            pltpu.VMEM((rows, FEATURES), BF),
            pltpu.VMEM((2 * sum(EARLY_ROWS), FEATURES), BF),
            pltpu.VMEM((2 * LATE_ROWS, FEATURES), BF),
        ]
        + scratch,
        compiler_params=pltpu.CompilerParams(vmem_limit_bytes=63 * 1024 * 1024),
        name="layer",
    )(horizon, *operands)


def join(own, other, whole):
    _, _, side = own_place()
    for k, part in ((side, own), (1 - side, other)):
        whole[pl.ds(pl.multiple_of(k * PART_ROWS, PART_ROWS), PART_ROWS)] = part[...]


BLOCKS = HIDDEN // FEATURES


def first_unpack_kernel(own, other, w1, w2, wo, whole, expand, shrink, output, sems):
    join(own, other, whole)
    moves = []

    def leave(source, target):
        moves.append(pltpu.make_async_copy(source, target, sems.at[len(moves)]))
        moves[-1].start()

    for f in range(BLOCKS - 1):
        cols = slice(f * FEATURES, (f + 1) * FEATURES)
        expand[f] = whole[f * FEATURES : (f + 1) * FEATURES].astype(F32)
        leave(expand.at[f], w1.at[:, cols])
        shrink[f] = whole[PART_ROWS + f * FEATURES : PART_ROWS + (f + 1) * FEATURES].astype(F32)
        leave(shrink.at[f], w2.at[cols])
    for k in range(2):
        end = (k + 1) * PART_ROWS
        output[k] = whole[end - OUTPUT_PIECE : end].astype(F32)
        leave(output.at[k], wo.at[k * OUTPUT_PIECE : (k + 1) * OUTPUT_PIECE])
    for move in moves:
        move.wait()


def second_unpack_kernel(
    w1_old, w2_old, wo_old, own, other, turned, w1, w2, wo, wq, wk, wv, wr, *refs
):
    vectors, (squares, output, longer, whole, sems, *kept) = refs[: V_EXPAND + 1], refs[V_EXPAND + 1 :]
    join(own, other, whole)
    moves = []

    def leave(source, target):
        moves.append(pltpu.make_async_copy(source, target, sems.at[len(moves)]))
        moves[-1].start()

    def late(at, count):
        at += EARLY_ROWS[1] if at < LATE_ROWS else EARLY_ROWS[1] + PART_ROWS - LATE_ROWS
        return whole[at : at + count]

    cosines = late(RELATIVE_AT, LANES)
    squares[5] = t_dot(turned[0:LANES], cosines) + t_dot(turned[LANES:], cosines)
    rows = late(VECTOR_AT, VECTOR_ROWS).astype(F32)
    for k in range(V_EXPAND):
        kept[k][...] = rows[k]
        leave(kept[k], vectors[k])
    for f in range(BLOCKS):
        longer[f * FEATURES : (f + 1) * FEATURES] = rows[V_EXPAND + f]
    leave(longer, vectors[V_EXPAND])
    cols = slice(HIDDEN - FEATURES, HIDDEN)
    squares[0] = whole[0:FEATURES].astype(F32)
    leave(squares.at[0], w1.at[:, cols])
    squares[1] = whole[PART_ROWS : PART_ROWS + FEATURES].astype(F32)
    leave(squares.at[1], w2.at[cols])
    for k, (ref, at) in enumerate(((wq, QUERY_AT), (wk, KEY_AT), (wv, VALUE_AT))):
        squares[k + 2] = late(at, FEATURES).astype(F32)
        leave(squares.at[k + 2], ref)
    leave(squares.at[5], wr)
    for k in range(2):
        start = k * PART_ROWS + FEATURES
        output[k] = whole[start : start + OUTPUT_PIECE].astype(F32)
        leave(output.at[k], wo.at[(k + 2) * OUTPUT_PIECE : (k + 3) * OUTPUT_PIECE])
    for move in moves:
        move.wait()


def unpack_all(parts, turned):
    vmem = pl.BlockSpec(memory_space=pltpu.VMEM)
    hbm = pl.BlockSpec(memory_space=pl.ANY)
    square, vector = (FEATURES, FEATURES), (FEATURES,)
    split = ((FEATURES, HIDDEN), (HIDDEN, FEATURES), square)
    rest = (square,) * 4 + (vector,) * V_EXPAND + ((HIDDEN,),)
    whole = pltpu.VMEM((2 * PART_ROWS, FEATURES), BF)
    output = pltpu.VMEM((2, OUTPUT_PIECE, FEATURES), F32)

    def shapes(dims):
        return tuple(jax.ShapeDtypeStruct(shape, F32) for shape in dims)

    params = pltpu.CompilerParams(vmem_limit_bytes=32 * 1024 * 1024)
    begun = pl.pallas_call(
        first_unpack_kernel,
        out_shape=shapes(split),
        in_specs=[vmem, vmem],
        out_specs=(hbm,) * 3,
        scratch_shapes=[
            whole,
            pltpu.VMEM((BLOCKS - 1, *square), F32),
            pltpu.VMEM((BLOCKS - 1, *square), F32),
            output,
            pltpu.SemaphoreType.DMA((2 * BLOCKS,)),
        ],
        compiler_params=params,
        name="unpack_first",
    )(*parts[:2])
    w1, w2, wo, wq, wk, wv, wr, cbias, pbias, gain1, shift1, gain2, shift2, b2, b1 = pl.pallas_call(
        second_unpack_kernel,
        out_shape=shapes(split + rest),
        in_specs=[hbm] * 3 + [vmem] * 3,
        out_specs=(hbm,) * (3 + len(rest)),
        scratch_shapes=[
            pltpu.VMEM((6, *square), F32),
            output,
            pltpu.VMEM((HIDDEN,), F32),
            whole,
            pltpu.SemaphoreType.DMA((8 + V_EXPAND + 1,)),
        ]
        + [pltpu.VMEM(vector, F32)] * V_EXPAND,
        input_output_aliases={0: 0, 1: 1, 2: 2},
        compiler_params=params,
        name="unpack_second",
    )(*begun, *parts[2:], turned)
    return gain1, shift1, wq, wk, wv, wr, cbias, pbias, wo, gain2, shift2, w1, b1, w2, b2


AXES = ("tm", "roll")


def exchange_plan(roll_count, tm_count):
    tm_bits = tm_count.bit_length() - 1
    roll_bits = roll_count.bit_length() - 1
    high = [roll_bits + b for b in range(1, tm_bits)]
    rolls = list(range(roll_bits))
    even = high + rolls
    odd = rolls[:1] + high + rolls[1:]
    return roll_bits, list(zip(even, odd))


def side_of(device):
    return bin(device).count("1") & 1


def swap_cores(value, core, count):
    return lax.ppermute(value, AXES, [(d, d ^ (1 << core)) for d in range(count)])


def swap(value, bits, core, count):
    return lax.ppermute(value, AXES, [(d, d ^ (1 << bits[side_of(d)]) ^ (1 << core)) for d in range(count)])


def add_low(a, b):
    return (a.astype(F32) + b.astype(F32)).astype(BF)


def sum_everywhere(halves, me, side):
    roll_count, tm_count = lax.axis_size("roll"), lax.axis_size("tm")
    count = roll_count * tm_count
    core, stages = exchange_plan(roll_count, tm_count)
    halving = 3

    def chain(kept, sent):
        got = swap_cores(sent, core, count)
        firsts = []
        for number, bits in enumerate(stages[:halving]):
            bit = jnp.where(side == 0, (me >> bits[0]) & 1, (me >> bits[1]) & 1)
            half = kept.shape[0] // 2

            def cut(value, which):
                return lax.dynamic_slice_in_dim(value, which * half, half, 0)

            leaving, staying = cut(kept, 1 - bit), cut(kept, bit)
            if number == 0:
                leaving, staying = lax.optimization_barrier((leaving, staying))
            sent = add_low(leaving, cut(got, 1 - bit))
            kept = add_low(staying, cut(got, bit))
            got = swap(sent, bits, core, count)
            firsts.append(bit == 0)
        buffer = add_low(kept, got)
        for bits in stages[halving:]:
            buffer = add_low(buffer, swap(buffer, bits, core, count))
        for bits, first in list(zip(stages, firsts))[::-1]:
            other = swap(buffer, bits, core, count)
            buffer = jnp.concatenate([jnp.where(first, buffer, other), jnp.where(first, other, buffer)], axis=0)
        return [buffer, swap_cores(buffer, core, count)]

    return sum([chain(*halves[2 * p : 2 * p + 2]) for p in range(PIPES)], [])


def body(
    layer_input, start_memory, horizon, cotangent, first_gain, first_shift, query_projection_weight,
    key_projection_weight, value_projection_weight, relative_weight, content_bias, position_bias,
    output_weight, second_gain, second_shift, expand_weight, expand_bias, shrink_weight, shrink_bias,
):
    rollouts, columns, features = layer_input.shape
    x = layer_input.reshape(rollouts * columns, features)
    tm_count = lax.axis_size("tm")
    arrived = lax.ppermute(x[-SEG:], "tm", [(i, (i + 1) % tm_count) for i in range(tm_count)])
    _, me, side = own_place()
    table = jnp.asarray(position_rows())
    basis, turned = (jnp.asarray(part) for part in relative_basis())

    def row(v):
        return v.reshape(1, -1)

    params = (
        row(first_gain), row(first_shift), query_projection_weight, key_projection_weight,
        value_projection_weight, relative_weight, row(content_bias), row(position_bias), output_weight,
        row(second_gain), row(second_shift), expand_weight, row(expand_bias), shrink_weight, row(shrink_bias),
    )
    out, dx, *halves = run_layer(
        horizon, x, start_memory.reshape(SEG, features), arrived,
        cotangent.reshape(rollouts * columns, features), table, basis, params,
    )
    summed = unpack_all(sum_everywhere(halves, me, side), turned)
    return (out.reshape(layer_input.shape), dx.reshape(layer_input.shape)) + tuple(summed)


def solution(mesh):
    in_specs = (
        P("roll", "tm", None), P("roll", None, None), P("roll", None), P("roll", "tm", None),
    ) + (P(),) * 15
    out_specs = (P("roll", "tm", None), P("roll", "tm", None)) + (P(),) * 15
    return jax.shard_map(body, mesh=mesh, in_specs=in_specs, out_specs=out_specs, check_vma=False)
```

```python
import functools
import math
import types

import jax
import jax.numpy as jnp
import numpy as np
from jax import lax
from jax.experimental import pallas as pl
from jax.experimental.pallas import tpu as pltpu
from jax.sharding import PartitionSpec as P

HEADS = 8
HEAD_DIM = 32
SEG = 48
STEP = 3
FEATURES = 256
HIDDEN = 1024
LANES = 128
GROUP = LANES // HEAD_DIM
EPSILON = 1e-05
MASKED = -4000000000.0
SCALING = 1.0 / math.sqrt(HEAD_DIM)
SCALING_BITS = SCALING / math.log(2.0)
GELU_A = 0.7978845608028654
GELU_B = 0.044715 * GELU_A
BF = jnp.bfloat16
F32 = jnp.float32

PIPES = 2
PART_ROWS = 832
EARLY_ROWS = (832, 320)
LATE_ROWS = 512
EXPAND_AT = (0, 256, 512, 1664)
SHRINK_AT = (832, 1088, 1344, 1984)
OUTPUT_AT = (768, 1600, 1920, 2240)
OUTPUT_PIECE = 64
QUERY_AT, KEY_AT, VALUE_AT, RELATIVE_AT, VECTOR_AT = 0, 256, 512, 768, 896
(V_CONTENT, V_POSITION, V_GAIN1, V_SHIFT1, V_GAIN2, V_SHIFT2, V_SHRINK, V_EXPAND) = range(8)
VECTOR_ROWS = 16


def position_rows():
    distance = (2 * SEG - 1 - np.arange(2 * SEG)).astype(np.float32)
    freqs = 10000.0 ** (-(2.0 * np.arange(FEATURES // 2)) / FEATURES)
    angles = distance[:, None] * freqs.astype(np.float32)[None, :]
    table = np.concatenate([np.sin(angles), np.cos(angles)], axis=-1)
    return np.pad(table, ((0, LANES - 2 * SEG), (0, 0))).astype(BF)


def relative_basis():
    count = 2 * SEG
    k, c = np.arange(count)[:, None], np.arange(count)[None, :]
    basis = np.cos(np.pi * k * (2 * c + 1) / (2 * count)) * np.where(k == 0, np.sqrt(1.0 / count), np.sqrt(2.0 / count))
    basis = np.pad(basis, ((0, LANES - count), (0, LANES - count)))

    def parts(values):
        high = values.astype(BF)
        low = (values - high.astype(np.float64)).astype(BF)
        return np.concatenate([high, low], axis=0)

    return parts(basis), parts(basis @ position_rows().astype(np.float64))


def tables():
    return jnp.asarray(position_rows()), jnp.asarray(relative_basis()[0])


def interleave(*steps):
    running = [[0, count, part] for count, part in steps]
    while running:
        slowest = min(running, key=lambda entry: entry[0] / entry[1])
        slowest[0] += 1
        if next(slowest[2], None) is None:
            running.remove(slowest)


def dot(a, b):
    return lax.dot_general(a, b, (((1,), (0,)), ((), ())), preferred_element_type=F32)


def dot_t(a, b):
    return lax.dot_general(a, b, (((1,), (1,)), ((), ())), preferred_element_type=F32)


def t_dot(a, b):
    return lax.dot_general(a, b, (((0,), (0,)), ((), ())), preferred_element_type=F32)


def normalize(rows):
    center = rows - jnp.mean(rows, axis=-1, keepdims=True)
    spread = jnp.mean(center * center, axis=-1, keepdims=True)
    scale = lax.rsqrt(spread + EPSILON)
    return center * scale, scale


def column_sum(rows):
    return jnp.sum(rows, axis=0, keepdims=True)


def stack_heads(rows, head_masks):
    return jnp.concatenate([rows * mask for mask in head_masks], axis=0)


def unshift(rows, row_bits):
    rolled = jnp.concatenate(
        [pltpu.roll(rows[a : a + 16], SEG - 16 - a, 1) for a in range(0, SEG - 16, 16)] + [rows[SEG - 16 :]], axis=0
    )
    for step, bit in row_bits:
        rolled = jnp.where(bit, pltpu.roll(rolled, step, 1), rolled)
    return rolled


def pick_heads(rows, lane_head):
    picked = rows[0:SEG]
    for h in range(1, GROUP):
        picked = jnp.where(lane_head == h, rows[h * SEG : (h + 1) * SEG], picked)
    return picked


COPIES = 21
(C_X, C_START, C_ARRIVED, C_COT, C_GAIN1, C_SHIFT1, C_WQ, C_WK, C_WV, C_WR, C_CBIAS, C_PBIAS, C_WO,
 C_GAIN2, C_SHIFT2, C_W1, C_B1, C_W2, C_B2, C_TABLE, C_BASIS) = range(COPIES)
FIRST_COPIES = (C_TABLE, C_WR, C_X, C_GAIN1, C_SHIFT1, C_START, C_ARRIVED, C_WK, C_WV, C_WQ, C_CBIAS, C_PBIAS)
LATER_COPIES = (C_WO, C_GAIN2, C_SHIFT2, C_W1, C_B1, C_COT, C_W2, C_B2, C_BASIS)


def own_place():
    position = lax.axis_index("tm")
    me = position * lax.axis_size("roll") + lax.axis_index("roll")
    side = me
    for shift in (16, 8, 4, 2, 1):
        side = side ^ (side >> shift)
    return position, me, side & 1


def layer_kernel(horizon_source, *refs):
    sources, refs = refs[:COPIES], refs[COPIES:]
    (out_target, dx_target, *halves), refs = refs[: 2 + 2 * PIPES], refs[2 + 2 * PIPES :]
    targets, (sems, out_sems, half_sems, horizon, out, dx, early, late, *scratch) = refs[:COPIES], refs[COPIES:]
    position, _, side = own_place()
    lengths = pltpu.make_async_copy(horizon_source, horizon, sems.at[COPIES])
    lengths.start()
    moves = [pltpu.make_async_copy(a, b, sems.at[i]) for i, (a, b) in enumerate(zip(sources, targets))]
    for i in FIRST_COPIES + LATER_COPIES:
        moves[i].start()
    leaving = []

    def leave(move):
        move.start()
        leaving.append(move)

    def send_rows(which, at):
        source, target = ((out, out_target), (dx, dx_target))[which]
        leave(pltpu.make_async_copy(source.at[at], target.at[at], out_sems.at[len(leaving)]))

    def send_early():
        start = 0
        for p in range(PIPES):
            for k, half in enumerate((side, 1 - side)):
                at = pl.ds(pl.multiple_of(start + half * EARLY_ROWS[p], 64), EARLY_ROWS[p])
                to = halves[2 * p + k].at[0 : EARLY_ROWS[p]]
                leave(pltpu.make_async_copy(early.at[at], to, half_sems.at[2 * p + k]))
            start += 2 * EARLY_ROWS[p]

    def send_late():
        for k, half in enumerate((side, 1 - side)):
            at = pl.ds(pl.multiple_of(half * LATE_ROWS, LATE_ROWS), LATE_ROWS)
            to = halves[2 + k].at[EARLY_ROWS[1] : PART_ROWS]
            leave(pltpu.make_async_copy(late.at[at], to, half_sems.at[2 * PIPES + k]))

    compute_layer(
        position, horizon, lengths, moves, (send_rows, send_early, send_late), *targets, out, dx, early, late, *scratch
    )
    for move in leaving:
        move.wait()


def compute_layer(
    position, horizon, lengths, moves, sends, x, start, arrived, cot, gain1, shift1, wq, wk, wv, wr, cbias, pbias, wo,
    gain2, shift2, w1, b1, w2, b2, table, basis,
    out, dx, early, late,
    nl, xhat, rstd, content, placed, keys_even, keys_odd, values_even, values_odd, relblock, raw, lows, inverses, mixed,
    hid, n2, act, bpre, bmix, bhid, bhl, bcont, bql, braw, kgm, kgs, vgm, vgs, vec,
):
    rows = x.shape[0]
    segments = rows // SEG
    send_rows, send_early, send_late = sends
    vec[...] = jnp.zeros_like(vec)

    def wait_for(*names):
        for i in names:
            moves[i].wait()

    wait_for(C_TABLE, C_WR)
    rel = dot(table[...], wr[...])
    wide_head = lax.broadcasted_iota(jnp.int32, (LANES, FEATURES), 1) // HEAD_DIM
    for h in range(HEADS):
        relblock[h * LANES : (h + 1) * LANES] = jnp.where(wide_head == h, rel, 0.0).astype(BF)

    wait_for(C_X, C_GAIN1, C_SHIFT1, C_START, C_ARRIVED, C_WK, C_WV)
    odd_lane = (lax.broadcasted_iota(jnp.int32, (1, LANES), 1) // HEAD_DIM) & 1
    parity_masks = [(odd_lane == q).astype(F32) for q in range(2)]

    def project(normed, at, count):
        key, value = dot(normed, wk[...]), dot(normed, wv[...])
        for q, (ks, vs) in enumerate(((keys_even, values_even), (keys_odd, values_odd))):
            for g in range(HEADS // GROUP):
                lanes = slice(g * LANES, (g + 1) * LANES)
                ks[pl.ds(at, count), lanes] = (key[:, lanes] * parity_masks[q]).astype(BF)
                vs[pl.ds(at, count), 2 * g * LANES : (2 * g + 1) * LANES] = (value[:, lanes] * parity_masks[q]).astype(BF)

    memory = jnp.where(position == 0, start[...].astype(F32), arrived[...].astype(F32))
    unit, scale = normalize(memory)
    xhat[0:SEG] = unit
    rstd[0:SEG] = scale
    normed = (unit * gain1[...] + shift1[...]).astype(BF)
    nl[0:SEG] = normed
    project(normed, 0, SEG)
    wait_for(C_WQ, C_CBIAS, C_PBIAS)
    lengths.wait()
    block = 8 * SEG
    for edge in range(block, rows + 1, block):
        ahead = slice(edge + SEG, edge + LANES - SEG)
        for ref in (keys_even, keys_odd, values_even, values_odd):
            ref[ahead] = jnp.zeros((LANES - 2 * SEG, ref.shape[1]), BF)
    for q, ref in enumerate((values_even, values_odd)):
        ones = jnp.broadcast_to(parity_masks[q], (ref.shape[0], LANES)).astype(BF)
        for g in range(HEADS // GROUP):
            ref[:, (2 * g + 1) * LANES : (2 * g + 2) * LANES] = ones
    blocks = rows // block
    lane_head = lax.broadcasted_iota(jnp.int32, (SEG, LANES), 1) // HEAD_DIM
    head_masks = [(lane_head == h).astype(F32).astype(BF) for h in range(GROUP)]
    key_at = lax.broadcasted_iota(jnp.int32, (SEG, LANES), 1)
    query_at = lax.broadcasted_iota(jnp.int32, (SEG, LANES), 0) + SEG
    low_row = 15 - (query_at & 15)
    row_bits = [(step, (low_row & step).astype(F32).astype(BF) > 0.5) for step in (8, 4, 2, 1)]
    upper = (lax.broadcasted_iota(jnp.int32, (SEG, FEATURES), 1) & (HEAD_DIM // 2)) != 0
    first_pair = key_at < 2 * HEAD_DIM
    pair_masks = [first_pair.astype(F32).astype(BF), (key_at >= 2 * HEAD_DIM).astype(F32).astype(BF)]
    blank = jnp.zeros((SEG, LANES), BF)

    def first(i):
        at = pl.ds(i * block, block)
        to = pl.ds(i * block + SEG, block)
        unit, scale = normalize(x[at].astype(F32))
        xhat[to] = unit
        rstd[to] = scale
        normed = (unit * gain1[...] + shift1[...]).astype(BF)
        nl[to] = normed
        yield 1
        project(normed, i * block + SEG, block)
        yield 1
        query = dot(normed, wq[...])
        content[at] = (query + cbias[...]).astype(BF)
        low = (query + pbias[...]).astype(BF)
        placed[at] = low
        yield 1
        for f in range(HEADS * LANES // FEATURES):
            cols = slice(f * FEATURES, (f + 1) * FEATURES)
            raw[at, cols] = dot_t(low, relblock[cols])
            yield 1

    def units_of(i):
        units = []
        for s in range(i * block // SEG, (i + 1) * block // SEG):
            u = types.SimpleNamespace()
            u.s, u.at, u.window = s, pl.ds(s * SEG, SEG), pl.ds(s * SEG, LANES)
            u.pairs = [pl.ds((s * HEADS // 2 + p) * SEG, SEG) for p in range(HEADS // 2)]
            units.append(u)
        return units

    def window_keys(u):
        return jnp.concatenate([keys_even[u.window], keys_odd[u.window]], axis=0)

    def window_values(u, g):
        lanes = slice(2 * g * LANES, (2 * g + 2) * LANES)
        return jnp.concatenate([values_even[u.window, lanes], values_odd[u.window, lanes]], axis=0)

    def group_lanes(g):
        return slice(g * LANES, (g + 1) * LANES)

    def allow(s):
        number = position * segments + s
        current = horizon[0, number]
        previous = jnp.where(number == 0, SEG // STEP, horizon[0, jnp.maximum(number - 1, 0)])
        live = key_at < jnp.where(key_at < SEG, STEP * previous, SEG + STEP * current)
        return (key_at <= query_at) & (live | (key_at == query_at))

    def score(u):
        parts = []
        for p in range(HEADS // 2):
            g = p // 2
            part = content[u.at, group_lanes(g)] * pair_masks[p % 2]
            parts.append(jnp.concatenate([part, blank] if g == 0 else [blank, part], axis=1))
        u.direct = dot_t(jnp.concatenate(parts, axis=0), window_keys(u))

    def mask(u):
        allowed = allow(u.s)
        u.scores = []
        for head in range(HEADS):
            p, q = head // 2, head % 2
            shifted = pltpu.roll(
                raw[u.at, head * LANES : (head + 1) * LANES], LANES - SEG + 1, 1, stride=1, stride_axis=0
            )
            direct = u.direct[p * SEG : (p + 1) * SEG, q * LANES : (q + 1) * LANES]
            u.scores.append(jnp.where(allowed, direct + shifted, MASKED))
        u.tops = [jnp.max(v, axis=-1, keepdims=True) for v in u.scores]

    def exponentiate(u):
        u.low = [jnp.exp2((v - top) * SCALING_BITS).astype(BF) for v, top in zip(u.scores, u.tops)]
        u.low = [jnp.concatenate(u.low[2 * p : 2 * p + 2], axis=1) for p in range(HEADS // 2)]
        for p in range(HEADS // 2):
            lows[u.pairs[p]] = u.low[p]

    def mix(u):
        u.both = [
            dot(jnp.concatenate(u.low[2 * g : 2 * g + 2], axis=0), window_values(u, g)) for g in range(HEADS // GROUP)
        ]

    def finish(u):
        for g in range(HEADS // GROUP):
            both = u.both[g]
            total = jnp.where(first_pair, both[:SEG, LANES:], both[SEG:, LANES:])
            inverse = 1.0 / total
            mx = jnp.where(first_pair, both[:SEG, :LANES], both[SEG:, :LANES]) * inverse
            mixed[u.at, group_lanes(g)] = mx.astype(BF)
            bcont[u.at, group_lanes(g)] = mx
            inverses[u.at, group_lanes(g)] = inverse

    def staged(i, stages):
        units = units_of(i)
        for stage in stages:
            for u in units:
                stage(u)
                yield 1

    def attend(i):
        return staged(i, (score, mask, exponentiate, mix, finish))

    def feed(i):
        at = pl.ds(i * block, block)
        hidden = x[at].astype(F32) + dot(mixed[at], wo[...])
        yield 1
        unit, scale = normalize(hidden)
        low = (unit * gain2[...] + shift2[...]).astype(BF)
        n2[at] = low
        yield 1
        back = cot[at]
        for f in range(HIDDEN // FEATURES):
            cols = slice(f * FEATURES, (f + 1) * FEATURES)
            v = dot(low, w1[:, cols]) + b1[:, cols]
            grad = dot_t(back, w2[cols])
            yield 1
            square = v * v
            half = 0.5 + 0.5 * jnp.tanh(v * (GELU_A + GELU_B * square))
            active = v * half
            act[at, cols] = active.astype(BF)
            slope = half + (2.0 * active) * (1.0 - half) * (GELU_A + (3.0 * GELU_B) * square)
            grad = grad * slope
            vec[V_EXPAND + f : V_EXPAND + f + 1] += column_sum(grad)
            bpre[at, cols] = grad.astype(BF)
            yield 1
        out[at] = (hidden + dot(act[at], w2[...]) + b2[...]).astype(BF)
        send_rows(0, at)
        yield 1
        bn = dot_t(bpre[at], w1[...])
        yield 1
        back = back.astype(F32)
        vec[V_SHRINK : V_SHRINK + 1] += column_sum(back)
        vec[V_GAIN2 : V_GAIN2 + 1] += column_sum(bn * unit)
        vec[V_SHIFT2 : V_SHIFT2 + 1] += column_sum(bn)
        u = bn * gain2[...]
        inner = u - jnp.mean(u, axis=-1, keepdims=True) - unit * jnp.mean(u * unit, axis=-1, keepdims=True)
        bh = back + inner * scale
        bhid[at] = bh
        bl = bh.astype(BF)
        bhl[at] = bl
        yield 1
        bmix[at] = dot_t(bl, wo[...]).astype(BF)
        yield 1

    def feed_weights():
        for f in range(HIDDEN // FEATURES):
            cols = slice(f * FEATURES, (f + 1) * FEATURES)
            early[EXPAND_AT[f] : EXPAND_AT[f] + FEATURES] = t_dot(n2[...], bpre[:, cols]).astype(BF)
            yield 1
            early[SHRINK_AT[f] : SHRINK_AT[f] + FEATURES] = t_dot(act[:, cols], cot[...]).astype(BF)
            yield 1
        weight = t_dot(mixed[...], bhl[...]).astype(BF)
        for k, to in enumerate(OUTPUT_AT):
            early[to : to + OUTPUT_PIECE] = weight[k * OUTPUT_PIECE : (k + 1) * OUTPUT_PIECE]
        send_early()
        yield 1

    def spread(u):
        u.back = (bmix[u.at].astype(F32) * inverses[u.at]).astype(BF)
        product = u.back.astype(F32) * -bcont[u.at]
        left, right = [], []
        for g in range(HEADS // GROUP):
            part = product[:, group_lanes(g)]
            left.append(part + pltpu.roll(part, LANES - HEAD_DIM // 2, 1))
            right.append(part + pltpu.roll(part, HEAD_DIM // 2, 1))
        left, right = jnp.concatenate(left, axis=1), jnp.concatenate(right, axis=1)
        u.along = jnp.where(upper, right, left - left.astype(BF).astype(F32)).astype(BF)

    def widen(u):
        u.wide = []
        for g in range(HEADS // GROUP):
            rows_in = [
                jnp.concatenate([u.back[:, group_lanes(g)] * m, u.along[:, group_lanes(g)] * m], axis=1)
                for m in pair_masks
            ]
            u.wide.append(dot_t(jnp.concatenate(rows_in, axis=0), window_values(u, g)))

    def differentiate(u):
        u.low, u.grad_low = [], []
        for p in range(HEADS // 2):
            low = lows[u.pairs[p]]
            bs = low.astype(F32) * u.wide[p // 2][(p % 2) * SEG : (p % 2 + 1) * SEG]
            u.low.append(low)
            u.grad_low.append(bs.astype(BF))
            for q in range(2):
                head = 2 * p + q
                braw[u.at, head * LANES : (head + 1) * LANES] = unshift(
                    u.grad_low[p][:, q * LANES : (q + 1) * LANES], row_bits
                )

    def by_head(pairs, g):
        return jnp.concatenate(
            [pairs[p][:, q * LANES : (q + 1) * LANES] for p in (2 * g, 2 * g + 1) for q in range(2)], axis=0
        )

    def collect_values(u):
        for g in range(HEADS // GROUP):
            lanes = group_lanes(g)
            vg = t_dot(by_head(u.low, g), stack_heads(u.back[:, lanes], head_masks)).astype(BF)
            vgm[u.at, lanes] = vg[0:SEG]
            vgs[u.at, lanes] = vg[SEG : 2 * SEG]

    def collect_keys(u):
        for g in range(HEADS // GROUP):
            lanes = group_lanes(g)
            kg = (t_dot(by_head(u.grad_low, g), stack_heads(content[u.at, lanes], head_masks)) * SCALING).astype(BF)
            kgm[u.at, lanes] = kg[0:SEG]
            kgs[u.at, lanes] = kg[SEG : 2 * SEG]

    def collect_queries(u):
        wide = dot(jnp.concatenate(u.grad_low, axis=0), window_keys(u))
        for g in range(HEADS // GROUP):
            lanes = group_lanes(g)
            bcont[u.at, lanes] = SCALING * jnp.where(
                first_pair, wide[2 * g * SEG : (2 * g + 1) * SEG, lanes], wide[(2 * g + 1) * SEG : (2 * g + 2) * SEG, lanes]
            )

    def attend_back(i):
        return staged(i, (spread, widen, differentiate, collect_values, collect_keys, collect_queries))

    def last(i):
        at = pl.ds(i * block, block)
        to = pl.ds(i * block + SEG, block)
        bplace = dot(braw[at], relblock[...]) * SCALING
        yield 1
        bc = bcont[at]
        vec[V_CONTENT : V_CONTENT + 1] += column_sum(bc)
        vec[V_POSITION : V_POSITION + 1] += column_sum(bplace)
        bq = (bc + bplace).astype(BF)
        bql[at] = bq
        yield 1
        bn = dot_t(bq, wq[...]) + dot_t(kgs[at], wk[...]) + dot_t(vgs[at], wv[...])
        yield 1
        bm = dot_t(kgm[at], wk[...]) + dot_t(vgm[at], wv[...])
        yield 1
        unit = xhat[to]
        vec[V_GAIN1 : V_GAIN1 + 1] += column_sum(bn * unit) + column_sum(bm * xhat[at])
        vec[V_SHIFT1 : V_SHIFT1 + 1] += column_sum(bn) + column_sum(bm)
        u = bn * gain1[...]
        inner = u - jnp.mean(u, axis=-1, keepdims=True) - unit * jnp.mean(u * unit, axis=-1, keepdims=True)
        dx[at] = (bhid[at] + inner * rstd[to]).astype(BF)
        send_rows(1, at)
        yield 1

    def attention_weights():
        segment_rows = nl[SEG : SEG + rows]
        memory_rows = nl[0:rows]
        late[QUERY_AT : QUERY_AT + FEATURES] = t_dot(segment_rows, bql[...]).astype(BF)
        yield 1
        late[KEY_AT : KEY_AT + FEATURES] = (t_dot(segment_rows, kgs[...]) + t_dot(memory_rows, kgm[...])).astype(BF)
        yield 1
        late[VALUE_AT : VALUE_AT + FEATURES] = (t_dot(segment_rows, vgs[...]) + t_dot(memory_rows, vgm[...])).astype(BF)
        yield 1
        for g in range(HEADS // GROUP):
            lanes = slice(g * LANES, (g + 1) * LANES)
            across = t_dot(placed[:, lanes], braw[:, g * GROUP * LANES : (g + 1) * GROUP * LANES])
            back = jnp.concatenate(
                [across[h * HEAD_DIM : (h + 1) * HEAD_DIM, h * LANES : (h + 1) * LANES] for h in range(GROUP)], axis=0
            ) * SCALING
            high = back.astype(BF)
            low = (back - high.astype(F32)).astype(BF)
            cosines = dot_t(basis[0:LANES], high) + (dot_t(basis[LANES:], high) + dot_t(basis[0:LANES], low))
            late[RELATIVE_AT : RELATIVE_AT + LANES, lanes] = cosines.astype(BF)
            yield 1

    phases = {
        "first": (8, first), "attend": (2 * block // SEG, attend), "feed": (14, feed), "back": (6 * block // SEG, attend_back), "last": (5, last),
    }
    for t in range(blocks + 4):
        if t == 2:
            wait_for(*LATER_COPIES)
        steps = []
        for lag, (count, phase) in enumerate(phases.values()):
            if 0 <= t - lag < blocks:
                steps.append((count, phase(t - lag)))
        if t == blocks + 2:
            steps.append((9, feed_weights()))
        if t == blocks + 3:
            pass
        interleave(*steps)
    interleave((5, attention_weights()))
    late[VECTOR_AT : VECTOR_AT + VECTOR_ROWS] = vec[...].astype(BF)
    late[VECTOR_AT + VECTOR_ROWS :] = jnp.zeros((2 * LATE_ROWS - VECTOR_AT - VECTOR_ROWS, FEATURES), BF)
    send_late()


def run_layer(horizon, x, start, arrived, cot, table, basis, params):
    rows = x.shape[0]
    operands = (x, start, arrived, cot, *params, table, basis)
    vmem = pl.BlockSpec(memory_space=pltpu.VMEM)
    hbm = pl.BlockSpec(memory_space=pltpu.HBM)
    padded = rows + SEG + LANES - 2 * SEG
    scratch = [
        pltpu.VMEM((rows + SEG, FEATURES), BF),
        pltpu.VMEM((rows + SEG, FEATURES), F32),
        pltpu.VMEM((rows + SEG, 1), F32),
        pltpu.VMEM((rows, FEATURES), BF),
        pltpu.VMEM((rows, FEATURES), BF),
        pltpu.VMEM((padded, FEATURES), BF),
        pltpu.VMEM((padded, FEATURES), BF),
        pltpu.VMEM((padded, 2 * FEATURES), BF),
        pltpu.VMEM((padded, 2 * FEATURES), BF),
        pltpu.VMEM((HEADS * LANES, FEATURES), BF),
        pltpu.VMEM((rows, HEADS * LANES), F32),
        pltpu.VMEM((rows * HEADS // 2, 2 * LANES), BF),
        pltpu.VMEM((rows, FEATURES), F32),
        pltpu.VMEM((rows, FEATURES), BF),
        pltpu.VMEM((rows, FEATURES), F32),
        pltpu.VMEM((rows, FEATURES), BF),
        pltpu.VMEM((rows, HIDDEN), BF),
        pltpu.VMEM((rows, HIDDEN), BF),
        pltpu.VMEM((rows, FEATURES), BF),
        pltpu.VMEM((rows, FEATURES), F32),
        pltpu.VMEM((rows, FEATURES), BF),
        pltpu.VMEM((rows, FEATURES), F32),
        pltpu.VMEM((rows, FEATURES), BF),
        pltpu.VMEM((rows, HEADS * LANES), BF),
        pltpu.VMEM((rows, FEATURES), BF),
        pltpu.VMEM((rows, FEATURES), BF),
        pltpu.VMEM((rows, FEATURES), BF),
        pltpu.VMEM((rows, FEATURES), BF),
        pltpu.VMEM((VECTOR_ROWS, FEATURES), F32),
    ]
    return pl.pallas_call(
        layer_kernel,
        out_shape=(
            jax.ShapeDtypeStruct((rows, FEATURES), BF),
            jax.ShapeDtypeStruct((rows, FEATURES), BF),
        )
        + (jax.ShapeDtypeStruct((PART_ROWS, FEATURES), BF),) * (2 * PIPES),
        in_specs=[hbm] * (COPIES + 1),
        out_specs=(hbm,) * (2 + 2 * PIPES),
        scratch_shapes=[pltpu.VMEM(a.shape, a.dtype) for a in operands]
        + [
            pltpu.SemaphoreType.DMA((COPIES + 1,)),
            pltpu.SemaphoreType.DMA((4 * (rows // SEG) + 2 * PIPES,)),
            pltpu.SemaphoreType.DMA((2 * PIPES + 2,)),
            pltpu.SMEM(horizon.shape, horizon.dtype),
            pltpu.VMEM((rows, FEATURES), BF),
            pltpu.VMEM((rows, FEATURES), BF),
            pltpu.VMEM((2 * sum(EARLY_ROWS), FEATURES), BF),
            pltpu.VMEM((2 * LATE_ROWS, FEATURES), BF),
        ]
        + scratch,
        compiler_params=pltpu.CompilerParams(vmem_limit_bytes=63 * 1024 * 1024),
        name="layer",
    )(horizon, *operands)


def join(own, other, whole):
    _, _, side = own_place()
    for k, part in ((side, own), (1 - side, other)):
        whole[pl.ds(pl.multiple_of(k * PART_ROWS, PART_ROWS), PART_ROWS)] = part[...]


BLOCKS = HIDDEN // FEATURES


def first_unpack_kernel(own, other, w1, w2, wo, whole, expand, shrink, output, sems):
    join(own, other, whole)
    moves = []

    def leave(source, target):
        moves.append(pltpu.make_async_copy(source, target, sems.at[len(moves)]))
        moves[-1].start()

    for f in range(BLOCKS - 1):
        cols = slice(f * FEATURES, (f + 1) * FEATURES)
        expand[f] = whole[f * FEATURES : (f + 1) * FEATURES].astype(F32)
        leave(expand.at[f], w1.at[:, cols])
        shrink[f] = whole[PART_ROWS + f * FEATURES : PART_ROWS + (f + 1) * FEATURES].astype(F32)
        leave(shrink.at[f], w2.at[cols])
    for k in range(2):
        end = (k + 1) * PART_ROWS
        output[k] = whole[end - OUTPUT_PIECE : end].astype(F32)
        leave(output.at[k], wo.at[k * OUTPUT_PIECE : (k + 1) * OUTPUT_PIECE])
    for move in moves:
        move.wait()


def second_unpack_kernel(
    w1_old, w2_old, wo_old, own, other, turned, w1, w2, wo, wq, wk, wv, wr, *refs
):
    vectors, (squares, output, longer, whole, sems, *kept) = refs[: V_EXPAND + 1], refs[V_EXPAND + 1 :]
    join(own, other, whole)
    moves = []

    def leave(source, target):
        moves.append(pltpu.make_async_copy(source, target, sems.at[len(moves)]))
        moves[-1].start()

    def late(at, count):
        at += EARLY_ROWS[1] if at < LATE_ROWS else EARLY_ROWS[1] + PART_ROWS - LATE_ROWS
        return whole[at : at + count]

    cosines = late(RELATIVE_AT, LANES)
    squares[5] = t_dot(turned[0:LANES], cosines) + t_dot(turned[LANES:], cosines)
    rows = late(VECTOR_AT, VECTOR_ROWS).astype(F32)
    for k in range(V_EXPAND):
        kept[k][...] = rows[k]
        leave(kept[k], vectors[k])
    for f in range(BLOCKS):
        longer[f * FEATURES : (f + 1) * FEATURES] = rows[V_EXPAND + f]
    leave(longer, vectors[V_EXPAND])
    cols = slice(HIDDEN - FEATURES, HIDDEN)
    squares[0] = whole[0:FEATURES].astype(F32)
    leave(squares.at[0], w1.at[:, cols])
    squares[1] = whole[PART_ROWS : PART_ROWS + FEATURES].astype(F32)
    leave(squares.at[1], w2.at[cols])
    for k, (ref, at) in enumerate(((wq, QUERY_AT), (wk, KEY_AT), (wv, VALUE_AT))):
        squares[k + 2] = late(at, FEATURES).astype(F32)
        leave(squares.at[k + 2], ref)
    leave(squares.at[5], wr)
    for k in range(2):
        start = k * PART_ROWS + FEATURES
        output[k] = whole[start : start + OUTPUT_PIECE].astype(F32)
        leave(output.at[k], wo.at[(k + 2) * OUTPUT_PIECE : (k + 3) * OUTPUT_PIECE])
    for move in moves:
        move.wait()


def unpack_all(parts, turned):
    vmem = pl.BlockSpec(memory_space=pltpu.VMEM)
    hbm = pl.BlockSpec(memory_space=pl.ANY)
    square, vector = (FEATURES, FEATURES), (FEATURES,)
    split = ((FEATURES, HIDDEN), (HIDDEN, FEATURES), square)
    rest = (square,) * 4 + (vector,) * V_EXPAND + ((HIDDEN,),)
    whole = pltpu.VMEM((2 * PART_ROWS, FEATURES), BF)
    output = pltpu.VMEM((2, OUTPUT_PIECE, FEATURES), F32)

    def shapes(dims):
        return tuple(jax.ShapeDtypeStruct(shape, F32) for shape in dims)

    params = pltpu.CompilerParams(vmem_limit_bytes=32 * 1024 * 1024)
    begun = pl.pallas_call(
        first_unpack_kernel,
        out_shape=shapes(split),
        in_specs=[vmem, vmem],
        out_specs=(hbm,) * 3,
        scratch_shapes=[
            whole,
            pltpu.VMEM((BLOCKS - 1, *square), F32),
            pltpu.VMEM((BLOCKS - 1, *square), F32),
            output,
            pltpu.SemaphoreType.DMA((2 * BLOCKS,)),
        ],
        compiler_params=params,
        name="unpack_first",
    )(*parts[:2])
    w1, w2, wo, wq, wk, wv, wr, cbias, pbias, gain1, shift1, gain2, shift2, b2, b1 = pl.pallas_call(
        second_unpack_kernel,
        out_shape=shapes(split + rest),
        in_specs=[hbm] * 3 + [vmem] * 3,
        out_specs=(hbm,) * (3 + len(rest)),
        scratch_shapes=[
            pltpu.VMEM((6, *square), F32),
            output,
            pltpu.VMEM((HIDDEN,), F32),
            whole,
            pltpu.SemaphoreType.DMA((8 + V_EXPAND + 1,)),
        ]
        + [pltpu.VMEM(vector, F32)] * V_EXPAND,
        input_output_aliases={0: 0, 1: 1, 2: 2},
        compiler_params=params,
        name="unpack_second",
    )(*begun, *parts[2:], turned)
    return gain1, shift1, wq, wk, wv, wr, cbias, pbias, wo, gain2, shift2, w1, b1, w2, b2


AXES = ("tm", "roll")


def exchange_plan(roll_count, tm_count):
    tm_bits = tm_count.bit_length() - 1
    roll_bits = roll_count.bit_length() - 1
    high = [roll_bits + b for b in range(1, tm_bits)]
    rolls = list(range(roll_bits))
    even = high + rolls
    odd = rolls[:1] + high + rolls[1:]
    return roll_bits, list(zip(even, odd))


def side_of(device):
    return bin(device).count("1") & 1


def swap_cores(value, core, count):
    return lax.ppermute(value, AXES, [(d, d ^ (1 << core)) for d in range(count)])


def swap(value, bits, core, count):
    return lax.ppermute(value, AXES, [(d, d ^ (1 << bits[side_of(d)]) ^ (1 << core)) for d in range(count)])


def add_low(a, b):
    return (a.astype(F32) + b.astype(F32)).astype(BF)


def sum_everywhere(halves, me, side):
    roll_count, tm_count = lax.axis_size("roll"), lax.axis_size("tm")
    count = roll_count * tm_count
    core, stages = exchange_plan(roll_count, tm_count)
    halving = 3

    def chain(kept, sent):
        got = swap_cores(sent, core, count)
        firsts = []
        for number, bits in enumerate(stages[:halving]):
            bit = jnp.where(side == 0, (me >> bits[0]) & 1, (me >> bits[1]) & 1)
            half = kept.shape[0] // 2

            def cut(value, which):
                return lax.dynamic_slice_in_dim(value, which * half, half, 0)

            leaving, staying = cut(kept, 1 - bit), cut(kept, bit)
            if number == 0:
                leaving = lax.optimization_barrier(leaving)
            sent = add_low(leaving, cut(got, 1 - bit))
            kept = add_low(staying, cut(got, bit))
            got = swap(sent, bits, core, count)
            firsts.append(bit == 0)
        buffer = add_low(kept, got)
        for bits in stages[halving:]:
            buffer = add_low(buffer, swap(buffer, bits, core, count))
        for bits, first in list(zip(stages, firsts))[::-1]:
            other = swap(buffer, bits, core, count)
            buffer = jnp.concatenate([jnp.where(first, buffer, other), jnp.where(first, other, buffer)], axis=0)
        return [buffer, swap_cores(buffer, core, count)]

    return sum([chain(*halves[2 * p : 2 * p + 2]) for p in range(PIPES)], [])


def body(
    layer_input, start_memory, horizon, cotangent, first_gain, first_shift, query_projection_weight,
    key_projection_weight, value_projection_weight, relative_weight, content_bias, position_bias,
    output_weight, second_gain, second_shift, expand_weight, expand_bias, shrink_weight, shrink_bias,
):
    rollouts, columns, features = layer_input.shape
    x = layer_input.reshape(rollouts * columns, features)
    tm_count = lax.axis_size("tm")
    arrived = lax.ppermute(x[-SEG:], "tm", [(i, (i + 1) % tm_count) for i in range(tm_count)])
    _, me, side = own_place()
    table = jnp.asarray(position_rows())
    basis, turned = (jnp.asarray(part) for part in relative_basis())

    def row(v):
        return v.reshape(1, -1)

    params = (
        row(first_gain), row(first_shift), query_projection_weight, key_projection_weight,
        value_projection_weight, relative_weight, row(content_bias), row(position_bias), output_weight,
        row(second_gain), row(second_shift), expand_weight, row(expand_bias), shrink_weight, row(shrink_bias),
    )
    out, dx, *halves = run_layer(
        horizon, x, start_memory.reshape(SEG, features), arrived,
        cotangent.reshape(rollouts * columns, features), table, basis, params,
    )
    summed = unpack_all(sum_everywhere(halves, me, side), turned)
    return (out.reshape(layer_input.shape), dx.reshape(layer_input.shape)) + tuple(summed)


def solution(mesh):
    in_specs = (
        P("roll", "tm", None), P("roll", None, None), P("roll", None), P("roll", "tm", None),
    ) + (P(),) * 15
    out_specs = (P("roll", "tm", None), P("roll", "tm", None)) + (P(),) * 15
    return jax.shard_map(body, mesh=mesh, in_specs=in_specs, out_specs=out_specs, check_vma=False)
```
